512 devices in a mesh: event: 16 (over x, z_hi, core), row: 32 (over y, z_lo).
Axes of the slice: x: 4, y: 4, z: 16 (z_hi: 2, z_lo: 8; z = z_hi * 8 + z_lo), core: 2. Of those that a mesh axis runs over, the one named last changes fastest.
Arguments:
- initial_head: float32 [16, 48, 128, 384], P('event', None, 'row'), may hold values from -6 to -1.5
- sat_conductivity: float32 [256], replicated, may hold values from 0.3 to 3
- vg_alpha: float32 [256], replicated, may hold values from 0.25 to 1
- vg_n: float32 [256], replicated, may hold values from 1.3 to 2.5
- zone_map: int32 [64, 192], P('row'), may hold values from 0 to 255, as said below
- forcing_plan: int32 [16, 2, 64], P('event', None, 'row'), may hold values from 0 to 3
- tensiometer_cells: int32 [16, 8192], P('event', 'row'), may hold values from 0 to 73727
- tensiometer_heads: float32 [16, 8192], P('event', 'row'), may hold values from -6 to -1
Outputs:
- final_head: float32 [16, 48, 128, 384], P('event', None, 'row')
- misfit: float32 [], replicated
- grad_conductivity: float32 [256], replicated
- grad_alpha: float32 [256], replicated
- grad_n: float32 [256], replicated
The draws below stay inside these ranges and needn't reach their ends.
Inputs may be any that keep to these rules, and one draw needn't show every extreme that they name: `zone_map`: the zone of a block in block row a lies among the 16 zones from a * 2 * 2 onward, taken modulo 256. `tensiometer_cells`: tensiometer j lies in the rows j // 256 * 4 to j // 256 * 4 + 3; the entry is its offset inside that block of rows, as depth * 4 * 384 + row offset * 384 + column.
All inputs are finite; a program needn't handle non-finite values.
Results may differ from the reference program's by a relative error of at most 0.0003.
Values sent between devices are 32-bit elements; how exact they have to be, the bound alone decides.
No kernel may reach another device: no remote copies, remote signals or barrier semaphores. Data moves between devices by JAX's collectives and lax.ppermute only.
A program may use at most 64 MiB of HBM per device.

```python
import math
import jax
import jax.numpy as jnp
from jax import lax

ROWS_DEV = 4
NY = 384
NZ = 48
STEPS = 2
SENS_DEV = 256
ZONES_DEV = 8
NX = 128
EVENTS = 16
SENSORS = 8192
ZONES = 256


def draw_zone_map(key, part):
    key = jax.random.fold_in(key, 11)
    block_rows = jnp.arange(NX // 2, dtype=jnp.int32)
    base = block_rows * (2 * ZONES_DEV) // ROWS_DEV
    offset = jax.random.randint(key, (NX // 2, NY // 2), 0, 2 * ZONES_DEV, dtype=jnp.int32)
    return (base[:, None] + offset) % ZONES


def place_ends(result, own_key, low, top_value):
    longest = result.shape.index(max(result.shape))
    spots = []
    for shift in (0, 1):
        where = [jax.random.randint(jax.random.fold_in(own_key, axis), (), 0, length) for axis, length in enumerate(result.shape)]
        where[longest] = (where[longest] + shift) % result.shape[longest]
        spots.append(tuple(where))
    return result.at[spots[0]].set(low).at[spots[1]].set(top_value)


def block_scale(key, dims, split, smallest, top_value):
    gain, own = 1.0, jax.random.fold_in(key, 6)
    for dim, blocks in split:
        steps = jnp.exp(jax.random.uniform(jax.random.fold_in(own, dim), (blocks,), jnp.float32, smallest / len(split), top_value / len(split)))
        gain = gain * jnp.repeat(steps, dims[dim] // blocks).reshape([-1 if axis == dim else 1 for axis in range(len(dims))])
    return gain


def setup_inputs(seed: int = 0) -> dict:
    streams_of = jax.random.split(jax.random.key(seed), 9)
    initial_head = jnp.clip(-6.0 + 4.5 * jax.random.uniform(streams_of[0], (EVENTS, NZ, NX, NY), jnp.float32) ** block_scale(streams_of[0], (EVENTS, NZ, NX, NY), ((0, 16), (2, 32)), -0.2, 0.2), -6.0, -1.5)
    sat_conductivity = jnp.clip(jnp.exp(jax.random.uniform(streams_of[1], (ZONES,), jnp.float32, math.log(0.3), math.log(3.0))), 0.3, 3.0)
    vg_alpha = jnp.clip(jnp.exp(jax.random.uniform(streams_of[2], (ZONES,), jnp.float32, math.log(0.25), math.log(1.0))), 0.25, 1.0)
    vg_n = jnp.clip(jax.random.uniform(streams_of[3], (ZONES,), jnp.float32, 1.3, 2.5), 1.3, 2.5)
    zone_map = draw_zone_map(jax.random.fold_in(streams_of[8], 71), 0)
    forcing_plan = place_ends(jax.random.randint(streams_of[5], (EVENTS, STEPS, NX // 2), 0, 4), jax.random.fold_in(streams_of[5], 1), 0, 3).astype(jnp.int32)
    tensiometer_cells = place_ends(jax.random.randint(streams_of[6], (EVENTS, SENSORS), 0, NZ * ROWS_DEV * NY), jax.random.fold_in(streams_of[6], 1), 0, (NZ * ROWS_DEV * NY) - 1).astype(jnp.int32)
    tensiometer_heads = jnp.clip(-6.0 + 5.0 * jax.random.uniform(streams_of[7], (EVENTS, SENSORS), jnp.float32) ** block_scale(streams_of[7], (EVENTS, SENSORS), ((0, 16), (1, 32)), -0.2, 0.2), -6.0, -1.0)
    return {"initial_head": initial_head, "sat_conductivity": sat_conductivity, "vg_alpha": vg_alpha, "vg_n": vg_n, "zone_map": zone_map, "forcing_plan": forcing_plan, "tensiometer_cells": tensiometer_cells, "tensiometer_heads": tensiometer_heads}


CFL = 0.4
IRRIGATION = 0.2
WATER_RANGE = 0.35

def conductivity(head_now, sat_cond, air_entry, shape_n):
    x = air_entry * -head_now
    u = jnp.power(x, shape_n)
    m = 1.0 - 1.0 / shape_n
    frac = u / (1.0 + u)
    saturation = jnp.power(1.0 + u, -m)
    return sat_cond * jnp.sqrt(saturation) * jnp.square(1.0 - jnp.power(frac, m))

def capacity(head_now, air_entry, shape_n):
    x = air_entry * -head_now
    u = jnp.power(x, shape_n)
    m = 1.0 - 1.0 / shape_n
    return WATER_RANGE * m * shape_n * air_entry * jnp.power(x, shape_n - 1.0) * jnp.power(1.0 + u, -m - 1.0)

def fluxes(head_pad, cond_pad, level_top, open_mask):
    head_mid = head_pad[:, 1:-1]
    cond_mid = cond_pad[:, 1:-1]
    face_x = 0.5 * (cond_pad[:, :-1] + cond_pad[:, 1:]) * open_mask[None, :, None]
    flow_x = face_x * (head_pad[:, 1:] - head_pad[:, :-1])
    net_x = flow_x[:, 1:] - flow_x[:, :-1]
    face_y = 0.5 * (cond_mid[:, :, :-1] + cond_mid[:, :, 1:])
    flow_y = face_y * (head_mid[:, :, 1:] - head_mid[:, :, :-1])
    zero_y = jnp.zeros_like(cond_mid[:, :, :1])
    flow_y = jnp.concatenate([zero_y, flow_y, zero_y], 2)
    net_y = flow_y[:, :, 1:] - flow_y[:, :, :-1]
    face_y = jnp.concatenate([zero_y, face_y, zero_y], 2)
    face_z = 0.5 * (cond_mid[:-1] + cond_mid[1:])
    flow_z = face_z * (1.0 + head_mid[:-1] - head_mid[1:])
    top_flow = level_top[None] * IRRIGATION * cond_mid[:1]
    flow_z = jnp.concatenate([top_flow, flow_z, cond_mid[-1:]], 0)
    net_z = flow_z[:-1] - flow_z[1:]
    face_z = jnp.concatenate([cond_mid[:1], face_z, cond_mid[-1:]], 0)
    cond_sum = face_x[:, 1:] + face_x[:, :-1] + (face_y[:, :, 1:] + face_y[:, :, :-1]) + (face_z[:-1] + face_z[1:])
    return (net_x + net_y + net_z, cond_sum)

def reference(initial_head, sat_conductivity, vg_alpha, vg_n, zone_map, forcing_plan, tensiometer_cells, tensiometer_heads):
    open_mask = jnp.concatenate([jnp.zeros((1,), jnp.float32), jnp.ones((NX - 1,), jnp.float32), jnp.zeros((1,), jnp.float32)])
    sensor = jnp.arange(SENSORS, dtype=jnp.int32)

    def spread(table):
        return jnp.repeat(jnp.repeat(table[zone_map], 2, axis=0), 2, axis=1)

    def one_event(inputs):
        head_start, plan, cells, targets = inputs
        levels = jnp.repeat(plan.astype(jnp.float32), 2, axis=1)
        depth_index = (cells // (ROWS_DEV * NY)).astype(jnp.int32)
        row_index = (sensor // SENS_DEV * ROWS_DEV + cells // NY % ROWS_DEV).astype(jnp.int32)
        column_index = (cells % NY).astype(jnp.int32)

        def misfit_of(tables):
            sat_cond = spread(tables[0])
            air_entry = spread(tables[1])
            shape_n = spread(tables[2])
            head_now = head_start
            for step in range(STEPS):
                cond = conductivity(head_now, sat_cond, air_entry, shape_n)
                store = capacity(head_now, air_entry, shape_n)
                head_pad = jnp.pad(head_now, ((0, 0), (1, 1), (0, 0)))
                cond_pad = jnp.pad(cond, ((0, 0), (1, 1), (0, 0)))
                net_flow, cond_sum = fluxes(head_pad, cond_pad, levels[step][:, None], open_mask)
                step_size = lax.stop_gradient(CFL / jnp.max(cond_sum / store))
                head_now = head_now + step_size * net_flow / store
            picked = head_now[depth_index, row_index, column_index]
            diff = picked - targets
            return (0.5 / EVENTS * jnp.sum(diff * diff), head_now)
        loss, vjp_fn, final = jax.vjp(misfit_of, (sat_conductivity, vg_alpha, vg_n), has_aux=True)
        grads = vjp_fn(jnp.ones_like(loss))[0]
        return (final, loss, grads[0], grads[1], grads[2])
    finals, losses, grad_k, grad_a, grad_m = lax.map(one_event, (initial_head, forcing_plan, tensiometer_cells, tensiometer_heads))
    return (finals, jnp.sum(losses), lax.optimization_barrier(jnp.sum(grad_k, 0)), lax.optimization_barrier(jnp.sum(grad_a, 0)), lax.optimization_barrier(jnp.sum(grad_m, 0)))
```

```python
import jax
import jax.numpy as jnp
from jax import lax
from jax.sharding import PartitionSpec as P

STEPS = 2


CFL = 0.4
IRRIGATION = 0.2
WATER_RANGE = 0.35


def with_halo(x, sides, width):
    for axis, dim in sides:
        count, length = (lax.axis_size(axis), x.shape[dim])
        up = [(i, (i + 1) % count) for i in range(count - 1)]
        down = [(j, i) for i, j in up]
        last = lax.slice_in_dim(x, length - width, length, axis=dim)
        first = lax.slice_in_dim(x, 0, width, axis=dim)
        before = lax.ppermute(last, axis, up)
        after = lax.ppermute(first, axis, down)
        x = jnp.concatenate([before, x, after], axis=dim)
    return x


def conductivity(head_now, sat_cond, air_entry, shape_n):
    x = air_entry * -head_now
    u = jnp.power(x, shape_n)
    m = 1.0 - 1.0 / shape_n
    frac = u / (1.0 + u)
    saturation = jnp.power(1.0 + u, -m)
    return sat_cond * jnp.sqrt(saturation) * jnp.square(1.0 - jnp.power(frac, m))


def capacity(head_now, air_entry, shape_n):
    x = air_entry * -head_now
    u = jnp.power(x, shape_n)
    m = 1.0 - 1.0 / shape_n
    return (
        WATER_RANGE
        * m
        * shape_n
        * air_entry
        * jnp.power(x, shape_n - 1.0)
        * jnp.power(1.0 + u, -m - 1.0)
    )


def fluxes(head_pad, cond_pad, level_top, open_mask):
    head_mid = head_pad[:, 1:-1]
    cond_mid = cond_pad[:, 1:-1]
    face_x = 0.5 * (cond_pad[:, :-1] + cond_pad[:, 1:]) * open_mask[None, :, None]
    flow_x = face_x * (head_pad[:, 1:] - head_pad[:, :-1])
    net_x = flow_x[:, 1:] - flow_x[:, :-1]
    face_y = 0.5 * (cond_mid[:, :, :-1] + cond_mid[:, :, 1:])
    flow_y = face_y * (head_mid[:, :, 1:] - head_mid[:, :, :-1])
    zero_y = jnp.zeros_like(cond_mid[:, :, :1])
    flow_y = jnp.concatenate([zero_y, flow_y, zero_y], 2)
    net_y = flow_y[:, :, 1:] - flow_y[:, :, :-1]
    face_y = jnp.concatenate([zero_y, face_y, zero_y], 2)
    face_z = 0.5 * (cond_mid[:-1] + cond_mid[1:])
    flow_z = face_z * (1.0 + head_mid[:-1] - head_mid[1:])
    top_flow = level_top[None] * IRRIGATION * cond_mid[:1]
    flow_z = jnp.concatenate([top_flow, flow_z, cond_mid[-1:]], 0)
    net_z = flow_z[:-1] - flow_z[1:]
    face_z = jnp.concatenate([cond_mid[:1], face_z, cond_mid[-1:]], 0)
    cond_sum = (
        face_x[:, 1:]
        + face_x[:, :-1]
        + (face_y[:, :, 1:] + face_y[:, :, :-1])
        + (face_z[:-1] + face_z[1:])
    )
    return (net_x + net_y + net_z, cond_sum)


def gather_small(vector, axes, size, groups):
    spread = jnp.broadcast_to(vector[None], (size, 1, vector.shape[-1])) + 0.0
    return lax.all_to_all(spread, axes, 0, 0, tiled=True, axis_index_groups=groups)


def device(x, z_hi, core, y, z_lo):
    return ((x * 2 + z_hi) * 2 + core) * 32 + y * 8 + z_lo


PLANES = [
    [device(x, z_hi, core, y, z_lo) for y in range(4) for x in range(4) for core in range(2)]
    for z_hi in range(2)
    for z_lo in range(8)
]
RINGS = [
    [device(x, z_hi, core, y, z_lo) for z_hi in range(2) for z_lo in range(8)]
    for x in range(4)
    for core in range(2)
    for y in range(4)
]


def zone_onehot(zone_rows, zones):
    flat_zones = zone_rows.reshape(-1)
    return (jnp.arange(zones, dtype=jnp.int32)[:, None] == flat_zones[None, :]).astype(jnp.float32)


def edge_adds(returned, rows):
    depth, width = (returned.shape[0], returned.shape[2])
    middle = jnp.zeros((depth, rows - 2, width), jnp.float32)
    return jnp.concatenate([returned[:, :1], middle, returned[:, 3:]], 1)


def local(
    initial_head,
    sat_conductivity,
    vg_alpha,
    vg_n,
    zone_map,
    forcing_plan,
    tensiometer_cells,
    tensiometer_heads,
):
    head_now = initial_head[0]
    depth, rows, width = head_now.shape
    zones = sat_conductivity.shape[0]
    tables = jnp.stack([sat_conductivity, vg_alpha, vg_n])
    position = lax.axis_index("row")
    count = lax.axis_size("row")
    events = initial_head.shape[0] * lax.axis_size("event")
    lower_open = (position > 0).astype(jnp.float32)
    upper_open = (position < count - 1).astype(jnp.float32)
    open_mask = jnp.concatenate(
        [lower_open[None], jnp.ones((rows - 1,), jnp.float32), upper_open[None]]
    )
    levels = jnp.repeat(forcing_plan[0].astype(jnp.float32), 2, axis=1)
    highest = lax.Precision.HIGHEST
    onehot = zone_onehot(zone_map, zones)
    values = jnp.dot(tables, onehot, precision=highest).reshape(3, rows // 2, width // 2)
    values = jnp.repeat(jnp.repeat(values, 2, axis=1), 2, axis=2)
    params = (values[0], values[1], values[2])

    def local_cells(head_cells, cell_params):
        return (
            conductivity(head_cells, cell_params[0], cell_params[1], cell_params[2]),
            capacity(head_cells, cell_params[1], cell_params[2]),
        )

    records = []
    for step in range(STEPS):
        level_top = levels[step][:, None]
        (cond, store), vjp_cells = jax.vjp(local_cells, head_now, params)
        padded = with_halo(jnp.stack([head_now, cond]), (("row", 2),), 1)

        def local_flow(head_pad, cond_pad, level_top=level_top):
            return fluxes(head_pad, cond_pad, level_top, open_mask)

        (net_flow, cond_sum), vjp_flow = jax.vjp(local_flow, padded[0], padded[1])
        own_rate = jnp.max(cond_sum / store)
        rate = jnp.max(gather_small(jnp.broadcast_to(own_rate, (1, 128)), "row", 32, None))
        step_size = CFL / rate
        head_now = head_now + step_size * net_flow / store
        records.append((vjp_cells, vjp_flow, net_flow, cond_sum, store, step_size))
    flat_final = head_now.reshape(-1)
    cells = tensiometer_cells[0]
    diff = flat_final[cells] - tensiometer_heads[0]
    local_misfit = 0.5 / events * jnp.sum(diff * diff)
    adjoint = jnp.zeros_like(flat_final).at[cells].add(diff / events).reshape(head_now.shape)
    grad_cells = jnp.zeros_like(values)
    for step in reversed(range(STEPS)):
        vjp_cells, vjp_flow, net_flow, cond_sum, store, step_size = records[step]
        grad_net = adjoint * step_size / store
        grad_store = -adjoint * step_size * net_flow / (store * store)
        zero_sum = jnp.zeros_like(cond_sum)
        grad_head_pad, grad_cond_pad = vjp_flow((grad_net, zero_sum))
        rims = jnp.stack(
            [
                jnp.stack([grad_head_pad[:, 0], grad_head_pad[:, -1]], 1),
                jnp.stack([grad_cond_pad[:, 0], grad_cond_pad[:, -1]], 1),
            ]
        )
        returned = with_halo(rims, (("row", 2),), 1)
        grad_inner = grad_head_pad[:, 1:-1] + edge_adds(returned[0], rows)
        grad_cond = grad_cond_pad[:, 1:-1] + edge_adds(returned[1], rows)
        grad_from_cells, grad_params = vjp_cells((grad_cond, grad_store))
        adjoint = adjoint + grad_inner + grad_from_cells
        grad_cells = grad_cells + jnp.stack(grad_params)
    block_grads = grad_cells.reshape(3, rows // 2, 2, width // 2, 2).sum(axis=(2, 4))
    block_grads = block_grads.reshape(3, -1)
    zone_grads = lax.dot_general(block_grads, onehot, (((1,), (1,)), ((), ())), precision=highest)
    sums = jnp.concatenate([zone_grads.reshape(1, -1), jnp.broadcast_to(local_misfit, (1, 128))], 1)
    sums = jnp.sum(gather_small(sums, ("event", "row"), 32, PLANES), 0)
    sums = jnp.sum(gather_small(sums, ("event", "row"), 16, RINGS), 0)[0]
    grad_k, grad_a, grad_m = sums[:zones], sums[zones : 2 * zones], sums[2 * zones : 3 * zones]
    misfit = sums[3 * zones]
    return (head_now[None], misfit, grad_k, grad_a, grad_m)


def solution(mesh):
    return jax.shard_map(
        local,
        mesh=mesh,
        in_specs=(
            P("event", None, "row", None),
            P(),
            P(),
            P(),
            P("row", None),
            P("event", None, "row"),
            P("event", "row"),
            P("event", "row"),
        ),
        out_specs=(P("event", None, "row", None), P(), P(), P(), P()),
        check_vma=False,
    )
```

```python
import jax
import jax.numpy as jnp
from jax import lax
from jax.experimental import pallas as pl
from jax.experimental.pallas import tpu as pltpu
from jax.sharding import PartitionSpec as P

CFL = 0.4
IRRIGATION = 0.2
WATER_RANGE = 0.35

TILES = 6
SUB = 8
WIDTH = 384
ROWS = 8
FIELD = (ROWS, TILES, SUB, WIDTH)
OWN = (4, TILES, SUB, WIDTH)
NEAR = 28
ZONES = 256
KS, AL, N, N1, M, MP, IC0, IN1, LEV0, LEV1, IKS, IAL = range(12)
F32 = jnp.float32


def device(x, z_hi, core, y, z_lo):
    return ((x * 2 + z_hi) * 2 + core) * 32 + y * 8 + z_lo


PLANES = [
    [device(x, z_hi, core, y, z_lo) for y in range(4) for x in range(4) for core in range(2)]
    for z_hi in range(2)
    for z_lo in range(8)
]
RINGS = [
    [device(x, z_hi, core, y, z_lo) for z_hi in range(2) for z_lo in range(8)]
    for x in range(4)
    for core in range(2)
    for y in range(4)
]


def lanes_left(x):
    return pltpu.roll(x, WIDTH - 1, 1)


def lanes_right(x):
    return pltpu.roll(x, 1, 1)


def subs_up(x):
    return pltpu.roll(x, SUB - 1, 0)


def subs_down(x):
    return pltpu.roll(x, 1, 0)


def iota(shape, dim):
    return lax.broadcasted_iota(jnp.int32, shape, dim)


def split3(x):
    hi = x.astype(jnp.bfloat16)
    rest = x - hi.astype(F32)
    mid = rest.astype(jnp.bfloat16)
    return hi, mid, (rest - mid.astype(F32)).astype(jnp.bfloat16)


def exact_dot(pick, x, dims=(((1,), (0,)), ((), ()))):
    parts = [lax.dot_general(pick, part, dims, preferred_element_type=F32) for part in split3(x)]
    return parts[0] + (parts[1] + parts[2])


def pack_kernel(head, zone, plan, own, up, down, zones):
    for depth in range(TILES * SUB):
        block = head[depth]
        j, s = depth % TILES, depth // TILES
        for row in range(4):
            own[row, j, s : s + 1, :] = block[row : row + 1, :]
    wide = (iota((192, WIDTH), 1) // 2 == iota((192, WIDTH), 0)).astype(F32)
    blocks = jnp.dot(zone[...].astype(F32), wide, preferred_element_type=F32)
    zones[...] = blocks
    sub = iota((SUB, WIDTH), 0)
    for pair, out in ((0, down), (1, up)):
        out[0:TILES] = own[2 * pair]
        out[TILES : 2 * TILES] = own[2 * pair + 1]
        level = plan[0, pair].astype(F32)
        ids = jnp.broadcast_to(blocks[pair : pair + 1, :], (SUB, WIDTH))
        out[2 * TILES] = jnp.where(sub == 0, ids, level)


def cell_math(head, p):
    wet = jnp.log(-p[AL] * head)
    u = jnp.exp(p[N] * wet)
    d = 1.0 + u
    w = jnp.log(d)
    inv = 1.0 / d
    r = u * inv
    mw = p[M] * w
    q = jnp.exp(-0.5 * mw)
    f = jnp.exp(p[N1] * wet - mw)
    t = 1.0 - f
    kq = p[KS] * q * t
    half, twice = -0.5 * t, 2.0 * f
    e1 = p[MP] * w + p[M] * wet * r
    cond = kq * t
    cond_l = kq * p[N1] * (half * r - twice * inv)
    cond_n = kq * (half * e1 - twice * (wet - e1))
    inv_store = d * p[IC0] / f
    store_l = p[N] - r * (2.0 * p[N] - 1.0)
    store_n = p[IN1] + wet - e1 - r * wet
    return cond, cond_l, cond_n, inv_store, store_l, store_n


def row_params(prm, r):
    return [prm[r, i : i + 1, :] for i in range(12)]


def masks():
    last = iota((SUB, WIDTH), 1) == WIDTH - 1
    sub = iota((SUB, WIDTH), 0)
    return last, sub == 0, sub == SUB - 1


def row_open(meta, r):
    low = jnp.where(r == 2, meta[1], jnp.where(r == 6, meta[2], 1)).astype(F32)
    high = jnp.where(r == 5, meta[2], jnp.where(r == 1, meta[1], 1)).astype(F32)
    return low, high


def net_row(h, k, r, top, low, high):
    last, is_top, is_bottom = masks()
    hs = [h[r, j] for j in range(TILES)]
    ks = [k[r, j] for j in range(TILES)]

    def face(j):
        if j < TILES - 1:
            kd = 0.5 * (ks[j] + ks[j + 1])
            return kd, kd * (1.0 + hs[j] - hs[j + 1])
        kd = 0.5 * (ks[j] + subs_up(ks[0]))
        flow = kd * (1.0 + hs[j] - subs_up(hs[0]))
        return jnp.where(is_bottom, ks[j], kd), jnp.where(is_bottom, ks[j], flow)

    final = face(TILES - 1)
    above = (
        jnp.where(is_top, ks[0], subs_down(final[0])),
        jnp.where(is_top, top * ks[0], subs_down(final[1])),
    )
    for j in range(TILES):
        below = final if j == TILES - 1 else face(j)
        hj, kj = hs[j], ks[j]
        kf = jnp.where(last, 0.0, 0.5 * (kj + lanes_left(kj)))
        flow = kf * (lanes_left(hj) - hj)
        k_low = 0.5 * low * (k[r - 1, j] + kj)
        k_high = 0.5 * high * (k[r + 1, j] + kj)
        net = flow - lanes_right(flow) + above[1] - below[1]
        net = net + k_low * (h[r - 1, j] - hj) + k_high * (h[r + 1, j] - hj)
        total = kf + lanes_right(kf) + above[0] + below[0] + k_low + k_high
        above = below
        yield j, net, total


def first_kernel(
    meta, plan, tab_k, tab_a, tab_n, own, zones, from_low, from_high,
    h0, k1, kl1, kn1, ic1, g1, p1, q1, prm, zrel, spread,
):
    position, lower, upper = meta[0], meta[1], meta[2]
    has_low, has_high = lower > 0, upper > 0
    for row in range(2):
        for j in range(TILES):
            h0[row, j] = jnp.where(has_low, from_low[row * TILES + j], own[0, j])
            h0[6 + row, j] = jnp.where(has_high, from_high[row * TILES + j], own[3, j])
    h0[2:6] = own[...]
    extra_low, extra_high = from_low[2 * TILES], from_high[2 * TILES]
    z_low = jnp.where(has_low, extra_low[0:1, :], zones[0:1, :])
    z_high = jnp.where(has_high, extra_high[0:1, :], zones[1:2, :])
    sub = iota((SUB, WIDTH), 0)

    def by_row(a, b, c, d):
        return jnp.where(sub < 4, jnp.where(sub < 2, a, b), jnp.where(sub < 6, c, d))

    zone = by_row(z_low, zones[0:1, :], zones[1:2, :], z_high).astype(jnp.int32)
    base = 8 * position - 4
    rel = (zone - base) & (ZONES - 1)
    zrel[...] = rel
    sat = jnp.ones((SUB, WIDTH), F32)
    alpha, n = sat, 2.0 * sat
    for i in range(NEAR):
        at = (base + i) & (ZONES - 1)
        here = rel == i
        sat = jnp.where(here, tab_k[at], sat)
        alpha = jnp.where(here, tab_a[at], alpha)
        n = jnp.where(here, tab_n[at], n)
    n1 = n - 1.0
    lev_0 = by_row(extra_low[1:2, :], plan[0, 0].astype(F32), plan[0, 1].astype(F32), extra_high[1:2, :])
    lev_1 = by_row(0.0, plan[1, 0].astype(F32), plan[1, 1].astype(F32), 0.0) + 0.0 * sat
    made = (
        sat, alpha, n, n1, 1.0 - 1.0 / n, 1.0 / (n * n), 1.0 / (WATER_RANGE * n1 * alpha), 1.0 / n1,
        IRRIGATION * lev_0, IRRIGATION * lev_1, 1.0 / sat, 1.0 / alpha,
    )
    for i, value in enumerate(made):
        for r in range(ROWS):
            prm[r, i : i + 1, :] = value[r : r + 1, :]

    def cells(r, carry):
        p = row_params(prm, r)
        for j in range(TILES):
            k1[r, j], kl1[r, j], kn1[r, j], ic1[r, j], p1[r, j], q1[r, j] = cell_math(h0[r, j], p)
        return carry

    lax.fori_loop(0, ROWS, cells, 0)

    def flow(r, most):
        low, high = row_open(meta, r)
        is_own = jnp.logical_and(r >= 2, r <= 5)
        real = jnp.logical_or(is_own, jnp.where(r < 2, has_low, has_high))
        for j, net, total in net_row(h0, k1, r, prm[r, LEV0 : LEV0 + 1, :], low, high):
            ic = ic1[r, j]
            g = jnp.where(real, net * ic, 0.0)
            g1[r, j] = g
            p1[r, j] = g * p1[r, j]
            q1[r, j] = g * q1[r, j]
            most = jnp.maximum(most, jnp.where(is_own, total * ic, 0.0))
        return most

    most = lax.fori_loop(1, 7, flow, jnp.zeros((SUB, WIDTH), F32))
    most = jnp.maximum(jnp.maximum(most[:, :128], most[:, 128:256]), most[:, 256:])
    most = jnp.max(most, 0, keepdims=True)
    spread[...] = jnp.broadcast_to(most[None], spread.shape)


def second_kernel(
    meta, rates, sensors, h0, k1, kl1, kn1, ic1, g1, p1, q1, prm, zrel,
    h1_out, g2, spread,
    h1, k2, kl2, kn2, ic2, sl2, sn2, va, vb, wa, wb, w0, w1, w2, maps,
):
    size = CFL / jnp.max(rates[...])
    nothing = jnp.zeros((TILES, SUB, WIDTH), F32)
    for r in (0, ROWS - 1):
        for ref in (h1, k2, w0, w1, w2):
            ref[r] = nothing
    for r in (1, 6):
        for ref in (va, vb, wa, wb):
            ref[r] = nothing
    maps[...] = jnp.zeros(maps.shape, F32)

    def cells(r, carry):
        p = row_params(prm, r)
        for j in range(TILES):
            head = h0[r, j] + size * g1[r, j]
            h1[r, j] = head
            k2[r, j], kl2[r, j], kn2[r, j], ic2[r, j], sl2[r, j], sn2[r, j] = cell_math(head, p)
        return carry

    lax.fori_loop(1, 7, cells, 0)

    def flow(r, most):
        low, high = row_open(meta, r)
        for j, net, total in net_row(h1, k2, r, prm[r, LEV1 : LEV1 + 1, :], low, high):
            ic = ic2[r, j]
            g2[r - 2, j] = net * ic
            h1_out[r - 2, j] = h1[r, j]
            most = jnp.maximum(most, total * ic)
        return most

    most = jnp.max(lax.fori_loop(2, 6, flow, jnp.zeros((SUB, WIDTH), F32)))

    def places(cell):
        line = jnp.floor((cell + 0.5) * (1.0 / WIDTH))
        column = cell - WIDTH * line
        depth = jnp.floor((line + 0.5) * 0.25)
        block = jnp.floor((depth + 0.5) * (1.0 / TILES))
        return (line - 4.0 * depth) * 48.0 + (depth - TILES * block) * 8.0 + block, column

    count = sensors.shape[1]
    wide = sensors[...]
    tall = jnp.transpose(wide)
    line_wide = places(wide[0:1, :])[0].astype(jnp.int32)
    line_tall, column_tall = places(tall[:, 0:1])
    goal = tall[:, 1:2]
    pick = (iota((count, 192), 1) == line_tall.astype(jnp.int32)).astype(F32).astype(jnp.bfloat16)
    put = (iota((192, count), 0) == line_wide).astype(F32).astype(jnp.bfloat16)
    column = iota((count, WIDTH), 1) == column_tall.astype(jnp.int32)
    field_g = g2[...].reshape(192, WIDTH)
    field_h = h1_out[...].reshape(192, WIDTH) + size * field_g
    seen_h = jnp.sum(jnp.where(column, exact_dot(pick, field_h), 0.0), 1, keepdims=True)
    seen_g = jnp.sum(jnp.where(column, exact_dot(pick, field_g), 0.0), 1, keepdims=True)
    diff = seen_h - goal
    events = 16.0
    loss = (
        jnp.sum(diff * diff) * (0.5 / events),
        jnp.sum(diff * seen_g) * (1.0 / events),
        jnp.sum(seen_g * seen_g) * (0.5 / events),
    )
    va[2:6] = exact_dot(put, jnp.where(column, diff * (1.0 / events), 0.0)).reshape(OWN)
    vb[2:6] = exact_dot(put, jnp.where(column, seen_g * (1.0 / events), 0.0)).reshape(OWN)

    def scaled(r, carry):
        for j in range(TILES):
            ic = ic2[r, j]
            wa[r, j] = va[r, j] * ic
            wb[r, j] = vb[r, j] * ic
        return carry

    lax.fori_loop(2, 6, scaled, 0)
    last, is_top, is_bottom = masks()

    def back_two(r, carry):
        low, high = row_open(meta, r)
        top = prm[r, LEV1 : LEV1 + 1, :]
        own = jnp.logical_and(r >= 2, r <= 5)
        hs = [h1[r, j] for j in range(TILES)]
        ks = [k2[r, j] for j in range(TILES)]
        sums = [jnp.zeros((SUB, WIDTH), F32) for _ in range(12)]
        ws = [[w[r, j] for j in range(TILES)] for w in (wa, wb)]

        def face(j):
            if j < TILES - 1:
                half = 0.5 * (1.0 + hs[j] - hs[j + 1])
                kd = 0.5 * (ks[j] + ks[j + 1])
                out = []
                for w in ws:
                    dw = w[j + 1] - w[j]
                    out.append((half * dw, kd * dw))
                return out
            half = 0.5 * (1.0 + hs[j] - subs_up(hs[0]))
            kd = 0.5 * (ks[j] + subs_up(ks[0]))
            out = []
            for w in ws:
                dw = subs_up(w[0]) - w[j]
                out.append((jnp.where(is_bottom, -w[j], half * dw), jnp.where(is_bottom, 0.0, kd * dw)))
            return out

        final = face(TILES - 1)
        above = [
            (jnp.where(is_top, top * w[0], subs_down(f[0])), subs_down(f[1]))
            for w, f in zip(ws, final)
        ]
        for j in range(TILES):
            below = final if j == TILES - 1 else face(j)
            hj, kj = hs[j], ks[j]
            h_low, h_high = h1[r - 1, j], h1[r + 1, j]
            half_c = jnp.where(last, 0.0, 0.5 * (lanes_left(hj) - hj))
            kf = jnp.where(last, 0.0, 0.5 * (lanes_left(kj) + kj))
            half_l, half_h = 0.5 * low * (h_low - hj), 0.5 * high * (h_high - hj)
            k_low, k_high = 0.5 * low * (k2[r - 1, j] + kj), 0.5 * high * (k2[r + 1, j] + kj)
            kl, kn = kl2[r, j], kn2[r, j]
            inv_h = 1.0 / hj
            g = jnp.where(own, g2[jnp.clip(r - 2, 0, 3), j], 0.0)
            gl, gn = g * sl2[r, j], g * sn2[r, j]
            back = []
            for part, (w_ref, v_ref) in enumerate(((wa, va), (wb, vb))):
                w = ws[part][j]
                dw = w - lanes_left(w)
                e, f = half_c * dw, kf * dw
                d_low, d_high = w - w_ref[r - 1, j], w - w_ref[r + 1, j]
                gk = e + lanes_right(e) + below[part][0] + above[part][0]
                gk = gk + half_l * d_low + half_h * d_high
                gh = lanes_right(f) - f + below[part][1] - above[part][1]
                gh = gh - k_low * d_low - k_high * d_high
                v = v_ref[r, j]
                to_l = gk * kl - v * gl
                sums[3 * part] += gk * kj
                sums[3 * part + 1] += to_l
                sums[3 * part + 2] += gk * kn - v * gn
                back.append((v, gh + (to_l + v * g) * inv_h))
            (v_a, j_a), (v_b, j_b) = back
            us = (v_a + size * j_a, v_b + j_a + size * j_b, j_b)
            ic, pp, qq = ic1[r, j], p1[r, j], q1[r, j]
            for i, (u, w_ref) in enumerate(zip(us, (w0, w1, w2))):
                w_ref[r, j] = u * ic
                sums[6 + 2 * i] -= u * pp
                sums[7 + 2 * i] -= u * qq
            above = below
        flat = [jnp.sum(x, 0, keepdims=True) for x in sums]
        for q in range(3):
            of_a, of_b = flat[q], flat[3 + q]
            rows = [size * of_a, of_a + size * of_b, of_b]
            for c in range(3):
                if q > 0:
                    rows[c] = rows[c] + size * flat[6 + 2 * c + q - 1]
                maps[r, 4 * q + c : 4 * q + c + 1, :] = rows[c]
        return carry

    for ref in (wa, wb):
        ref[0] = nothing
        ref[7] = nothing
    lax.fori_loop(1, 7, back_two, 0)

    def back_one(r, carry):
        low, high = row_open(meta, r)
        top = prm[r, LEV0 : LEV0 + 1, :]
        before, after = jnp.maximum(r - 1, 0), jnp.minimum(r + 1, ROWS - 1)
        hs = [h0[r, j] for j in range(TILES)]
        refs = (w0, w1, w2)
        ws = [[w[r, j] for j in range(TILES)] for w in refs]
        sums = [jnp.zeros((SUB, WIDTH), F32) for _ in range(9)]

        def face(j):
            if j < TILES - 1:
                half = 0.5 * (1.0 + hs[j] - hs[j + 1])
                return [half * (w[j + 1] - w[j]) for w in ws]
            half = 0.5 * (1.0 + hs[j] - subs_up(hs[0]))
            return [jnp.where(is_bottom, -w[j], half * (subs_up(w[0]) - w[j])) for w in ws]

        final = face(TILES - 1)
        above = [jnp.where(is_top, top * w[0], subs_down(f)) for w, f in zip(ws, final)]
        for j in range(TILES):
            below = final if j == TILES - 1 else face(j)
            hj = hs[j]
            half_c = jnp.where(last, 0.0, 0.5 * (lanes_left(hj) - hj))
            half_l = 0.5 * low * (h0[before, j] - hj)
            half_h = 0.5 * high * (h0[after, j] - hj)
            kj, kl, kn = k1[r, j], kl1[r, j], kn1[r, j]
            for part, w_ref in enumerate(refs):
                w = ws[part][j]
                e = half_c * (w - lanes_left(w))
                gk = e + lanes_right(e) + below[part] + above[part]
                gk = gk + half_l * (w - w_ref[before, j]) + half_h * (w - w_ref[after, j])
                sums[3 * part] += gk * kj
                sums[3 * part + 1] += gk * kl
                sums[3 * part + 2] += gk * kn
            above = below
        inv_k, inv_a = prm[r, IKS : IKS + 1, :], prm[r, IAL : IAL + 1, :]
        for q in range(3):
            for c in range(3):
                at = 4 * q + c
                row = maps[r, at : at + 1, :] + size * jnp.sum(sums[3 * c + q], 0, keepdims=True)
                maps[r, at : at + 1, :] = row if q == 2 else row * (inv_k if q == 0 else inv_a)
        return carry

    lax.fori_loop(0, ROWS, back_one, 0)

    left = jnp.concatenate([maps[r] for r in range(ROWS)], 1)
    near = zrel[...]
    zone_id = iota((32, WIDTH), 0)
    onehot = jnp.concatenate([(zone_id == near[r : r + 1, :]).astype(F32) for r in range(ROWS)], 1)
    onehot = onehot.astype(jnp.bfloat16)
    nt = (((1,), (1,)), ((), ()))
    parts = [lax.dot_general(part, onehot, nt, preferred_element_type=F32) for part in split3(left)]
    by_zone = parts[0] + (parts[1] + parts[2])
    fields = [by_zone[4 * q : 4 * q + 4, :] for q in range(3)]
    sub4 = iota((4, 32), 0)
    fields.append(jnp.where(sub4 == 0, loss[0], jnp.where(sub4 == 1, loss[1], loss[2])))
    sums = jnp.concatenate(fields, 1)
    state = jnp.where(iota((4, 128), 1) < 64, most, size)
    payload = jnp.where(iota((4, 128), 0) == 3, state, sums)
    spread[...] = jnp.broadcast_to(payload[None], spread.shape)


def ring_kernel(parts, spread):
    lane = iota((SUB, 256), 1)
    total = jnp.zeros((SUB, 256), F32)
    blank = jnp.zeros((SUB, 128), F32)
    most = None
    loss = jnp.zeros((SUB, 256), F32)
    for z in range(8):
        tile = jnp.concatenate([parts[z], parts[8 + z]], 0)
        most = tile if most is None else jnp.maximum(most, tile)
        tile = jnp.concatenate([tile, blank], 1)
        for q in range(3):
            start = 84 * q + 8 * z
            moved = pltpu.roll(tile, (start - 32 * q) % 256, 1)
            total = total + jnp.where(jnp.logical_and(lane >= start, lane < start + NEAR), moved, 0.0)
        loss = loss + tile
    total = jnp.where(lane == 252, pltpu.roll(loss, 252 - 96, 1), total)
    state = jnp.concatenate(
        [jnp.broadcast_to(most[:, 0:1], (SUB, 128)), jnp.broadcast_to(most[:, 64:65], (SUB, 128))], 1
    )
    total = jnp.where(iota((SUB, 256), 0) % 4 == 3, state, total)
    spread[...] = jnp.broadcast_to(total[None], spread.shape)


def last_kernel(meta, parts, h1, g2, final, grad_k, grad_a, grad_n, misfit, rates):
    sub = iota((SUB, 256), 0)
    power = sub % 4
    sums = [jnp.zeros((SUB, 256), F32) for _ in range(4)]
    for pair in range(8):
        tiles = [parts[8 * y + pair] for y in range(4)]
        most = jnp.maximum(jnp.maximum(tiles[0], tiles[1]), jnp.maximum(tiles[2], tiles[3]))
        step = CFL / most
        rates[pair] = step
        moves = []
        for row in (3, 7):
            move = step[row : row + 1, :128] - most[row : row + 1, 128:]
            moves.append(jnp.concatenate([move, move], 1))
        move = jnp.where(sub < 4, moves[0], moves[1])
        weight = jnp.where(power == 0, 1.0, jnp.where(power == 1, move, move * move))
        for y in range(4):
            sums[y] = sums[y] + jnp.where(power == 3, 0.0, tiles[y] * weight)
    lane = iota((1, 256), 1)
    rows = [jnp.sum(x, 0, keepdims=True) for x in sums]
    for q, out in enumerate((grad_k, grad_a, grad_n)):
        total = jnp.zeros((1, 256), F32)
        for y in range(4):
            field = rows[y] if q == 0 else pltpu.roll(rows[y], 256 - 84 * q, 1)
            total = total + pltpu.roll(jnp.where(lane < 84, field, 0.0), (64 * y - 4) % 256, 1)
        out[...] = total
    misfit[0, 0] = jnp.sum(jnp.where(lane == 252, rows[0] + rows[1] + rows[2] + rows[3], 0.0))
    mine = rates[meta[3]]
    size = jnp.where(meta[4] == 0, mine[3:4, :128], mine[7:8, :128])
    size = jnp.concatenate([size, size, size], 1)
    for j in range(TILES):
        for row in range(4):
            tile = h1[row, j] + size * g2[row, j]
            for s in range(SUB):
                final[TILES * s + j, row : row + 1, :] = tile[s : s + 1, :]


VMEM = pl.BlockSpec(memory_space=pltpu.VMEM)
SMEM = pl.BlockSpec(memory_space=pltpu.SMEM)


def call(kernel, name, ins, outs, out_specs=None, scratch=()):
    out_shape = [jax.ShapeDtypeStruct(*o) if isinstance(o, tuple) else o for o in outs]
    return pl.pallas_call(
        kernel,
        name=name,
        in_specs=ins,
        out_specs=out_specs or [VMEM] * len(outs),
        out_shape=out_shape,
        scratch_shapes=scratch,
        compiler_params=pltpu.CompilerParams(vmem_limit_bytes=48 * 1024 * 1024),
    )


def local(
    initial_head,
    sat_conductivity,
    vg_alpha,
    vg_n,
    zone_map,
    forcing_plan,
    tensiometer_cells,
    tensiometer_heads,
):
    position = lax.axis_index("row")
    count = lax.axis_size("row")
    event = lax.axis_index("event")
    meta = jnp.stack(
        [
            position,
            (position > 0).astype(jnp.int32),
            (position < count - 1).astype(jnp.int32),
            event // 4 * 2 + event % 2,
            event // 2 % 2,
        ]
    )
    plan = forcing_plan[0]
    edge = (2 * TILES + 1, SUB, WIDTH)
    own, up, down, zones = call(
        pack_kernel,
        "pack_edges",
        [VMEM, VMEM, SMEM],
        [(OWN, F32), (edge, F32), (edge, F32), ((2, WIDTH), F32)],
    )(initial_head[0], zone_map, plan)
    upward = [(i, i + 1) for i in range(count - 1)]
    from_low = lax.ppermute(up, "row", upward)
    from_high = lax.ppermute(down, "row", [(j, i) for i, j in upward])
    first = call(
        first_kernel,
        "first_step",
        [SMEM] * 5 + [VMEM] * 4,
        [(FIELD, F32)] * 8
        + [((ROWS, 16, WIDTH), F32), ((ROWS, WIDTH), jnp.int32), ((32, 1, 128), F32)],
    )(meta, plan, sat_conductivity, vg_alpha, vg_n, own, zones, from_low, from_high)
    fields, rates = first[:-1], first[-1]
    rates = lax.all_to_all(rates, "row", 0, 0, tiled=True)
    sensors = jnp.concatenate(
        [tensiometer_cells.astype(F32), tensiometer_heads, jnp.zeros((6, 256), F32)], 0
    )
    scratch = [pltpu.VMEM(FIELD, F32)] * 14 + [pltpu.VMEM((ROWS, 16, WIDTH), F32)]
    h1, g2, sums = call(
        second_kernel,
        "second_step_and_adjoint",
        [SMEM] + [VMEM] * 12,
        [(OWN, F32), (OWN, F32), ((16, 4, 128), F32)],
        scratch=scratch,
    )(meta, rates, sensors, *fields)
    sums = lax.all_to_all(sums, ("event", "row"), 0, 0, tiled=True, axis_index_groups=RINGS)
    (sums,) = call(ring_kernel, "ring_sums", [VMEM], [((32, SUB, 256), F32)])(sums)
    sums = lax.all_to_all(sums, ("event", "row"), 0, 0, tiled=True, axis_index_groups=PLANES)
    row = ((1, ZONES), F32)
    final, grad_k, grad_a, grad_n, misfit = call(
        last_kernel,
        "final_head_and_sums",
        [SMEM, VMEM, VMEM, VMEM],
        [((48, 4, WIDTH), F32), row, row, row, ((1, 1), F32)],
        [VMEM] * 4 + [SMEM],
        scratch=[pltpu.VMEM((8, SUB, 256), F32)],
    )(meta, sums, h1, g2)
    return (final[None], misfit[0, 0], grad_k[0], grad_a[0], grad_n[0])


def solution(mesh):
    return jax.shard_map(
        local,
        mesh=mesh,
        in_specs=(
            P("event", None, "row", None),
            P(),
            P(),
            P(),
            P("row", None),
            P("event", None, "row"),
            P("event", "row"),
            P("event", "row"),
        ),
        out_specs=(P("event", None, "row", None), P(), P(), P(), P()),
        check_vma=False,
    )
```

```python
import jax
import jax.numpy as jnp
from jax import lax
from jax.experimental import pallas as pl
from jax.experimental.pallas import tpu as pltpu
from jax.sharding import PartitionSpec as P

CFL = 0.4
IRRIGATION = 0.2
WATER_RANGE = 0.35

TILES = 6
SUB = 8
WIDTH = 384
ROWS = 8
FIELD = (ROWS, TILES, SUB, WIDTH)
OWN = (4, TILES, SUB, WIDTH)
NEAR = 28
ZONES = 256
KS, AL, N, N1, M, MP, IC0, IN1, LEV0, LEV1, IKS, IAL = range(12)
F32 = jnp.float32


def device(x, z_hi, core, y, z_lo):
    return ((x * 2 + z_hi) * 2 + core) * 32 + y * 8 + z_lo


PLANES = [
    [device(x, z_hi, core, y, z_lo) for y in range(4) for x in range(4) for core in range(2)]
    for z_hi in range(2)
    for z_lo in range(8)
]
RINGS = [
    [device(x, z_hi, core, y, z_lo) for z_hi in range(2) for z_lo in range(8)]
    for x in range(4)
    for core in range(2)
    for y in range(4)
]


def lanes_left(x):
    return pltpu.roll(x, WIDTH - 1, 1)


def lanes_right(x):
    return pltpu.roll(x, 1, 1)


def subs_up(x):
    return pltpu.roll(x, SUB - 1, 0)


def subs_down(x):
    return pltpu.roll(x, 1, 0)


def iota(shape, dim):
    return lax.broadcasted_iota(jnp.int32, shape, dim)


def split3(x):
    hi = x.astype(jnp.bfloat16)
    rest = x - hi.astype(F32)
    mid = rest.astype(jnp.bfloat16)
    return hi, mid, (rest - mid.astype(F32)).astype(jnp.bfloat16)


def exact_dot(pick, x, dims=(((1,), (0,)), ((), ()))):
    parts = [lax.dot_general(pick, part, dims, preferred_element_type=F32) for part in split3(x)]
    return parts[0] + (parts[1] + parts[2])


def axes():
    event = lax.axis_index("event")
    return lax.axis_index("row"), event // 4 * 2 + event % 2, event // 2 % 2


def pack_kernel(head_in, zone_in, plan_in, own, send_odd, send_even, zones, head, zone, plan, sems):
    copies = [
        pltpu.make_async_copy(src, dst, sems.at[i])
        for i, (src, dst) in enumerate(((head_in, head), (zone_in, zone), (plan_in, plan)))
    ]
    for copy in copies:
        copy.start()
    wide = (iota((192, WIDTH), 1) // 2 == iota((192, WIDTH), 0)).astype(F32)
    copies[1].wait()
    copies[2].wait()
    blocks = jnp.dot(zone[...].astype(F32), wide, preferred_element_type=F32)
    zones[...] = blocks
    level = plan[...].astype(F32)
    copies[0].wait()
    for depth in range(TILES * SUB):
        block = head[depth]
        j, s = depth % TILES, depth // TILES
        for row in range(4):
            own[row, j, s : s + 1, :] = block[row : row + 1, :]
    sub = iota((SUB, WIDTH), 0)
    odd = lax.axis_index("row") % 2 == 1

    def fill(out, pair):
        out[0:TILES] = own[2 * pair]
        out[TILES : 2 * TILES] = own[2 * pair + 1]
        out[2 * TILES] = jnp.where(sub == 0, blocks[pair : pair + 1, :], level[0:1, pair : pair + 1])

    @pl.when(odd)
    def _():
        fill(send_odd, 1)
        fill(send_even, 0)

    @pl.when(jnp.logical_not(odd))
    def _():
        fill(send_odd, 0)
        fill(send_even, 1)


def cell_math(head, p, with_store=True):
    wet = jnp.log(-p[AL] * head)
    u = jnp.exp(p[N] * wet)
    d = 1.0 + u
    w = jnp.log(d)
    inv = 1.0 / d
    r = u * inv
    mw = p[M] * w
    q = jnp.exp(-0.5 * mw)
    f = jnp.exp(p[N1] * wet - mw)
    t = 1.0 - f
    kq = p[KS] * q * t
    half, twice = -0.5 * t, 2.0 * f
    e1 = p[MP] * w + p[M] * wet * r
    cond = kq * t
    cond_l = kq * p[N1] * (half * r - twice * inv)
    cond_n = kq * (half * e1 - twice * (wet - e1))
    if not with_store:
        return cond, cond_l, cond_n
    inv_store = d * p[IC0] / f
    store_l = p[N] - r * (2.0 * p[N] - 1.0)
    store_n = p[IN1] + wet - e1 - r * wet
    return cond, cond_l, cond_n, inv_store, store_l, store_n


def derived(sat, alpha, n):
    n1 = n - 1.0
    return (
        sat, alpha, n, n1, 1.0 - 1.0 / n, 1.0 / (n * n), 1.0 / (WATER_RANGE * n1 * alpha), 1.0 / n1,
    )


def row_params(prm, r):
    return [prm[r, i : i + 1, :] for i in range(8)]


def masks():
    last = iota((SUB, WIDTH), 1) == WIDTH - 1
    sub = iota((SUB, WIDTH), 0)
    return last, sub == 0, sub == SUB - 1


def row_open(position, r):
    lower = (position > 0).astype(jnp.int32)
    upper = (position < lax.axis_size("row") - 1).astype(jnp.int32)
    low = jnp.where(r == 2, lower, jnp.where(r == 6, upper, 1)).astype(F32)
    high = jnp.where(r == 5, upper, jnp.where(r == 1, lower, 1)).astype(F32)
    return low, high


def net_row(h, k, r, top, low, high):
    last, is_top, is_bottom = masks()
    hs = [h[r, j] for j in range(TILES)]
    ks = [k[r, j] for j in range(TILES)]

    def face(j):
        if j < TILES - 1:
            kd = 0.5 * (ks[j] + ks[j + 1])
            return kd, kd * (1.0 + hs[j] - hs[j + 1])
        kd = 0.5 * (ks[j] + subs_up(ks[0]))
        flow = kd * (1.0 + hs[j] - subs_up(hs[0]))
        return jnp.where(is_bottom, ks[j], kd), jnp.where(is_bottom, ks[j], flow)

    final = face(TILES - 1)
    above = (
        jnp.where(is_top, ks[0], subs_down(final[0])),
        jnp.where(is_top, top * ks[0], subs_down(final[1])),
    )
    for j in range(TILES):
        below = final if j == TILES - 1 else face(j)
        hj, kj = hs[j], ks[j]
        kf = jnp.where(last, 0.0, 0.5 * (kj + lanes_left(kj)))
        flow = kf * (lanes_left(hj) - hj)
        k_low = 0.5 * low * (k[r - 1, j] + kj)
        k_high = 0.5 * high * (k[r + 1, j] + kj)
        net = flow - lanes_right(flow) + above[1] - below[1]
        net = net + k_low * (h[r - 1, j] - hj) + k_high * (h[r + 1, j] - hj)
        total = kf + lanes_right(kf) + above[0] + below[0] + k_low + k_high
        above = below
        yield j, net, total


def own_kernel(tab_k, tab_a, tab_n, own, zones, k, kl, kn, ic, sl, sn, prm, near):
    base = 8 * lax.axis_index("row") - 4
    sub = iota((SUB, WIDTH), 0)
    rel = (jnp.where(sub < 2, zones[0:1, :], zones[1:2, :]).astype(jnp.int32) - base) & (ZONES - 1)
    sat = jnp.ones((SUB, WIDTH), F32)
    alpha, n = sat, 2.0 * sat
    lane = iota((SUB, 128), 1)
    line = iota((SUB, 128), 0)
    table = jnp.ones((SUB, 128), F32)
    for i in range(NEAR):
        at = (base + i) & (ZONES - 1)
        here = rel == i
        sat = jnp.where(here, tab_k[at], sat)
        alpha = jnp.where(here, tab_a[at], alpha)
        n = jnp.where(here, tab_n[at], n)
        column = jnp.where(line == 0, tab_k[at], jnp.where(line == 1, tab_a[at], tab_n[at]))
        table = jnp.where(lane == i, column, table)
    near[...] = table
    for i, value in enumerate(derived(sat, alpha, n)):
        for r in range(4):
            prm[r, i : i + 1, :] = value[r : r + 1, :]

    def cells(r, carry):
        p = row_params(prm, r)
        for j in range(TILES):
            k[r, j], kl[r, j], kn[r, j], ic[r, j], sl[r, j], sn[r, j] = cell_math(own[r, j], p)
        return carry

    lax.fori_loop(0, 4, cells, 0)


def first_kernel(
    plan, near, own, zones, own_prm, k, kl, kn, ic, sl, sn, got_odd, got_even,
    h0, k1, kl1, kn1, ic1, g1, p1, q1, prm, zrel, spread,
):
    position = lax.axis_index("row")
    has_low, has_high = position > 0, position < lax.axis_size("row") - 1
    odd = position % 2 == 1
    for row in range(2):
        for j in range(TILES):
            at = row * TILES + j
            one, other = got_odd[at], got_even[at]
            h0[row, j] = jnp.where(has_low, jnp.where(odd, other, one), own[0, j])
            h0[6 + row, j] = jnp.where(has_high, jnp.where(odd, one, other), own[3, j])
    h0[2:6] = own[...]
    for here, there in ((k, k1), (kl, kl1), (kn, kn1)):
        there[2:6] = here[...]
    ic1[1:5] = ic[...]
    one, other = got_odd[2 * TILES], got_even[2 * TILES]
    extra_low, extra_high = jnp.where(odd, other, one), jnp.where(odd, one, other)
    z_low = jnp.where(has_low, extra_low[0:1, :], zones[0:1, :])
    z_high = jnp.where(has_high, extra_high[0:1, :], zones[1:2, :])
    sub = iota((SUB, WIDTH), 0)

    def by_row(a, b, c, d):
        return jnp.where(sub < 4, jnp.where(sub < 2, a, b), jnp.where(sub < 6, c, d))

    zone = by_row(z_low, zones[0:1, :], zones[1:2, :], z_high).astype(jnp.int32)
    rel = (zone - (8 * position - 4)) & (ZONES - 1)
    zrel[...] = rel
    ids = iota((32, WIDTH), 0)
    sides = []
    for r in (0, 7):
        pick = (ids == rel[r : r + 1, :]).astype(F32).astype(jnp.bfloat16)
        parts = [jnp.dot(x, pick, preferred_element_type=F32) for x in split3(near[:, :32])]
        sides.append(parts[0] + (parts[1] + parts[2]))
    sat, alpha, n = (
        by_row(sides[0][i : i + 1, :], own_prm[0, i : i + 1, :], own_prm[2, i : i + 1, :], sides[1][i : i + 1, :])
        for i in range(3)
    )
    lev_0 = by_row(extra_low[1:2, :], plan[0, 0].astype(F32), plan[0, 1].astype(F32), extra_high[1:2, :])
    lev_1 = by_row(0.0, plan[1, 0].astype(F32), plan[1, 1].astype(F32), 0.0) + 0.0 * sat
    made = derived(sat, alpha, n) + (IRRIGATION * lev_0, IRRIGATION * lev_1, 1.0 / sat, 1.0 / alpha)
    for i, value in enumerate(made):
        for r in range(ROWS):
            prm[r, i : i + 1, :] = value[r : r + 1, :]

    def outer(i, carry):
        r = 7 * i
        p = row_params(prm, r)
        for j in range(TILES):
            k1[r, j], kl1[r, j], kn1[r, j] = cell_math(h0[r, j], p, False)
        return carry

    def inner(i, carry):
        r = 1 + 5 * i
        p = row_params(prm, r)
        for j in range(TILES):
            values = cell_math(h0[r, j], p)
            k1[r, j], kl1[r, j], kn1[r, j], ic1[r - 1, j], p1[r - 1, j], q1[r - 1, j] = values
        return carry

    lax.fori_loop(0, 2, outer, 0)
    lax.fori_loop(0, 2, inner, 0)
    p1[1:5] = sl[...]
    q1[1:5] = sn[...]

    def flow(r, most):
        low, high = row_open(position, r)
        is_own = jnp.logical_and(r >= 2, r <= 5)
        real = jnp.logical_or(is_own, jnp.logical_or(jnp.logical_and(r < 2, has_low), jnp.logical_and(r > 5, has_high)))
        for j, net, total in net_row(h0, k1, r, prm[r, LEV0 : LEV0 + 1, :], low, high):
            ic = ic1[r - 1, j]
            g = jnp.where(real, net * ic, 0.0)
            g1[r - 1, j] = g
            p1[r - 1, j] = g * p1[r - 1, j]
            q1[r - 1, j] = g * q1[r - 1, j]
            most = jnp.maximum(most, jnp.where(is_own, total * ic, 0.0))
        return most

    most = lax.fori_loop(1, 7, flow, jnp.zeros((SUB, WIDTH), F32))
    most = jnp.maximum(jnp.maximum(most[:, :128], most[:, 128:256]), most[:, 256:])
    most = jnp.max(most, 0, keepdims=True)
    spread[...] = jnp.broadcast_to(most[None], spread.shape)


def second_kernel(
    rates, cells_at, goals, h0, k1, kl1, kn1, ic1, g1, p1, q1, prm, zrel,
    h1_out, g2, spread,
    h1, k2, kl2, kn2, ic2, sl2, sn2, va, vb, wa, wb, w0, w1, w2, maps,
):
    position = lax.axis_index("row")
    size = CFL / jnp.max(rates[...])
    nothing = jnp.zeros((TILES, SUB, WIDTH), F32)
    for r in (0, ROWS - 1):
        for ref in (w0, w1, w2):
            ref[r] = nothing
    for r in (1, 6):
        for ref in (wa, wb):
            ref[r] = nothing

    def cells(r, carry):
        p = row_params(prm, r)
        for j in range(TILES):
            head = h0[r, j] + size * g1[r - 1, j]
            h1[r, j] = head
            h1_out[r - 2, j] = head
            values = cell_math(head, p)
            k2[r, j], kl2[r, j], kn2[r, j], ic2[r - 2, j], sl2[r - 2, j], sn2[r - 2, j] = values
        return carry

    def edge_cells(i, carry):
        r = 1 + 5 * i
        p = row_params(prm, r)
        for j in range(TILES):
            head = h0[r, j] + size * g1[r - 1, j]
            h1[r, j] = head
            k2[r, j], kl2[r, j], kn2[r, j] = cell_math(head, p, False)
        return carry

    lax.fori_loop(0, 2, edge_cells, 0)
    lax.fori_loop(2, 6, cells, 0)

    def flow(r, most):
        low, high = row_open(position, r)
        for j, net, total in net_row(h1, k2, r, prm[r, LEV1 : LEV1 + 1, :], low, high):
            ic = ic2[r - 2, j]
            g2[r - 2, j] = net * ic
            most = jnp.maximum(most, total * ic)
        return most

    most = jnp.max(lax.fori_loop(2, 6, flow, jnp.zeros((SUB, WIDTH), F32)))

    def places(cell):
        line = jnp.floor((cell + 0.5) * (1.0 / WIDTH))
        column = cell - WIDTH * line
        depth = jnp.floor((line + 0.5) * 0.25)
        block = jnp.floor((depth + 0.5) * (1.0 / TILES))
        return (line - 4.0 * depth) * 48.0 + (depth - TILES * block) * 8.0 + block, column

    count = cells_at.shape[1]
    line_of = iota((SUB, count), 0)
    wide = jnp.where(line_of == 0, cells_at[...].astype(F32), goals[...])
    tall = jnp.transpose(wide)
    line_wide = places(wide[0:1, :])[0].astype(jnp.int32)
    line_tall, column_tall = places(tall[:, 0:1])
    goal = tall[:, 1:2]
    pick = (iota((count, 192), 1) == line_tall.astype(jnp.int32)).astype(F32).astype(jnp.bfloat16)
    put = (iota((192, count), 0) == line_wide).astype(F32).astype(jnp.bfloat16)
    column = iota((count, WIDTH), 1) == column_tall.astype(jnp.int32)
    field_g = g2[...].reshape(192, WIDTH)
    field_h = h1_out[...].reshape(192, WIDTH) + size * field_g
    seen_h = jnp.sum(jnp.where(column, exact_dot(pick, field_h), 0.0), 1, keepdims=True)
    seen_g = jnp.sum(jnp.where(column, exact_dot(pick, field_g), 0.0), 1, keepdims=True)
    diff = seen_h - goal
    events = 16.0
    loss = (
        jnp.sum(diff * diff) * (0.5 / events),
        jnp.sum(diff * seen_g) * (1.0 / events),
        jnp.sum(seen_g * seen_g) * (0.5 / events),
    )
    va[...] = exact_dot(put, jnp.where(column, diff * (1.0 / events), 0.0)).reshape(OWN)
    vb[...] = exact_dot(put, jnp.where(column, seen_g * (1.0 / events), 0.0)).reshape(OWN)

    def scaled(r, carry):
        for j in range(TILES):
            ic = ic2[r - 2, j]
            wa[r, j] = va[r - 2, j] * ic
            wb[r, j] = vb[r - 2, j] * ic
        return carry

    lax.fori_loop(2, 6, scaled, 0)
    last, is_top, is_bottom = masks()

    def store_two(r, sums):
        flat = [jnp.sum(x, 0, keepdims=True) for x in sums]
        for q in range(3):
            of_a, of_b = flat[q], flat[3 + q]
            rows = [size * of_a, of_a + size * of_b, of_b]
            for c in range(3):
                if q > 0:
                    rows[c] = rows[c] - size * flat[6 + 2 * c + q - 1]
                maps[r, 4 * q + c : 4 * q + c + 1, :] = rows[c]

    def store_heads(r, j, back, sums):
        (v_a, j_a), (v_b, j_b) = back
        us = (v_a + size * j_a, v_b + j_a + size * j_b, j_b)
        ic, pp, qq = ic1[r - 1, j], p1[r - 1, j], q1[r - 1, j]
        for i, (u, w_ref) in enumerate(zip(us, (w0, w1, w2))):
            w_ref[r, j] = u * ic
            sums[6 + 2 * i] += u * pp
            sums[7 + 2 * i] += u * qq

    def edge_two(i, carry):
        r = 1 + 5 * i
        near = 2 + 3 * i
        low, high = row_open(position, r)
        is_open = jnp.where(i == 0, high, low)
        sums = [jnp.zeros((SUB, WIDTH), F32) for _ in range(12)]
        for j in range(TILES):
            hj = h1[r, j]
            half = (0.5 * is_open) * (h1[near, j] - hj)
            kd = (0.5 * is_open) * (k2[near, j] + k2[r, j])
            kj, kl, kn = k2[r, j], kl2[r, j], kn2[r, j]
            inv_h = 1.0 / hj
            back = []
            for part, w_ref in enumerate((wa, wb)):
                w = w_ref[near, j]
                gk, gh = -half * w, kd * w
                to_l = gk * kl
                sums[3 * part] += gk * kj
                sums[3 * part + 1] += to_l
                sums[3 * part + 2] += gk * kn
                back.append((0.0, gh + to_l * inv_h))
            store_heads(r, j, back, sums)
        store_two(r, sums)
        return carry

    def back_two(r, carry):
        low, high = row_open(position, r)
        top = prm[r, LEV1 : LEV1 + 1, :]
        hs = [h1[r, j] for j in range(TILES)]
        ks = [k2[r, j] for j in range(TILES)]
        sums = [jnp.zeros((SUB, WIDTH), F32) for _ in range(12)]
        ws = [[w[r, j] for j in range(TILES)] for w in (wa, wb)]

        def face(j):
            if j < TILES - 1:
                half = 0.5 * (1.0 + hs[j] - hs[j + 1])
                kd = 0.5 * (ks[j] + ks[j + 1])
                out = []
                for w in ws:
                    dw = w[j + 1] - w[j]
                    out.append((half * dw, kd * dw))
                return out
            half = 0.5 * (1.0 + hs[j] - subs_up(hs[0]))
            kd = 0.5 * (ks[j] + subs_up(ks[0]))
            out = []
            for w in ws:
                dw = subs_up(w[0]) - w[j]
                out.append((jnp.where(is_bottom, -w[j], half * dw), jnp.where(is_bottom, 0.0, kd * dw)))
            return out

        final = face(TILES - 1)
        above = [
            (jnp.where(is_top, top * w[0], subs_down(f[0])), subs_down(f[1]))
            for w, f in zip(ws, final)
        ]
        for j in range(TILES):
            below = final if j == TILES - 1 else face(j)
            hj, kj = hs[j], ks[j]
            half_c = jnp.where(last, 0.0, 0.5 * (lanes_left(hj) - hj))
            kf = jnp.where(last, 0.0, 0.5 * (lanes_left(kj) + kj))
            half_l, half_h = (0.5 * low) * (h1[r - 1, j] - hj), (0.5 * high) * (h1[r + 1, j] - hj)
            k_low, k_high = (0.5 * low) * (k2[r - 1, j] + kj), (0.5 * high) * (k2[r + 1, j] + kj)
            kl, kn = kl2[r, j], kn2[r, j]
            inv_h = 1.0 / hj
            g = g2[r - 2, j]
            gl, gn = g * sl2[r - 2, j], g * sn2[r - 2, j]
            back = []
            for part, (w_ref, v_ref) in enumerate(((wa, va), (wb, vb))):
                w = ws[part][j]
                dw = w - lanes_left(w)
                e, f = half_c * dw, kf * dw
                d_low, d_high = w - w_ref[r - 1, j], w - w_ref[r + 1, j]
                gk = e + lanes_right(e) + below[part][0] + above[part][0]
                gk = gk + half_l * d_low + half_h * d_high
                gh = lanes_right(f) - f + below[part][1] - above[part][1]
                gh = gh - k_low * d_low - k_high * d_high
                v = v_ref[r - 2, j]
                to_l = gk * kl - v * gl
                sums[3 * part] += gk * kj
                sums[3 * part + 1] += to_l
                sums[3 * part + 2] += gk * kn - v * gn
                back.append((v, gh + (to_l + v * g) * inv_h))
            store_heads(r, j, back, sums)
            above = below
        store_two(r, sums)
        return carry

    lax.fori_loop(0, 2, edge_two, 0)
    lax.fori_loop(2, 6, back_two, 0)

    refs = (w0, w1, w2)

    def store_one(r, sums, first):
        inv_k, inv_a = prm[r, IKS : IKS + 1, :], prm[r, IAL : IAL + 1, :]
        for q in range(3):
            for c in range(3):
                at = 4 * q + c
                row = size * jnp.sum(sums[3 * c + q], 0, keepdims=True)
                if not first:
                    row = row + maps[r, at : at + 1, :]
                maps[r, at : at + 1, :] = row if q == 2 else row * (inv_k if q == 0 else inv_a)

    def edge_one(i, carry):
        r = 7 * i
        near = 1 + 5 * i
        sums = [jnp.zeros((SUB, WIDTH), F32) for _ in range(9)]
        for j in range(TILES):
            half = 0.5 * (h0[r, j] - h0[near, j])
            kj, kl, kn = k1[r, j], kl1[r, j], kn1[r, j]
            for part, w_ref in enumerate(refs):
                gk = half * w_ref[near, j]
                sums[3 * part] += gk * kj
                sums[3 * part + 1] += gk * kl
                sums[3 * part + 2] += gk * kn
        store_one(r, sums, True)
        return carry

    def back_one(r, carry):
        low, high = row_open(position, r)
        top = prm[r, LEV0 : LEV0 + 1, :]
        hs = [h0[r, j] for j in range(TILES)]
        ws = [[w[r, j] for j in range(TILES)] for w in refs]
        sums = [jnp.zeros((SUB, WIDTH), F32) for _ in range(9)]

        def face(j):
            if j < TILES - 1:
                half = 0.5 * (1.0 + hs[j] - hs[j + 1])
                return [half * (w[j + 1] - w[j]) for w in ws]
            half = 0.5 * (1.0 + hs[j] - subs_up(hs[0]))
            return [jnp.where(is_bottom, -w[j], half * (subs_up(w[0]) - w[j])) for w in ws]

        final = face(TILES - 1)
        above = [jnp.where(is_top, top * w[0], subs_down(f)) for w, f in zip(ws, final)]
        for j in range(TILES):
            below = final if j == TILES - 1 else face(j)
            hj = hs[j]
            half_c = jnp.where(last, 0.0, 0.5 * (lanes_left(hj) - hj))
            half_l = (0.5 * low) * (h0[r - 1, j] - hj)
            half_h = (0.5 * high) * (h0[r + 1, j] - hj)
            kj, kl, kn = k1[r, j], kl1[r, j], kn1[r, j]
            for part, w_ref in enumerate(refs):
                w = ws[part][j]
                e = half_c * (w - lanes_left(w))
                gk = e + lanes_right(e) + below[part] + above[part]
                gk = gk + half_l * (w - w_ref[r - 1, j]) + half_h * (w - w_ref[r + 1, j])
                sums[3 * part] += gk * kj
                sums[3 * part + 1] += gk * kl
                sums[3 * part + 2] += gk * kn
            above = below
        store_one(r, sums, False)
        return carry

    for r in range(ROWS):
        for at in (3, 7, 11):
            maps[r, at : at + 1, :] = jnp.zeros((1, WIDTH), F32)
        maps[r, 12:16, :] = jnp.zeros((4, WIDTH), F32)
    lax.fori_loop(0, 2, edge_one, 0)
    lax.fori_loop(1, 7, back_one, 0)

    left = jnp.concatenate([maps[r] for r in range(ROWS)], 1)
    near = zrel[...]
    zone_id = iota((32, WIDTH), 0)
    onehot = jnp.concatenate([(zone_id == near[r : r + 1, :]).astype(F32) for r in range(ROWS)], 1)
    onehot = onehot.astype(jnp.bfloat16)
    nt = (((1,), (1,)), ((), ()))
    parts = [lax.dot_general(part, onehot, nt, preferred_element_type=F32) for part in split3(left)]
    by_zone = parts[0] + (parts[1] + parts[2])
    fields = [by_zone[4 * q : 4 * q + 4, :] for q in range(3)]
    sub4 = iota((4, 32), 0)
    fields.append(jnp.where(sub4 == 0, loss[0], jnp.where(sub4 == 1, loss[1], loss[2])))
    sums = jnp.concatenate(fields, 1)
    state = jnp.where(iota((4, 128), 1) < 64, most, size)
    payload = jnp.where(iota((4, 128), 0) == 3, state, sums)
    spread[...] = jnp.broadcast_to(payload[None], spread.shape)


def ring_kernel(parts, spread):
    lane = iota((SUB, 256), 1)
    total = jnp.zeros((SUB, 256), F32)
    blank = jnp.zeros((SUB, 128), F32)
    most = None
    loss = jnp.zeros((SUB, 256), F32)
    for z in range(8):
        tile = jnp.concatenate([parts[z], parts[8 + z]], 0)
        most = tile if most is None else jnp.maximum(most, tile)
        tile = jnp.concatenate([tile, blank], 1)
        for q in range(3):
            start = 84 * q + 8 * z
            moved = pltpu.roll(tile, (start - 32 * q) % 256, 1)
            total = total + jnp.where(jnp.logical_and(lane >= start, lane < start + NEAR), moved, 0.0)
        loss = loss + tile
    total = jnp.where(lane == 252, pltpu.roll(loss, 252 - 96, 1), total)
    state = jnp.concatenate(
        [jnp.broadcast_to(most[:, 0:1], (SUB, 128)), jnp.broadcast_to(most[:, 64:65], (SUB, 128))], 1
    )
    total = jnp.where(iota((SUB, 256), 0) % 4 == 3, state, total)
    spread[...] = jnp.broadcast_to(total[None], spread.shape)


def last_kernel(parts, h1, g2, final, grad_k, grad_a, grad_n, misfit, rates):
    sub = iota((SUB, 256), 0)
    power = sub % 4
    sums = [jnp.zeros((SUB, 256), F32) for _ in range(4)]
    for pair in range(8):
        tiles = [parts[8 * y + pair] for y in range(4)]
        most = jnp.maximum(jnp.maximum(tiles[0], tiles[1]), jnp.maximum(tiles[2], tiles[3]))
        step = CFL / most
        rates[pair] = step
        moves = []
        for row in (3, 7):
            move = step[row : row + 1, :128] - most[row : row + 1, 128:]
            moves.append(jnp.concatenate([move, move], 1))
        move = jnp.where(sub < 4, moves[0], moves[1])
        weight = jnp.where(power == 0, 1.0, jnp.where(power == 1, move, move * move))
        for y in range(4):
            sums[y] = sums[y] + jnp.where(power == 3, 0.0, tiles[y] * weight)
    lane = iota((1, 256), 1)
    rows = [jnp.sum(x, 0, keepdims=True) for x in sums]
    for q, out in enumerate((grad_k, grad_a, grad_n)):
        total = jnp.zeros((1, 256), F32)
        for y in range(4):
            field = rows[y] if q == 0 else pltpu.roll(rows[y], 256 - 84 * q, 1)
            total = total + pltpu.roll(jnp.where(lane < 84, field, 0.0), (64 * y - 4) % 256, 1)
        out[...] = total
    misfit[0, 0] = jnp.sum(jnp.where(lane == 252, rows[0] + rows[1] + rows[2] + rows[3], 0.0))
    _, pair, z_hi = axes()
    mine = rates[pair]
    size = jnp.where(z_hi == 0, mine[3:4, :128], mine[7:8, :128])
    size = jnp.concatenate([size, size, size], 1)
    for j in range(TILES):
        for row in range(4):
            tile = h1[row, j] + size * g2[row, j]
            for s in range(SUB):
                final[TILES * s + j, row : row + 1, :] = tile[s : s + 1, :]


VMEM = pl.BlockSpec(memory_space=pltpu.VMEM)
SMEM = pl.BlockSpec(memory_space=pltpu.SMEM)


def call(kernel, name, ins, outs, out_specs=None, scratch=(), cost=None):
    return pl.pallas_call(
        kernel,
        name=name,
        in_specs=ins,
        out_specs=out_specs or [VMEM] * len(outs),
        out_shape=[jax.ShapeDtypeStruct(shape, dtype) for shape, dtype in outs],
        scratch_shapes=scratch,
        cost_estimate=cost,
        compiler_params=pltpu.CompilerParams(vmem_limit_bytes=32 * 1024 * 1024),
    )


def local(
    initial_head,
    sat_conductivity,
    vg_alpha,
    vg_n,
    zone_map,
    forcing_plan,
    tensiometer_cells,
    tensiometer_heads,
):
    count = lax.axis_size("row")
    plan = forcing_plan[0]
    edge = (2 * TILES + 1, SUB, WIDTH)
    own, send_odd, send_even, zones = call(
        pack_kernel,
        "pack_edges",
        [pl.BlockSpec(memory_space=pl.ANY)] * 3,
        [(OWN, F32), (edge, F32), (edge, F32), ((2, WIDTH), F32)],
        scratch=[
            pltpu.VMEM((48, 4, WIDTH), F32),
            pltpu.VMEM((2, 192), jnp.int32),
            pltpu.VMEM((2, 2), jnp.int32),
            pltpu.SemaphoreType.DMA((3,)),
        ],
    )(initial_head[0], zone_map, plan)
    odd = [(i, i + 1) for i in range(1, count - 1, 2)]
    even = [(i, i + 1) for i in range(0, count, 2)]
    got_odd = lax.ppermute(send_odd, "row", odd + [(j, i) for i, j in odd])
    got_even = lax.ppermute(send_even, "row", even + [(j, i) for i, j in even])
    own_fields = call(
        own_kernel,
        "own_cells",
        [SMEM] * 3 + [VMEM] * 2,
        [(OWN, F32)] * 6 + [((4, 16, WIDTH), F32), ((SUB, 128), F32)],
        cost=pl.CostEstimate(flops=100_000_000, bytes_accessed=8_000_000, transcendentals=600_000),
    )(sat_conductivity, vg_alpha, vg_n, own, zones)
    own_prm, near = own_fields[6:]
    wide = (6, TILES, SUB, WIDTH)
    first = call(
        first_kernel,
        "first_step",
        [SMEM] + [VMEM] * 12,
        [(FIELD, F32)] * 4
        + [(wide, F32)] * 4
        + [((ROWS, 16, WIDTH), F32), ((ROWS, WIDTH), jnp.int32), ((32, 1, 128), F32)],
    )(plan, near, own, zones, own_prm, *own_fields[:6], got_odd, got_even)
    fields, rates = first[:-1], first[-1]
    rates = lax.all_to_all(rates, "row", 0, 0, tiled=True)
    h1, g2, sums = call(
        second_kernel,
        "second_step_and_adjoint",
        [VMEM] * 13,
        [(OWN, F32), (OWN, F32), ((16, 4, 128), F32)],
        scratch=[pltpu.VMEM(FIELD, F32)] * 4
        + [pltpu.VMEM(OWN, F32)] * 5
        + [pltpu.VMEM(FIELD, F32)] * 5
        + [pltpu.VMEM((ROWS, 16, WIDTH), F32)],
    )(rates, tensiometer_cells, tensiometer_heads, *fields)
    sums = lax.all_to_all(sums, ("event", "row"), 0, 0, tiled=True, axis_index_groups=RINGS)
    (sums,) = call(ring_kernel, "ring_sums", [VMEM], [((32, SUB, 256), F32)])(sums)
    sums = lax.all_to_all(sums, ("event", "row"), 0, 0, tiled=True, axis_index_groups=PLANES)
    row = ((1, ZONES), F32)
    final, grad_k, grad_a, grad_n, misfit = call(
        last_kernel,
        "final_head_and_sums",
        [VMEM, VMEM, VMEM],
        [((48, 4, WIDTH), F32), row, row, row, ((1, 1), F32)],
        [VMEM] * 4 + [SMEM],
        scratch=[pltpu.VMEM((8, SUB, 256), F32)],
    )(sums, h1, g2)
    return (final[None], misfit[0, 0], grad_k[0], grad_a[0], grad_n[0])


def solution(mesh):
    return jax.shard_map(
        local,
        mesh=mesh,
        in_specs=(
            P("event", None, "row", None),
            P(),
            P(),
            P(),
            P("row", None),
            P("event", None, "row"),
            P("event", "row"),
            P("event", "row"),
        ),
        out_specs=(P("event", None, "row", None), P(), P(), P(), P()),
        check_vma=False,
    )
```

```python
import jax
import jax.numpy as jnp
from jax import lax
from jax.experimental import pallas as pl
from jax.experimental.pallas import tpu as pltpu
from jax.sharding import PartitionSpec as P

CFL = 0.4
IRRIGATION = 0.2
WATER_RANGE = 0.35

TILES = 6
SUB = 8
WIDTH = 384
ROWS = 8
FIELD = (ROWS, TILES, SUB, WIDTH)
OWN = (4, TILES, SUB, WIDTH)
NEAR = 28
ZONES = 256
KS, AL, N, N1, M, MP, IC0, IN1, LEV0, LEV1, IKS, IAL = range(12)
F32 = jnp.float32


def device(x, z_hi, core, y, z_lo):
    return ((x * 2 + z_hi) * 2 + core) * 32 + y * 8 + z_lo


PLANES = [
    [device(x, z_hi, core, y, z_lo) for y in range(4) for x in range(4) for core in range(2)]
    for z_hi in range(2)
    for z_lo in range(8)
]
RINGS = [
    [device(x, z_hi, core, y, z_lo) for z_hi in range(2) for z_lo in range(8)]
    for x in range(4)
    for core in range(2)
    for y in range(4)
]


def lanes_left(x):
    return pltpu.roll(x, WIDTH - 1, 1)


def lanes_right(x):
    return pltpu.roll(x, 1, 1)


def subs_up(x):
    return pltpu.roll(x, SUB - 1, 0)


def subs_down(x):
    return pltpu.roll(x, 1, 0)


def iota(shape, dim):
    return lax.broadcasted_iota(jnp.int32, shape, dim)


def split3(x):
    hi = x.astype(jnp.bfloat16)
    rest = x - hi.astype(F32)
    mid = rest.astype(jnp.bfloat16)
    return hi, mid, (rest - mid.astype(F32)).astype(jnp.bfloat16)


def exact_dot(pick, x, dims=(((1,), (0,)), ((), ()))):
    parts = [lax.dot_general(pick, part, dims, preferred_element_type=F32) for part in split3(x)]
    return parts[0] + (parts[1] + parts[2])


def axes():
    event = lax.axis_index("event")
    return lax.axis_index("row"), event // 4 * 2 + event % 2, event // 2 % 2


def pack_kernel(head_in, zone_in, plan_in, h0, send_odd, send_even, zones, head, zone, plan, sems):
    copies = [
        pltpu.make_async_copy(src, dst, sems.at[i])
        for i, (src, dst) in enumerate(((head_in, head), (zone_in, zone), (plan_in, plan)))
    ]
    for copy in copies:
        copy.start()
    wide = (iota((192, WIDTH), 1) // 2 == iota((192, WIDTH), 0)).astype(F32)
    copies[1].wait()
    copies[2].wait()
    blocks = jnp.dot(zone[...].astype(F32), wide, preferred_element_type=F32)
    zones[...] = blocks
    level = plan[...].astype(F32)
    copies[0].wait()
    for depth in range(TILES * SUB):
        block = head[depth]
        j, s = depth % TILES, depth // TILES
        for row in range(4):
            h0[2 + row, j, s : s + 1, :] = block[row : row + 1, :]
    sub = iota((SUB, WIDTH), 0)
    odd = lax.axis_index("row") % 2 == 1

    def fill(out, pair):
        out[0:TILES] = h0[2 + 2 * pair]
        out[TILES : 2 * TILES] = h0[3 + 2 * pair]
        out[2 * TILES] = jnp.where(sub == 0, blocks[pair : pair + 1, :], level[0:1, pair : pair + 1])

    @pl.when(odd)
    def _():
        fill(send_odd, 1)
        fill(send_even, 0)

    @pl.when(jnp.logical_not(odd))
    def _():
        fill(send_odd, 0)
        fill(send_even, 1)


def cell_math(head, p, with_store=True):
    wet = jnp.log(-p[AL] * head)
    u = jnp.exp(p[N] * wet)
    d = 1.0 + u
    w = jnp.log(d)
    inv = 1.0 / d
    r = u * inv
    mw = p[M] * w
    q = jnp.exp(-0.5 * mw)
    f = jnp.exp(p[N1] * wet - mw)
    t = 1.0 - f
    kq = p[KS] * q * t
    half, twice = -0.5 * t, 2.0 * f
    e1 = p[MP] * w + p[M] * wet * r
    cond = kq * t
    cond_l = kq * p[N1] * (half * r - twice * inv)
    cond_n = kq * (half * e1 - twice * (wet - e1))
    if not with_store:
        return cond, cond_l, cond_n
    inv_store = d * p[IC0] / f
    store_l = p[N] - r * (2.0 * p[N] - 1.0)
    store_n = p[IN1] + wet - e1 - r * wet
    return cond, cond_l, cond_n, inv_store, store_l, store_n


def derived(sat, alpha, n):
    n1 = n - 1.0
    return (
        sat, alpha, n, n1, 1.0 - 1.0 / n, 1.0 / (n * n), 0.5 / (WATER_RANGE * n1 * alpha), 1.0 / n1,
    )


def row_params(prm, r):
    return [prm[r, i : i + 1, :] for i in range(8)]


def masks():
    last = iota((SUB, WIDTH), 1) == WIDTH - 1
    sub = iota((SUB, WIDTH), 0)
    return last, sub == 0, sub == SUB - 1


def net_row(h, k, r, top, beside):
    last, is_top, is_bottom = masks()
    hs = [h[r, j] for j in range(TILES)]
    ks = [k[r, j] for j in range(TILES)]

    def face(j):
        if j < TILES - 1:
            kd = ks[j] + ks[j + 1]
            return kd, kd * (1.0 + hs[j] - hs[j + 1])
        kd = ks[j] + subs_up(ks[0])
        flow = kd * (1.0 + hs[j] - subs_up(hs[0]))
        return jnp.where(is_bottom, 2.0 * ks[j], kd), jnp.where(is_bottom, 2.0 * ks[j], flow)

    final = face(TILES - 1)
    above = (
        jnp.where(is_top, 2.0 * ks[0], subs_down(final[0])),
        jnp.where(is_top, top * ks[0], subs_down(final[1])),
    )
    for j in range(TILES):
        below = final if j == TILES - 1 else face(j)
        hj, kj = hs[j], ks[j]
        kf = jnp.where(last, 0.0, kj + lanes_left(kj))
        flow = kf * (lanes_left(hj) - hj)
        net = flow - lanes_right(flow) + above[1] - below[1]
        total = kf + lanes_right(kf) + above[0] + below[0]
        for other in beside:
            kx = k[other, j] + kj
            net = net + kx * (h[other, j] - hj)
            total = total + kx
        above = below
        yield j, net, total


def places(cell):
    line = jnp.floor((cell + 0.5) * (1.0 / WIDTH))
    column = cell - WIDTH * line
    depth = jnp.floor((line + 0.5) * 0.25)
    block = jnp.floor((depth + 0.5) * (1.0 / TILES))
    return (line - 4.0 * depth) * 48.0 + (depth - TILES * block) * 8.0 + block, column


def own_kernel(
    tab_k, tab_a, tab_n, plan, h0, zones, cells_at, goals,
    k1, kl1, kn1, ic1, g1, p1, q1, prm, part, most_out, near, pick, put, column, goal,
):
    base = 8 * lax.axis_index("row") - 4
    sub = iota((SUB, WIDTH), 0)
    rel = (jnp.where(sub < 2, zones[0:1, :], zones[1:2, :]).astype(jnp.int32) - base) & (ZONES - 1)
    sat = jnp.ones((SUB, WIDTH), F32)
    alpha, n = sat, 2.0 * sat
    lane = iota((SUB, 128), 1)
    line = iota((SUB, 128), 0)
    table = jnp.ones((SUB, 128), F32)
    for i in range(NEAR):
        at = (base + i) & (ZONES - 1)
        here = rel == i
        sat = jnp.where(here, tab_k[at], sat)
        alpha = jnp.where(here, tab_a[at], alpha)
        n = jnp.where(here, tab_n[at], n)
        entry = jnp.where(line == 0, tab_k[at], jnp.where(line == 1, tab_a[at], tab_n[at]))
        table = jnp.where(lane == i, entry, table)
    near[...] = table
    levels = [
        2.0 * IRRIGATION * jnp.where(sub < 2, plan[step, 0].astype(F32), plan[step, 1].astype(F32))
        for step in range(2)
    ]
    for i, value in enumerate(derived(sat, alpha, n) + (*levels, 1.0 / sat, 1.0 / alpha)):
        for r in range(4):
            prm[2 + r, i : i + 1, :] = value[r : r + 1, :]

    def cells(r, carry):
        p = row_params(prm, r)
        for j in range(TILES):
            values = cell_math(h0[r, j], p)
            k1[r, j], kl1[r, j], kn1[r, j], ic1[r - 1, j], p1[r - 1, j], q1[r - 1, j] = values
        return carry

    lax.fori_loop(2, 6, cells, 0)

    def flow(r, most):
        for j, net, total in net_row(h0, k1, r, prm[r, LEV0 : LEV0 + 1, :], (r - 1, r + 1)):
            ic = ic1[r - 1, j]
            g = net * ic
            g1[r - 1, j] = g
            p1[r - 1, j] = g * p1[r - 1, j]
            q1[r - 1, j] = g * q1[r - 1, j]
            most = jnp.maximum(most, total * ic)
        return most

    def edge_flow(i, carry):
        r = 2 + 3 * i
        for j, net, total in net_row(h0, k1, r, prm[r, LEV0 : LEV0 + 1, :], (3 + i,)):
            g1[r - 1, j] = net
            part[i, j] = total
        return carry

    most_out[...] = lax.fori_loop(3, 5, flow, jnp.zeros((SUB, WIDTH), F32))
    lax.fori_loop(0, 2, edge_flow, 0)

    count = cells_at.shape[1]
    wide = jnp.where(iota((SUB, count), 0) == 0, cells_at[...].astype(F32), goals[...])
    tall = jnp.transpose(wide)
    line_wide = places(wide[0:1, :])[0].astype(jnp.int32)
    line_tall, column_tall = places(tall[:, 0:1])
    pick[...] = (iota((count, 192), 1) == line_tall.astype(jnp.int32)).astype(F32).astype(jnp.bfloat16)
    put[...] = (iota((192, count), 0) == line_wide).astype(F32).astype(jnp.bfloat16)
    column[...] = (iota((count, WIDTH), 1) == column_tall.astype(jnp.int32)).astype(F32)
    goal[...] = jnp.broadcast_to(tall[:, 1:2], goal.shape)


def first_kernel(
    near, zones, part, most_in, got_odd, got_even, _h0, _k1, _kl1, _kn1, _ic1, _g1, _p1, _q1, _prm,
    h0, k1, kl1, kn1, ic1, g1, p1, q1, prm, zrel, spread,
):
    position = lax.axis_index("row")
    has_low, has_high = position > 0, position < lax.axis_size("row") - 1
    odd = position % 2 == 1
    for row in range(2):
        for j in range(TILES):
            at = row * TILES + j
            one, other = got_odd[at], got_even[at]
            h0[row, j] = jnp.where(has_low, jnp.where(odd, other, one), h0[2, j])
            h0[6 + row, j] = jnp.where(has_high, jnp.where(odd, one, other), h0[5, j])
    one, other = got_odd[2 * TILES], got_even[2 * TILES]
    extra_low, extra_high = jnp.where(odd, other, one), jnp.where(odd, one, other)
    z_low = jnp.where(has_low, extra_low[0:1, :], zones[0:1, :])
    z_high = jnp.where(has_high, extra_high[0:1, :], zones[1:2, :])
    sub = iota((SUB, WIDTH), 0)
    zone = jnp.where(
        sub < 4,
        jnp.where(sub < 2, z_low, zones[0:1, :]),
        jnp.where(sub < 6, zones[1:2, :], z_high),
    ).astype(jnp.int32)
    rel = (zone - (8 * position - 4)) & (ZONES - 1)
    zrel[...] = rel
    ids = iota((32, WIDTH), 0)
    sides = []
    for r in (0, 7):
        here = (ids == rel[r : r + 1, :]).astype(F32).astype(jnp.bfloat16)
        parts = [jnp.dot(x, here, preferred_element_type=F32) for x in split3(near[:, :32])]
        sides.append(parts[0] + (parts[1] + parts[2]))
    sat, alpha, n = (
        jnp.where(sub < 4, sides[0][i : i + 1, :], sides[1][i : i + 1, :]) for i in range(3)
    )
    level = 2.0 * IRRIGATION * jnp.where(sub < 4, extra_low[1:2, :], extra_high[1:2, :])
    for i, value in enumerate(derived(sat, alpha, n) + (level, level, 1.0 / sat, 1.0 / alpha)):
        for r in (0, 1, 6, 7):
            prm[r, i : i + 1, :] = value[r : r + 1, :]

    def outer(i, carry):
        r = 7 * i
        p = row_params(prm, r)
        for j in range(TILES):
            k1[r, j], kl1[r, j], kn1[r, j] = cell_math(h0[r, j], p, False)
        return carry

    def inner(i, carry):
        r, own = 1 + 5 * i, 2 + 3 * i
        real = jnp.where(i == 0, has_low, has_high)
        p = row_params(prm, r)
        for j in range(TILES):
            cond, kl1[r, j], kn1[r, j], ic1[r - 1, j], p1[r - 1, j], q1[r - 1, j] = cell_math(h0[r, j], p)
            k1[r, j] = jnp.where(real, cond, -k1[own, j])
        return carry

    lax.fori_loop(0, 2, outer, 0)
    lax.fori_loop(0, 2, inner, 0)

    def flow(i, most):
        r, own = 1 + 5 * i, 2 + 3 * i
        real = jnp.where(i == 0, has_low, has_high)
        for j, net, _ in net_row(h0, k1, r, prm[r, LEV0 : LEV0 + 1, :], (r - 1, r + 1)):
            g = jnp.where(real, net * ic1[r - 1, j], 0.0)
            g1[r - 1, j] = g
            p1[r - 1, j] = g * p1[r - 1, j]
            q1[r - 1, j] = g * q1[r - 1, j]
            kx = k1[r, j] + k1[own, j]
            ic = ic1[own - 1, j]
            g = (g1[own - 1, j] + kx * (h0[r, j] - h0[own, j])) * ic
            g1[own - 1, j] = g
            p1[own - 1, j] = g * p1[own - 1, j]
            q1[own - 1, j] = g * q1[own - 1, j]
            most = jnp.maximum(most, (part[i, j] + kx) * ic)
        return most

    most = lax.fori_loop(0, 2, flow, most_in[...])
    most = jnp.maximum(jnp.maximum(most[:, :128], most[:, 128:256]), most[:, 256:])
    most = jnp.max(most, 0, keepdims=True)
    spread[...] = jnp.broadcast_to(most[None], spread.shape)


def second_kernel(
    rates, pick, put, column, goal, h0, k1, kl1, kn1, ic1, g1, p1, q1, prm, zrel,
    h1_out, g2, spread,
    h1, k2, kl2, kn2, ic2, sl2, sn2, va, vb, wa, wb, w0, w1, w2, maps,
):
    position = lax.axis_index("row")
    size = CFL / jnp.max(rates[...])
    nothing = jnp.zeros((TILES, SUB, WIDTH), F32)
    for r in (0, ROWS - 1):
        for ref in (w0, w1, w2):
            ref[r] = nothing
    for r in (1, 6):
        for ref in (wa, wb):
            ref[r] = nothing

    def cells(r, carry):
        p = row_params(prm, r)
        for j in range(TILES):
            head = h0[r, j] + size * g1[r - 1, j]
            h1[r, j] = head
            h1_out[r - 2, j] = head
            values = cell_math(head, p)
            k2[r, j], kl2[r, j], kn2[r, j], ic2[r - 2, j], sl2[r - 2, j], sn2[r - 2, j] = values
        return carry

    def edge_cells(i, carry):
        r = 1 + 5 * i
        p = row_params(prm, r)
        own = 2 + 3 * i
        real = jnp.where(i == 0, position > 0, position < lax.axis_size("row") - 1)
        for j in range(TILES):
            head = jnp.where(real, h0[r, j] + size * g1[r - 1, j], h1[own, j])
            h1[r, j] = head
            cond, kl2[r, j], kn2[r, j] = cell_math(head, p, False)
            k2[r, j] = jnp.where(real, cond, -k2[own, j])
        return carry

    lax.fori_loop(2, 6, cells, 0)
    lax.fori_loop(0, 2, edge_cells, 0)

    def flow(r, most):
        for j, net, total in net_row(h1, k2, r, prm[r, LEV1 : LEV1 + 1, :], (r - 1, r + 1)):
            ic = ic2[r - 2, j]
            g2[r - 2, j] = net * ic
            most = jnp.maximum(most, total * ic)
        return most

    most = jnp.max(lax.fori_loop(2, 6, flow, jnp.zeros((SUB, WIDTH), F32)))

    field_g = g2[...].reshape(192, WIDTH)
    field_h = h1_out[...].reshape(192, WIDTH) + size * field_g
    seen_h = jnp.sum(column[...] * exact_dot(pick[...], field_h), 1, keepdims=True)
    seen_g = jnp.sum(column[...] * exact_dot(pick[...], field_g), 1, keepdims=True)
    diff = seen_h - goal[:, 0:1]
    events = 16.0
    loss = (
        jnp.sum(diff * diff) * (0.5 / events),
        jnp.sum(diff * seen_g) * (1.0 / events),
        jnp.sum(seen_g * seen_g) * (0.5 / events),
    )
    va[...] = exact_dot(put[...], column[...] * (diff * (1.0 / events))).reshape(OWN)
    vb[...] = exact_dot(put[...], column[...] * (seen_g * (1.0 / events))).reshape(OWN)

    def scaled(r, carry):
        for j in range(TILES):
            ic = ic2[r - 2, j]
            wa[r, j] = va[r - 2, j] * ic
            wb[r, j] = vb[r - 2, j] * ic
        return carry

    lax.fori_loop(2, 6, scaled, 0)
    last, is_top, is_bottom = masks()

    def store_two(r, sums):
        flat = [jnp.sum(x, 0, keepdims=True) for x in sums]
        for q in range(3):
            of_a, of_b = flat[q], flat[3 + q]
            rows = [size * of_a, of_a + size * of_b, of_b]
            for c in range(3):
                if q > 0:
                    rows[c] = rows[c] - size * flat[6 + 2 * c + q - 1]
                maps[r, 4 * q + c : 4 * q + c + 1, :] = rows[c]

    def store_heads(r, j, back, sums):
        (v_a, j_a), (v_b, j_b) = back
        us = (v_a + size * j_a, v_b + j_a + size * j_b, j_b)
        ic, pp, qq = ic1[r - 1, j], p1[r - 1, j], q1[r - 1, j]
        for i, (u, w_ref) in enumerate(zip(us, (w0, w1, w2))):
            w_ref[r, j] = u * ic
            sums[6 + 2 * i] += u * pp
            sums[7 + 2 * i] += u * qq

    def edge_two(i, carry):
        r = 1 + 5 * i
        near = 2 + 3 * i
        sums = [jnp.zeros((SUB, WIDTH), F32) for _ in range(12)]
        for j in range(TILES):
            hj = h1[r, j]
            half = h1[near, j] - hj
            kd = k2[near, j] + k2[r, j]
            kj, kl, kn = k2[r, j], kl2[r, j], kn2[r, j]
            inv_h = 1.0 / hj
            back = []
            for part, w_ref in enumerate((wa, wb)):
                w = w_ref[near, j]
                gk, gh = -half * w, kd * w
                to_l = gk * kl
                sums[3 * part] += gk * kj
                sums[3 * part + 1] += to_l
                sums[3 * part + 2] += gk * kn
                back.append((0.0, gh + to_l * inv_h))
            store_heads(r, j, back, sums)
        store_two(r, sums)
        return carry

    def back_two(r, carry):
        top = prm[r, LEV1 : LEV1 + 1, :]
        hs = [h1[r, j] for j in range(TILES)]
        ks = [k2[r, j] for j in range(TILES)]
        sums = [jnp.zeros((SUB, WIDTH), F32) for _ in range(12)]
        ws = [[w[r, j] for j in range(TILES)] for w in (wa, wb)]

        def face(j):
            if j < TILES - 1:
                half = 1.0 + hs[j] - hs[j + 1]
                kd = ks[j] + ks[j + 1]
                out = []
                for w in ws:
                    dw = w[j + 1] - w[j]
                    out.append((half * dw, kd * dw))
                return out
            half = 1.0 + hs[j] - subs_up(hs[0])
            kd = ks[j] + subs_up(ks[0])
            out = []
            for w in ws:
                dw = subs_up(w[0]) - w[j]
                out.append((jnp.where(is_bottom, -2.0 * w[j], half * dw), jnp.where(is_bottom, 0.0, kd * dw)))
            return out

        final = face(TILES - 1)
        above = [
            (jnp.where(is_top, top * w[0], subs_down(f[0])), subs_down(f[1]))
            for w, f in zip(ws, final)
        ]
        for j in range(TILES):
            below = final if j == TILES - 1 else face(j)
            hj, kj = hs[j], ks[j]
            half_c = jnp.where(last, 0.0, lanes_left(hj) - hj)
            kf = jnp.where(last, 0.0, lanes_left(kj) + kj)
            half_l, half_h = h1[r - 1, j] - hj, h1[r + 1, j] - hj
            k_low, k_high = k2[r - 1, j] + kj, k2[r + 1, j] + kj
            kl, kn = kl2[r, j], kn2[r, j]
            inv_h = 1.0 / hj
            g = g2[r - 2, j]
            gl, gn = g * sl2[r - 2, j], g * sn2[r - 2, j]
            back = []
            for part, (w_ref, v_ref) in enumerate(((wa, va), (wb, vb))):
                w = ws[part][j]
                dw = w - lanes_left(w)
                e, f = half_c * dw, kf * dw
                d_low, d_high = w - w_ref[r - 1, j], w - w_ref[r + 1, j]
                gk = e + lanes_right(e) + below[part][0] + above[part][0]
                gk = gk + half_l * d_low + half_h * d_high
                gh = lanes_right(f) - f + below[part][1] - above[part][1]
                gh = gh - k_low * d_low - k_high * d_high
                v = v_ref[r - 2, j]
                to_l = gk * kl - v * gl
                sums[3 * part] += gk * kj
                sums[3 * part + 1] += to_l
                sums[3 * part + 2] += gk * kn - v * gn
                back.append((v, gh + (to_l + v * g) * inv_h))
            store_heads(r, j, back, sums)
            above = below
        store_two(r, sums)
        return carry

    lax.fori_loop(0, 2, edge_two, 0)
    lax.fori_loop(2, 6, back_two, 0)

    refs = (w0, w1, w2)

    def store_one(r, sums, first):
        inv_k, inv_a = prm[r, IKS : IKS + 1, :], prm[r, IAL : IAL + 1, :]
        for q in range(3):
            for c in range(3):
                at = 4 * q + c
                row = size * jnp.sum(sums[3 * c + q], 0, keepdims=True)
                if not first:
                    row = row + maps[r, at : at + 1, :]
                maps[r, at : at + 1, :] = row if q == 2 else row * (inv_k if q == 0 else inv_a)

    def edge_one(i, carry):
        r = 7 * i
        near = 1 + 5 * i
        sums = [jnp.zeros((SUB, WIDTH), F32) for _ in range(9)]
        for j in range(TILES):
            half = h0[r, j] - h0[near, j]
            kj, kl, kn = k1[r, j], kl1[r, j], kn1[r, j]
            for part, w_ref in enumerate(refs):
                gk = half * w_ref[near, j]
                sums[3 * part] += gk * kj
                sums[3 * part + 1] += gk * kl
                sums[3 * part + 2] += gk * kn
        store_one(r, sums, True)
        return carry

    def back_one(r, carry):
        top = prm[r, LEV0 : LEV0 + 1, :]
        hs = [h0[r, j] for j in range(TILES)]
        ws = [[w[r, j] for j in range(TILES)] for w in refs]
        sums = [jnp.zeros((SUB, WIDTH), F32) for _ in range(9)]

        def face(j):
            if j < TILES - 1:
                half = 1.0 + hs[j] - hs[j + 1]
                return [half * (w[j + 1] - w[j]) for w in ws]
            half = 1.0 + hs[j] - subs_up(hs[0])
            return [jnp.where(is_bottom, -2.0 * w[j], half * (subs_up(w[0]) - w[j])) for w in ws]

        final = face(TILES - 1)
        above = [jnp.where(is_top, top * w[0], subs_down(f)) for w, f in zip(ws, final)]
        for j in range(TILES):
            below = final if j == TILES - 1 else face(j)
            hj = hs[j]
            half_c = jnp.where(last, 0.0, lanes_left(hj) - hj)
            half_l, half_h = h0[r - 1, j] - hj, h0[r + 1, j] - hj
            kj, kl, kn = k1[r, j], kl1[r, j], kn1[r, j]
            for part, w_ref in enumerate(refs):
                w = ws[part][j]
                e = half_c * (w - lanes_left(w))
                gk = e + lanes_right(e) + below[part] + above[part]
                gk = gk + half_l * (w - w_ref[r - 1, j]) + half_h * (w - w_ref[r + 1, j])
                sums[3 * part] += gk * kj
                sums[3 * part + 1] += gk * kl
                sums[3 * part + 2] += gk * kn
            above = below
        store_one(r, sums, False)
        return carry

    for r in range(ROWS):
        for at in (3, 7, 11):
            maps[r, at : at + 1, :] = jnp.zeros((1, WIDTH), F32)
        maps[r, 12:16, :] = jnp.zeros((4, WIDTH), F32)
    lax.fori_loop(0, 2, edge_one, 0)
    lax.fori_loop(1, 7, back_one, 0)

    left = jnp.concatenate([maps[r] for r in range(ROWS)], 1)
    near = zrel[...]
    zone_id = iota((32, WIDTH), 0)
    onehot = jnp.concatenate([(zone_id == near[r : r + 1, :]).astype(F32) for r in range(ROWS)], 1)
    onehot = onehot.astype(jnp.bfloat16)
    nt = (((1,), (1,)), ((), ()))
    parts = [lax.dot_general(part, onehot, nt, preferred_element_type=F32) for part in split3(left)]
    by_zone = parts[0] + (parts[1] + parts[2])
    fields = [by_zone[4 * q : 4 * q + 4, :] for q in range(3)]
    sub4 = iota((4, 32), 0)
    fields.append(jnp.where(sub4 == 0, loss[0], jnp.where(sub4 == 1, loss[1], loss[2])))
    sums = jnp.concatenate(fields, 1)
    state = jnp.where(iota((4, 128), 1) < 64, most, size)
    payload = jnp.where(iota((4, 128), 0) == 3, state, sums)
    spread[...] = jnp.broadcast_to(payload[None], spread.shape)


def ring_kernel(parts, spread):
    lane = iota((SUB, 256), 1)
    total = jnp.zeros((SUB, 256), F32)
    blank = jnp.zeros((SUB, 128), F32)
    most = None
    loss = jnp.zeros((SUB, 256), F32)
    for z in range(8):
        tile = jnp.concatenate([parts[z], parts[8 + z]], 0)
        most = tile if most is None else jnp.maximum(most, tile)
        tile = jnp.concatenate([tile, blank], 1)
        for q in range(3):
            start = 84 * q + 8 * z
            moved = pltpu.roll(tile, (start - 32 * q) % 256, 1)
            total = total + jnp.where(jnp.logical_and(lane >= start, lane < start + NEAR), moved, 0.0)
        loss = loss + tile
    total = jnp.where(lane == 252, pltpu.roll(loss, 252 - 96, 1), total)
    rows = []
    one = iota((1, 256), 1)
    for z_hi in range(2):
        state = most[4 * z_hi + 3 : 4 * z_hi + 4, :]
        for power in range(3):
            row = total[4 * z_hi + power : 4 * z_hi + power + 1, :]
            row = jnp.where(one == 253, state[:, 0:1], row)
            rows.append(jnp.where(one == 254, state[:, 64:65], row))
    rows = jnp.concatenate(rows, 1)
    spread[...] = jnp.broadcast_to(rows[None], spread.shape)


def last_kernel(parts, h1, g2, final, grad_k, grad_a, grad_n, misfit, rates):
    sums = [jnp.zeros((1, 256), F32) for _ in range(4)]
    for pair in range(8):
        tiles = [parts[8 * y + pair] for y in range(4)]
        for z_hi in range(2):
            powers = [[tile[:, 256 * (3 * z_hi + i) : 256 * (3 * z_hi + i + 1)] for i in range(3)] for tile in tiles]
            first = [part[0] for part in powers]
            most = jnp.maximum(jnp.maximum(first[0], first[1]), jnp.maximum(first[2], first[3]))
            step = CFL / most[:, 253:254]
            rates[2 * pair + z_hi] = jnp.broadcast_to(step, (1, 128))
            move = step - first[0][:, 254:255]
            for y in range(4):
                a, b, c = powers[y]
                sums[y] = sums[y] + (a + move * (b + move * c))
    lane = iota((1, 256), 1)
    rows = sums
    for q, out in enumerate((grad_k, grad_a, grad_n)):
        total = jnp.zeros((1, 256), F32)
        for y in range(4):
            field = rows[y] if q == 0 else pltpu.roll(rows[y], 256 - 84 * q, 1)
            total = total + pltpu.roll(jnp.where(lane < 84, field, 0.0), (64 * y - 4) % 256, 1)
        out[...] = total
    misfit[0, 0] = jnp.sum(jnp.where(lane == 252, rows[0] + rows[1] + rows[2] + rows[3], 0.0))
    _, pair, z_hi = axes()
    size = rates[2 * pair + z_hi]
    size = jnp.concatenate([size, size, size], 1)
    for j in range(TILES):
        for row in range(4):
            tile = h1[row, j] + size * g2[row, j]
            for s in range(SUB):
                final[TILES * s + j, row : row + 1, :] = tile[s : s + 1, :]


VMEM = pl.BlockSpec(memory_space=pltpu.VMEM)
SMEM = pl.BlockSpec(memory_space=pltpu.SMEM)


def call(kernel, name, ins, outs, out_specs=None, scratch=(), cost=None, in_place=None):
    return pl.pallas_call(
        kernel,
        name=name,
        in_specs=ins,
        out_specs=out_specs or [VMEM] * len(outs),
        out_shape=[jax.ShapeDtypeStruct(shape, dtype) for shape, dtype in outs],
        scratch_shapes=scratch,
        cost_estimate=cost,
        input_output_aliases=in_place or {},
        compiler_params=pltpu.CompilerParams(vmem_limit_bytes=32 * 1024 * 1024),
    )


def local(
    initial_head,
    sat_conductivity,
    vg_alpha,
    vg_n,
    zone_map,
    forcing_plan,
    tensiometer_cells,
    tensiometer_heads,
):
    count = lax.axis_size("row")
    plan = forcing_plan[0]
    edge = (2 * TILES + 1, SUB, WIDTH)
    h0, send_odd, send_even, zones = call(
        pack_kernel,
        "pack_edges",
        [pl.BlockSpec(memory_space=pltpu.HBM)] * 3,
        [(FIELD, F32), (edge, F32), (edge, F32), ((2, WIDTH), F32)],
        scratch=[
            pltpu.VMEM((48, 4, WIDTH), F32),
            pltpu.VMEM((2, 192), jnp.int32),
            pltpu.VMEM((2, 2), jnp.int32),
            pltpu.SemaphoreType.DMA((3,)),
        ],
    )(initial_head[0], zone_map, plan)
    odd = [(i, i + 1) for i in range(1, count - 1, 2)]
    even = [(i, i + 1) for i in range(0, count, 2)]
    got_odd = lax.ppermute(send_odd, "row", odd + [(j, i) for i, j in odd])
    got_even = lax.ppermute(send_even, "row", even + [(j, i) for i, j in even])
    wide = (6, TILES, SUB, WIDTH)
    fields = [(FIELD, F32)] * 3 + [(wide, F32)] * 4 + [((ROWS, 16, WIDTH), F32)]
    seen = tensiometer_cells.shape[1]
    own = call(
        own_kernel,
        "own_cells",
        [SMEM] * 4 + [VMEM] * 4,
        fields
        + [((2, TILES, SUB, WIDTH), F32), ((SUB, WIDTH), F32), ((SUB, 128), F32)]
        + [((seen, 192), jnp.bfloat16), ((192, seen), jnp.bfloat16), ((seen, WIDTH), F32), ((seen, 128), F32)],
        cost=pl.CostEstimate(flops=200_000_000, bytes_accessed=8_000_000, transcendentals=600_000),
    )(sat_conductivity, vg_alpha, vg_n, plan, h0, zones, tensiometer_cells, tensiometer_heads)
    own_fields, (part, most, near), sensors = own[:8], own[8:11], own[11:]
    first = call(
        first_kernel,
        "first_step",
        [VMEM] * 15,
        [(FIELD, F32)] + fields + [((ROWS, WIDTH), jnp.int32), ((32, 1, 128), F32)],
        in_place={6 + i: i for i in range(9)},
    )(near, zones, part, most, got_odd, got_even, h0, *own_fields)
    fields, rates = first[:-1], first[-1]
    rates = lax.all_to_all(rates, "row", 0, 0, tiled=True)
    h1, g2, sums = call(
        second_kernel,
        "second_step_and_adjoint",
        [VMEM] * 15,
        [(OWN, F32), (OWN, F32), ((16, 4, 128), F32)],
        scratch=[pltpu.VMEM(FIELD, F32)] * 4
        + [pltpu.VMEM(OWN, F32)] * 5
        + [pltpu.VMEM(FIELD, F32)] * 5
        + [pltpu.VMEM((ROWS, 16, WIDTH), F32)],
    )(rates, *sensors, *fields)
    sums = lax.all_to_all(sums, ("event", "row"), 0, 0, tiled=True, axis_index_groups=RINGS)
    (sums,) = call(ring_kernel, "ring_sums", [VMEM], [((32, 1, 6 * 256), F32)])(sums)
    sums = lax.all_to_all(sums, ("event", "row"), 0, 0, tiled=True, axis_index_groups=PLANES)
    row = ((1, ZONES), F32)
    final, grad_k, grad_a, grad_n, misfit = call(
        last_kernel,
        "final_head_and_sums",
        [VMEM, VMEM, VMEM],
        [((48, 4, WIDTH), F32), row, row, row, ((1, 1), F32)],
        [VMEM] * 4 + [SMEM],
        scratch=[pltpu.VMEM((16, 1, 128), F32)],
    )(sums, h1, g2)
    return (final[None], misfit[0, 0], grad_k[0], grad_a[0], grad_n[0])


def solution(mesh):
    return jax.shard_map(
        local,
        mesh=mesh,
        in_specs=(
            P("event", None, "row", None),
            P(),
            P(),
            P(),
            P("row", None),
            P("event", None, "row"),
            P("event", "row"),
            P("event", "row"),
        ),
        out_specs=(P("event", None, "row", None), P(), P(), P(), P()),
        check_vma=False,
    )
```

```python
import jax
import jax.numpy as jnp
from jax import lax
from jax.experimental import pallas as pl
from jax.experimental.pallas import tpu as pltpu
from jax.sharding import PartitionSpec as P

CFL = 0.4
IRRIGATION = 0.2
WATER_RANGE = 0.35

TILES = 6
SUB = 8
WIDTH = 384
ROWS = 8
FIELD = (ROWS, TILES, SUB, WIDTH)
OWN = (4, TILES, SUB, WIDTH)
NEAR = 28
ZONES = 256
KS, AL, N, N1, M, MP, IC0, IN1, LEV0, LEV1, IKS, IAL = range(12)
F32 = jnp.float32


def device(x, z_hi, core, y, z_lo):
    return ((x * 2 + z_hi) * 2 + core) * 32 + y * 8 + z_lo


PLANES = [
    [device(x, z_hi, core, y, z_lo) for y in range(4) for x in range(4) for core in range(2)]
    for z_hi in range(2)
    for z_lo in range(8)
]
RINGS = [
    [device(x, z_hi, core, y, z_lo) for z_hi in range(2) for z_lo in range(8)]
    for x in range(4)
    for core in range(2)
    for y in range(4)
]


def lanes_left(x):
    return pltpu.roll(x, WIDTH - 1, 1)


def lanes_right(x):
    return pltpu.roll(x, 1, 1)


def subs_up(x):
    return pltpu.roll(x, SUB - 1, 0)


def subs_down(x):
    return pltpu.roll(x, 1, 0)


def iota(shape, dim):
    return lax.broadcasted_iota(jnp.int32, shape, dim)


def split3(x):
    hi = x.astype(jnp.bfloat16)
    rest = x - hi.astype(F32)
    mid = rest.astype(jnp.bfloat16)
    return hi, mid, (rest - mid.astype(F32)).astype(jnp.bfloat16)


def exact_dot(pick, x, dims=(((1,), (0,)), ((), ()))):
    parts = [lax.dot_general(pick, part, dims, preferred_element_type=F32) for part in split3(x)]
    return parts[0] + (parts[1] + parts[2])


def axes():
    event = lax.axis_index("event")
    return lax.axis_index("row"), event // 4 * 2 + event % 2, event // 2 % 2


def pack_kernel(head_in, zone_in, plan_in, h0, send_odd, send_even, zones, head, zone, plan, sems):
    copies = [
        pltpu.make_async_copy(src, dst, sems.at[i])
        for i, (src, dst) in enumerate(((head_in, head), (zone_in, zone), (plan_in, plan)))
    ]
    for copy in copies:
        copy.start()
    wide = (iota((192, WIDTH), 1) // 2 == iota((192, WIDTH), 0)).astype(F32)
    copies[1].wait()
    copies[2].wait()
    blocks = jnp.dot(zone[...].astype(F32), wide, preferred_element_type=F32)
    zones[...] = blocks
    level = plan[...].astype(F32)
    copies[0].wait()
    for depth in range(TILES * SUB):
        block = head[depth]
        j, s = depth % TILES, depth // TILES
        for row in range(4):
            h0[2 + row, j, s : s + 1, :] = block[row : row + 1, :]
    sub = iota((SUB, WIDTH), 0)
    odd = lax.axis_index("row") % 2 == 1

    def fill(out, pair):
        out[0:TILES] = h0[2 + 2 * pair]
        out[TILES : 2 * TILES] = h0[3 + 2 * pair]
        out[2 * TILES] = jnp.where(sub == 0, blocks[pair : pair + 1, :], level[0:1, pair : pair + 1])

    @pl.when(odd)
    def _():
        fill(send_odd, 1)
        fill(send_even, 0)

    @pl.when(jnp.logical_not(odd))
    def _():
        fill(send_odd, 0)
        fill(send_even, 1)


def cell_math(head, p, with_store=True):
    wet = jnp.log(-p[AL] * head)
    u = jnp.exp(p[N] * wet)
    d = 1.0 + u
    w = jnp.log(d)
    inv = 1.0 / d
    r = u * inv
    mw = p[M] * w
    q = jnp.exp(-0.5 * mw)
    f = jnp.exp(p[N1] * wet - mw)
    t = 1.0 - f
    kq = p[KS] * q * t
    half, twice = -0.5 * t, 2.0 * f
    e1 = p[MP] * w + p[M] * wet * r
    cond = kq * t
    cond_l = kq * p[N1] * (half * r - twice * inv)
    cond_n = kq * (half * e1 - twice * (wet - e1))
    if not with_store:
        return cond, cond_l, cond_n
    inv_store = d * p[IC0] / f
    store_l = p[N] - r * (2.0 * p[N] - 1.0)
    store_n = p[IN1] + wet - e1 - r * wet
    return cond, cond_l, cond_n, inv_store, store_l, store_n


def derived(sat, alpha, n):
    n1 = n - 1.0
    return (
        sat, alpha, n, n1, 1.0 - 1.0 / n, 1.0 / (n * n), 0.5 / (WATER_RANGE * n1 * alpha), 1.0 / n1,
    )


def row_params(prm, r):
    return [prm[r, i : i + 1, :] for i in range(8)]


def masks():
    last = iota((SUB, WIDTH), 1) == WIDTH - 1
    sub = iota((SUB, WIDTH), 0)
    return last, sub == 0, sub == SUB - 1


def net_row(h, k, r, top, beside):
    last, is_top, is_bottom = masks()
    hs = [h[r, j] for j in range(TILES)]
    ks = [k[r, j] for j in range(TILES)]

    def face(j):
        if j < TILES - 1:
            kd = ks[j] + ks[j + 1]
            return kd, kd * (1.0 + hs[j] - hs[j + 1])
        kd = ks[j] + subs_up(ks[0])
        flow = kd * (1.0 + hs[j] - subs_up(hs[0]))
        return jnp.where(is_bottom, 2.0 * ks[j], kd), jnp.where(is_bottom, 2.0 * ks[j], flow)

    final = face(TILES - 1)
    above = (
        jnp.where(is_top, 2.0 * ks[0], subs_down(final[0])),
        jnp.where(is_top, top * ks[0], subs_down(final[1])),
    )
    for j in range(TILES):
        below = final if j == TILES - 1 else face(j)
        hj, kj = hs[j], ks[j]
        kf = jnp.where(last, 0.0, kj + lanes_left(kj))
        flow = kf * (lanes_left(hj) - hj)
        net = flow - lanes_right(flow) + above[1] - below[1]
        total = kf + lanes_right(kf) + above[0] + below[0]
        for other in beside:
            kx = k[other, j] + kj
            net = net + kx * (h[other, j] - hj)
            total = total + kx
        above = below
        yield j, net, total


def reach_row(h, phis, ic, psi, r, same, foreign, top):
    lane = iota((SUB, WIDTH), 1)
    even = lane % 2 == 0
    ends = jnp.logical_or(lane == 0, lane == WIDTH - 1)
    _, is_top, is_bottom = masks()

    def beside(x):
        left, right = lanes_right(x), lanes_left(x)
        return jnp.where(even, right, left), jnp.where(even, left, right)

    for j in range(TILES):
        hj, half = h[r, j], ic[r - 1, j]
        inner, outer = beside(hj)
        d_in = inner - hj
        d_out = jnp.where(ends, 0.0, outer - hj)
        h_below = h[r, j + 1] if j < TILES - 1 else subs_up(h[r, 0])
        h_above = h[r, j - 1] if j > 0 else subs_down(h[r, TILES - 1])
        d_below, d_above = h_below - hj - 1.0, 1.0 + h_above - hj
        self_below, self_above = d_below, d_above
        if j == TILES - 1:
            self_below, d_below = jnp.where(is_bottom, -2.0, d_below), jnp.where(is_bottom, 0.0, d_below)
        if j == 0:
            self_above, d_above = jnp.where(is_top, top, d_above), jnp.where(is_top, 0.0, d_above)
        d_same = h[same, j] - hj
        whole = d_in + d_out + self_below + self_above + d_same
        if foreign is not None:
            d_far = h[foreign, j] - hj
            whole = whole + d_far
        for i, phi in enumerate(phis):
            below = phi[r, j + 1] if j < TILES - 1 else subs_up(phi[r, 0])
            above = phi[r, j - 1] if j > 0 else subs_down(phi[r, TILES - 1])
            inner, outer = beside(phi[r, j])
            own = whole * phi[r, j] + d_in * inner + d_below * below + d_above * above + d_same * phi[same, j]
            psi[i][r - 1, j] = half * own
            psi[3 + i][r - 1, j] = (half * d_out) * outer
            if foreign is not None:
                psi[6 + i][r - 1, j] = (half * d_far) * phi[foreign, j]


def places(cell):
    line = jnp.floor((cell + 0.5) * (1.0 / WIDTH))
    column = cell - WIDTH * line
    depth = jnp.floor((line + 0.5) * 0.25)
    block = jnp.floor((depth + 0.5) * (1.0 / TILES))
    return (line - 4.0 * depth) * 48.0 + (depth - TILES * block) * 8.0 + block, column


def own_kernel(
    tab_k, tab_a, tab_n, plan, h0, zones, cells_at, goals,
    g1, *rest,
):
    psi, rest = rest[:9], rest[9:]
    prm, most_out, near, pick, put, column, goal, k1, kl1, kn1, ic1, p1, q1 = rest
    base = 8 * lax.axis_index("row") - 4
    sub = iota((SUB, WIDTH), 0)
    rel = (jnp.where(sub < 2, zones[0:1, :], zones[1:2, :]).astype(jnp.int32) - base) & (ZONES - 1)
    sat = jnp.ones((SUB, WIDTH), F32)
    alpha, n = sat, 2.0 * sat
    lane = iota((SUB, 128), 1)
    line = iota((SUB, 128), 0)
    table = jnp.ones((SUB, 128), F32)
    for i in range(NEAR):
        at = (base + i) & (ZONES - 1)
        here = rel == i
        sat = jnp.where(here, tab_k[at], sat)
        alpha = jnp.where(here, tab_a[at], alpha)
        n = jnp.where(here, tab_n[at], n)
        entry = jnp.where(line == 0, tab_k[at], jnp.where(line == 1, tab_a[at], tab_n[at]))
        table = jnp.where(lane == i, entry, table)
    near[...] = table
    levels = [
        2.0 * IRRIGATION * jnp.where(sub < 2, plan[step, 0].astype(F32), plan[step, 1].astype(F32))
        for step in range(2)
    ]
    for i, value in enumerate(derived(sat, alpha, n) + (*levels, 1.0 / sat, 1.0 / alpha)):
        for r in range(4):
            prm[2 + r, i : i + 1, :] = value[r : r + 1, :]

    def cells(r, carry):
        p = row_params(prm, r)
        for j in range(TILES):
            values = cell_math(h0[r, j], p)
            k1[r, j], kl1[r, j], kn1[r, j], ic1[r - 1, j], p1[r - 1, j], q1[r - 1, j] = values
        return carry

    lax.fori_loop(2, 6, cells, 0)

    def flow(r, most):
        for j, net, total in net_row(h0, k1, r, prm[r, LEV0 : LEV0 + 1, :], (r - 1, r + 1)):
            ic = ic1[r - 1, j]
            g = net * ic
            g1[r - 1, j] = g
            p1[r - 1, j] = g * p1[r - 1, j]
            q1[r - 1, j] = g * q1[r - 1, j]
            most = jnp.maximum(most, total * ic)
        return most

    def edge_flow(i, carry):
        r = 2 + 3 * i
        for j, net, total in net_row(h0, k1, r, prm[r, LEV0 : LEV0 + 1, :], (3 + i,)):
            g1[r - 1, j] = net
            g1[5 * i, j] = total
            for at, value in enumerate((k1[r, j], kl1[r, j], kn1[r, j])):
                psi[at][5 * i, j] = value
            for at, value in enumerate((ic1[r - 1, j], p1[r - 1, j], q1[r - 1, j])):
                psi[3 + at][5 * i, j] = value
        return carry

    most_out[...] = lax.fori_loop(3, 5, flow, jnp.zeros((SUB, WIDTH), F32))
    lax.fori_loop(0, 2, edge_flow, 0)
    phis = (k1, kl1, kn1)

    def reach(i, carry):
        r = 3 + i
        reach_row(h0, phis, ic1, psi, r, 2 + 3 * i, 4 - i, prm[r, LEV0 : LEV0 + 1, :])
        for j in range(TILES):
            psi[1][r - 1, j] = psi[1][r - 1, j] - p1[r - 1, j]
            psi[2][r - 1, j] = psi[2][r - 1, j] - q1[r - 1, j]
        return carry

    def edge_reach(i, carry):
        r = 2 + 3 * i
        reach_row(h0, phis, ic1, psi, r, 3 + i, None, prm[r, LEV0 : LEV0 + 1, :])
        return carry

    lax.fori_loop(0, 2, reach, 0)
    lax.fori_loop(0, 2, edge_reach, 0)

    count = cells_at.shape[1]
    wide = jnp.where(iota((SUB, count), 0) == 0, cells_at[...].astype(F32), goals[...])
    tall = jnp.transpose(wide)
    line_wide = places(wide[0:1, :])[0].astype(jnp.int32)
    line_tall, column_tall = places(tall[:, 0:1])
    pick[...] = (iota((count, 192), 1) == line_tall.astype(jnp.int32)).astype(F32).astype(jnp.bfloat16)
    put[...] = (iota((192, count), 0) == line_wide).astype(F32).astype(jnp.bfloat16)
    column[...] = (iota((count, WIDTH), 1) == column_tall.astype(jnp.int32)).astype(F32).astype(jnp.bfloat16)
    goal[...] = jnp.broadcast_to(tall[:, 1:2], goal.shape)


def first_kernel(
    near, zones, most_in, got_odd, got_even, *rest
):
    h0, g1, *psi = rest[12:23]
    prm, zrel, spread, k1, kl1, kn1, ic1, sl, sn, part, edge = rest[23:]
    position = lax.axis_index("row")
    has_low, has_high = position > 0, position < lax.axis_size("row") - 1
    odd = position % 2 == 1
    for row in range(2):
        for j in range(TILES):
            at = row * TILES + j
            one, other = got_odd[at], got_even[at]
            h0[row, j] = jnp.where(has_low, jnp.where(odd, other, one), h0[2, j])
            h0[6 + row, j] = jnp.where(has_high, jnp.where(odd, one, other), h0[5, j])
    for i in range(2):
        part[i] = g1[5 * i]
        for at, phi in enumerate((k1, kl1, kn1)):
            phi[2 + 3 * i] = psi[at][5 * i]
            edge[at, i] = psi[3 + at][5 * i]
    one, other = got_odd[2 * TILES], got_even[2 * TILES]
    extra_low, extra_high = jnp.where(odd, other, one), jnp.where(odd, one, other)
    z_low = jnp.where(has_low, extra_low[0:1, :], zones[0:1, :])
    z_high = jnp.where(has_high, extra_high[0:1, :], zones[1:2, :])
    sub = iota((SUB, WIDTH), 0)
    zone = jnp.where(
        sub < 4,
        jnp.where(sub < 2, z_low, zones[0:1, :]),
        jnp.where(sub < 6, zones[1:2, :], z_high),
    ).astype(jnp.int32)
    rel = (zone - (8 * position - 4)) & (ZONES - 1)
    zrel[...] = rel
    ids = iota((32, WIDTH), 0)
    sides = []
    for r in (0, 7):
        here = (ids == rel[r : r + 1, :]).astype(F32).astype(jnp.bfloat16)
        parts = [jnp.dot(x, here, preferred_element_type=F32) for x in split3(near[:, :32])]
        sides.append(parts[0] + (parts[1] + parts[2]))
    sat, alpha, n = (
        jnp.where(sub < 4, sides[0][i : i + 1, :], sides[1][i : i + 1, :]) for i in range(3)
    )
    level = 2.0 * IRRIGATION * jnp.where(sub < 4, extra_low[1:2, :], extra_high[1:2, :])
    for i, value in enumerate(derived(sat, alpha, n) + (level, level, 1.0 / sat, 1.0 / alpha)):
        for r in (0, 1, 6, 7):
            prm[r, i : i + 1, :] = value[r : r + 1, :]

    def outer(i, carry):
        r = 7 * i
        p = row_params(prm, r)
        for j in range(TILES):
            k1[r, j], kl1[r, j], kn1[r, j] = cell_math(h0[r, j], p, False)
        return carry

    def inner(i, carry):
        r, own = 1 + 5 * i, 2 + 3 * i
        real = jnp.where(i == 0, has_low, has_high)
        p = row_params(prm, r)
        for j in range(TILES):
            cond, kl1[r, j], kn1[r, j], ic1[r - 1, j], sl[i, j], sn[i, j] = cell_math(h0[r, j], p)
            k1[r, j] = jnp.where(real, cond, -k1[own, j])
        return carry

    lax.fori_loop(0, 2, outer, 0)
    lax.fori_loop(0, 2, inner, 0)

    def flow(i, most):
        r, own = 1 + 5 * i, 2 + 3 * i
        real = jnp.where(i == 0, has_low, has_high)
        reach_row(h0, (k1, kl1, kn1), ic1, psi, r, 7 * i, own, prm[r, LEV0 : LEV0 + 1, :])
        for j, net, _ in net_row(h0, k1, r, prm[r, LEV0 : LEV0 + 1, :], (r - 1, r + 1)):
            g = jnp.where(real, net * ic1[r - 1, j], 0.0)
            g1[r - 1, j] = g
            psi[1][r - 1, j] = psi[1][r - 1, j] - g * sl[i, j]
            psi[2][r - 1, j] = psi[2][r - 1, j] - g * sn[i, j]
            kx = k1[r, j] + k1[own, j]
            ic = edge[0, i, j]
            d = h0[r, j] - h0[own, j]
            g = (g1[own - 1, j] + kx * d) * ic
            g1[own - 1, j] = g
            d = d * ic
            psi[0][own - 1, j] = psi[0][own - 1, j] + d * k1[own, j]
            psi[1][own - 1, j] = psi[1][own - 1, j] + d * kl1[own, j] - g * edge[1, i, j]
            psi[2][own - 1, j] = psi[2][own - 1, j] + d * kn1[own, j] - g * edge[2, i, j]
            for q, phi in enumerate((k1, kl1, kn1)):
                psi[6 + q][own - 1, j] = d * phi[r, j]
            most = jnp.maximum(most, (part[i, j] + kx) * ic)
        return most

    most = lax.fori_loop(0, 2, flow, most_in[...])
    most = jnp.maximum(jnp.maximum(most[:, :128], most[:, 128:256]), most[:, 256:])
    most = jnp.max(most, 0, keepdims=True)
    spread[...] = jnp.broadcast_to(most[None], spread.shape)


def second_kernel(rates, pick, put, column_in, goal, h0, g1, *rest):
    psi, rest = rest[:9], rest[9:]
    prm, zrel, h1_out, g2, spread, *rest = rest
    h1, k2, kl2, kn2, ic2, sl2, sn2, va, vb, wa, wb, u0, u1, u2, maps, maps_f, maps_g = rest
    position = lax.axis_index("row")
    size = CFL / jnp.max(rates[...])
    nothing = jnp.zeros((TILES, SUB, WIDTH), F32)
    for r in (1, 6):
        for ref in (wa, wb):
            ref[r] = nothing

    def cells(r, carry):
        p = row_params(prm, r)
        for j in range(TILES):
            head = h0[r, j] + size * g1[r - 1, j]
            h1[r, j] = head
            h1_out[r - 2, j] = head
            values = cell_math(head, p)
            k2[r, j], kl2[r, j], kn2[r, j], ic2[r - 2, j], sl2[r - 2, j], sn2[r - 2, j] = values
        return carry

    def edge_cells(i, carry):
        r = 1 + 5 * i
        p = row_params(prm, r)
        own = 2 + 3 * i
        real = jnp.where(i == 0, position > 0, position < lax.axis_size("row") - 1)
        for j in range(TILES):
            head = jnp.where(real, h0[r, j] + size * g1[r - 1, j], h1[own, j])
            h1[r, j] = head
            cond, kl2[r, j], kn2[r, j] = cell_math(head, p, False)
            k2[r, j] = jnp.where(real, cond, -k2[own, j])
        return carry

    lax.fori_loop(2, 6, cells, 0)
    lax.fori_loop(0, 2, edge_cells, 0)

    def flow(r, most):
        for j, net, total in net_row(h1, k2, r, prm[r, LEV1 : LEV1 + 1, :], (r - 1, r + 1)):
            ic = ic2[r - 2, j]
            g2[r - 2, j] = net * ic
            most = jnp.maximum(most, total * ic)
        return most

    most = jnp.max(lax.fori_loop(2, 6, flow, jnp.zeros((SUB, WIDTH), F32)))

    column = column_in[...].astype(F32)
    field_g = g2[...].reshape(192, WIDTH)
    field_h = h1_out[...].reshape(192, WIDTH) + size * field_g
    seen_h = jnp.sum(column * exact_dot(pick[...], field_h), 1, keepdims=True)
    seen_g = jnp.sum(column * exact_dot(pick[...], field_g), 1, keepdims=True)
    diff = seen_h - goal[:, 0:1]
    events = 16.0
    loss = (
        jnp.sum(diff * diff) * (0.5 / events),
        jnp.sum(diff * seen_g) * (1.0 / events),
        jnp.sum(seen_g * seen_g) * (0.5 / events),
    )
    va[...] = exact_dot(put[...], column * (diff * (1.0 / events))).reshape(OWN)
    vb[...] = exact_dot(put[...], column * (seen_g * (1.0 / events))).reshape(OWN)

    def scaled(r, carry):
        for j in range(TILES):
            ic = ic2[r - 2, j]
            wa[r, j] = va[r - 2, j] * ic
            wb[r, j] = vb[r - 2, j] * ic
        return carry

    lax.fori_loop(2, 6, scaled, 0)
    last, is_top, is_bottom = masks()

    def store_two(r, sums):
        flat = [jnp.sum(x, 0, keepdims=True) for x in sums]
        for q in range(3):
            of_a, of_b = flat[q], flat[3 + q]
            for c, row in enumerate((size * of_a, of_a + size * of_b, of_b)):
                maps[r - 1, 4 * q + c : 4 * q + c + 1, :] = row

    def store_heads(r, j, back):
        (v_a, j_a), (v_b, j_b) = back
        u0[r - 1, j] = v_a + size * j_a
        u1[r - 1, j] = v_b + j_a + size * j_b
        u2[r - 1, j] = j_b

    def edge_two(i, carry):
        r = 1 + 5 * i
        near = 2 + 3 * i
        sums = [jnp.zeros((SUB, WIDTH), F32) for _ in range(6)]
        for j in range(TILES):
            hj = h1[r, j]
            half = h1[near, j] - hj
            kd = k2[near, j] + k2[r, j]
            kj, kl, kn = k2[r, j], kl2[r, j], kn2[r, j]
            inv_h = 1.0 / hj
            back = []
            for part, w_ref in enumerate((wa, wb)):
                w = w_ref[near, j]
                gk, gh = -half * w, kd * w
                to_l = gk * kl
                sums[3 * part] += gk * kj
                sums[3 * part + 1] += to_l
                sums[3 * part + 2] += gk * kn
                back.append((0.0, gh + to_l * inv_h))
            store_heads(r, j, back)
        store_two(r, sums)
        return carry

    def back_two(r, carry):
        top = prm[r, LEV1 : LEV1 + 1, :]
        hs = [h1[r, j] for j in range(TILES)]
        ks = [k2[r, j] for j in range(TILES)]
        sums = [jnp.zeros((SUB, WIDTH), F32) for _ in range(6)]
        ws = [[w[r, j] for j in range(TILES)] for w in (wa, wb)]

        def face(j):
            if j < TILES - 1:
                half = 1.0 + hs[j] - hs[j + 1]
                kd = ks[j] + ks[j + 1]
                out = []
                for w in ws:
                    dw = w[j + 1] - w[j]
                    out.append((half * dw, kd * dw))
                return out
            half = 1.0 + hs[j] - subs_up(hs[0])
            kd = ks[j] + subs_up(ks[0])
            out = []
            for w in ws:
                dw = subs_up(w[0]) - w[j]
                out.append((jnp.where(is_bottom, -2.0 * w[j], half * dw), jnp.where(is_bottom, 0.0, kd * dw)))
            return out

        final = face(TILES - 1)
        above = [
            (jnp.where(is_top, top * w[0], subs_down(f[0])), subs_down(f[1]))
            for w, f in zip(ws, final)
        ]
        for j in range(TILES):
            below = final if j == TILES - 1 else face(j)
            hj, kj = hs[j], ks[j]
            half_c = jnp.where(last, 0.0, lanes_left(hj) - hj)
            kf = jnp.where(last, 0.0, lanes_left(kj) + kj)
            half_l, half_h = h1[r - 1, j] - hj, h1[r + 1, j] - hj
            k_low, k_high = k2[r - 1, j] + kj, k2[r + 1, j] + kj
            kl, kn = kl2[r, j], kn2[r, j]
            inv_h = 1.0 / hj
            g = g2[r - 2, j]
            gl, gn = g * sl2[r - 2, j], g * sn2[r - 2, j]
            back = []
            for part, (w_ref, v_ref) in enumerate(((wa, va), (wb, vb))):
                w = ws[part][j]
                dw = w - lanes_left(w)
                e, f = half_c * dw, kf * dw
                d_low, d_high = w - w_ref[r - 1, j], w - w_ref[r + 1, j]
                gk = e + lanes_right(e) + below[part][0] + above[part][0]
                gk = gk + half_l * d_low + half_h * d_high
                gh = lanes_right(f) - f + below[part][1] - above[part][1]
                gh = gh - k_low * d_low - k_high * d_high
                v = v_ref[r - 2, j]
                to_l = gk * kl - v * gl
                sums[3 * part] += gk * kj
                sums[3 * part + 1] += to_l
                sums[3 * part + 2] += gk * kn - v * gn
                back.append((v, gh + (to_l + v * g) * inv_h))
            store_heads(r, j, back)
            above = below
        store_two(r, sums)
        return carry

    lax.fori_loop(0, 2, edge_two, 0)
    lax.fori_loop(2, 6, back_two, 0)

    for ref in (maps, maps_f, maps_g):
        for r in range(6):
            for at in (3, 7, 11):
                ref[r, at : at + 1, :] = jnp.zeros((1, WIDTH), F32)
            ref[r, 12:16, :] = jnp.zeros((4, WIDTH), F32)

    def first_part(r, carry):
        for q in range(3):
            sums = [[jnp.zeros((SUB, WIDTH), F32) for _ in range(3)] for _ in range(3)]
            for j in range(TILES):
                us = [ref[r, j] for ref in (u0, u1, u2)]
                for kind in range(3):
                    factor = psi[3 * kind + q][r, j]
                    for c in range(3):
                        sums[kind][c] += us[c] * factor
            for c in range(3):
                at = 4 * q + c
                own, column_off, row_off = (jnp.sum(sums[kind][c], 0, keepdims=True) for kind in range(3))
                maps[r, at : at + 1, :] = maps[r, at : at + 1, :] + size * own
                maps_f[r, at : at + 1, :] = size * column_off
                maps_g[r, at : at + 1, :] = size * row_off
        return carry

    lax.fori_loop(0, 6, first_part, 0)

    odd = iota((16, WIDTH), 1) % 2 == 1
    which = iota((16, WIDTH), 0)
    pieces = []
    for r in range(6):
        off = maps_f[r]
        off = jnp.where(odd, lanes_left(off), lanes_right(off))
        other = r + 1 if r % 2 == 0 else r - 1
        scale = jnp.where(which < 4, prm[r + 1, IKS : IKS + 1, :], jnp.where(which < 8, prm[r + 1, IAL : IAL + 1, :], 1.0))
        pieces.append((maps[r] + off + maps_g[other]) * scale)
    left = jnp.concatenate(pieces, 1)
    near = zrel[...]
    zone_id = iota((32, WIDTH), 0)
    onehot = jnp.concatenate([(zone_id == near[r : r + 1, :]).astype(F32) for r in range(1, 7)], 1)
    onehot = onehot.astype(jnp.bfloat16)
    nt = (((1,), (1,)), ((), ()))
    parts = [lax.dot_general(part, onehot, nt, preferred_element_type=F32) for part in split3(left)]
    by_zone = parts[0] + (parts[1] + parts[2])
    fields = [by_zone[4 * q : 4 * q + 4, :] for q in range(3)]
    sub4 = iota((4, 32), 0)
    fields.append(jnp.where(sub4 == 0, loss[0], jnp.where(sub4 == 1, loss[1], loss[2])))
    sums = jnp.concatenate(fields, 1)
    state = jnp.where(iota((4, 128), 1) < 64, most, size)
    payload = jnp.where(iota((4, 128), 0) == 3, state, sums)
    spread[...] = jnp.broadcast_to(payload[None], spread.shape)


def ring_kernel(parts, spread):
    lane = iota((SUB, 256), 1)
    total = jnp.zeros((SUB, 256), F32)
    blank = jnp.zeros((SUB, 128), F32)
    most = None
    loss = jnp.zeros((SUB, 256), F32)
    for z in range(8):
        tile = jnp.concatenate([parts[z], parts[8 + z]], 0)
        most = tile if most is None else jnp.maximum(most, tile)
        tile = jnp.concatenate([tile, blank], 1)
        for q in range(3):
            start = 84 * q + 8 * z
            moved = pltpu.roll(tile, (start - 32 * q) % 256, 1)
            total = total + jnp.where(jnp.logical_and(lane >= start, lane < start + NEAR), moved, 0.0)
        loss = loss + tile
    total = jnp.where(lane == 252, pltpu.roll(loss, 252 - 96, 1), total)
    rows = []
    one = iota((1, 256), 1)
    for z_hi in range(2):
        state = most[4 * z_hi + 3 : 4 * z_hi + 4, :]
        for power in range(3):
            row = total[4 * z_hi + power : 4 * z_hi + power + 1, :]
            row = jnp.where(one == 253, state[:, 0:1], row)
            rows.append(jnp.where(one == 254, state[:, 64:65], row))
    rows = jnp.concatenate(rows, 1)
    spread[...] = jnp.broadcast_to(rows[None], spread.shape)


def last_kernel(parts, h1, g2, final, grad_k, grad_a, grad_n, misfit, rates):
    sums = [jnp.zeros((1, 256), F32) for _ in range(4)]
    for pair in range(8):
        tiles = [parts[8 * y + pair] for y in range(4)]
        for z_hi in range(2):
            powers = [[tile[:, 256 * (3 * z_hi + i) : 256 * (3 * z_hi + i + 1)] for i in range(3)] for tile in tiles]
            first = [part[0] for part in powers]
            most = jnp.maximum(jnp.maximum(first[0], first[1]), jnp.maximum(first[2], first[3]))
            step = CFL / most[:, 253:254]
            rates[2 * pair + z_hi] = jnp.broadcast_to(step, (1, 128))
            move = step - first[0][:, 254:255]
            for y in range(4):
                a, b, c = powers[y]
                sums[y] = sums[y] + (a + move * (b + move * c))
    lane = iota((1, 256), 1)
    rows = sums
    for q, out in enumerate((grad_k, grad_a, grad_n)):
        total = jnp.zeros((1, 256), F32)
        for y in range(4):
            field = rows[y] if q == 0 else pltpu.roll(rows[y], 256 - 84 * q, 1)
            total = total + pltpu.roll(jnp.where(lane < 84, field, 0.0), (64 * y - 4) % 256, 1)
        out[...] = total
    misfit[0, 0] = jnp.sum(jnp.where(lane == 252, rows[0] + rows[1] + rows[2] + rows[3], 0.0))
    _, pair, z_hi = axes()
    size = rates[2 * pair + z_hi]
    size = jnp.concatenate([size, size, size], 1)
    for j in range(TILES):
        for row in range(4):
            tile = h1[row, j] + size * g2[row, j]
            for s in range(SUB):
                final[TILES * s + j, row : row + 1, :] = tile[s : s + 1, :]


VMEM = pl.BlockSpec(memory_space=pltpu.VMEM)
SMEM = pl.BlockSpec(memory_space=pltpu.SMEM)


def call(kernel, name, ins, outs, out_specs=None, scratch=(), cost=None, in_place=None, room=8):
    return pl.pallas_call(
        kernel,
        name=name,
        in_specs=ins,
        out_specs=out_specs or [VMEM] * len(outs),
        out_shape=[jax.ShapeDtypeStruct(shape, dtype) for shape, dtype in outs],
        scratch_shapes=scratch,
        cost_estimate=cost,
        input_output_aliases=in_place or {},
        compiler_params=pltpu.CompilerParams(vmem_limit_bytes=room * 1024 * 1024),
    )


def local(
    initial_head,
    sat_conductivity,
    vg_alpha,
    vg_n,
    zone_map,
    forcing_plan,
    tensiometer_cells,
    tensiometer_heads,
):
    count = lax.axis_size("row")
    plan = forcing_plan[0]
    edge = (2 * TILES + 1, SUB, WIDTH)
    h0, send_odd, send_even, zones = call(
        pack_kernel,
        "pack_edges",
        [pl.BlockSpec(memory_space=pltpu.HBM)] * 3,
        [(FIELD, F32), (edge, F32), (edge, F32), ((2, WIDTH), F32)],
        scratch=[
            pltpu.VMEM((48, 4, WIDTH), F32),
            pltpu.VMEM((2, 192), jnp.int32),
            pltpu.VMEM((2, 2), jnp.int32),
            pltpu.SemaphoreType.DMA((3,)),
        ],
    )(initial_head[0], zone_map, plan)
    odd = [(i, i + 1) for i in range(1, count - 1, 2)]
    even = [(i, i + 1) for i in range(0, count, 2)]
    got_odd = lax.ppermute(send_odd, "row", odd + [(j, i) for i, j in odd])
    got_even = lax.ppermute(send_even, "row", even + [(j, i) for i, j in even])
    wide = (6, TILES, SUB, WIDTH)
    fields = [(wide, F32)] * 10 + [((ROWS, 16, WIDTH), F32)]
    pair = (2, TILES, SUB, WIDTH)
    whole = [pltpu.VMEM(FIELD, F32)] * 3 + [pltpu.VMEM(wide, F32)]
    seen = tensiometer_cells.shape[1]
    own = call(
        own_kernel,
        "own_cells",
        [SMEM] * 4 + [VMEM] * 4,
        fields
        + [((SUB, WIDTH), F32), ((SUB, 128), F32)]
        + [((seen, 192), jnp.bfloat16), ((192, seen), jnp.bfloat16), ((seen, WIDTH), jnp.bfloat16), ((seen, 128), F32)],
        scratch=whole + [pltpu.VMEM(wide, F32)] * 2,
        cost=pl.CostEstimate(flops=200_000_000, bytes_accessed=8_000_000, transcendentals=600_000),
    )(sat_conductivity, vg_alpha, vg_n, plan, h0, zones, tensiometer_cells, tensiometer_heads)
    own_fields, (most, near), sensors = own[:11], own[11:13], own[13:]
    first = call(
        first_kernel,
        "first_step",
        [VMEM] * 17,
        [(FIELD, F32)] + fields + [((ROWS, WIDTH), jnp.int32), ((32, 1, 128), F32)],
        scratch=whole + [pltpu.VMEM(pair, F32)] * 3 + [pltpu.VMEM((3, *pair), F32)],
        in_place={5 + i: i for i in range(12)},
    )(near, zones, most, got_odd, got_even, h0, *own_fields)
    fields, rates = first[:-1], first[-1]
    rates = lax.all_to_all(rates, "row", 0, 0, tiled=True)
    h1, g2, sums = call(
        second_kernel,
        "second_step_and_adjoint",
        [VMEM] * 18,
        [(OWN, F32), (OWN, F32), ((16, 4, 128), F32)],
        scratch=[pltpu.VMEM(FIELD, F32)] * 4
        + [pltpu.VMEM(OWN, F32)] * 5
        + [pltpu.VMEM(FIELD, F32)] * 2
        + [pltpu.VMEM(wide, F32)] * 3
        + [pltpu.VMEM((6, 16, WIDTH), F32)] * 3,
        room=20,
    )(rates, *sensors, *fields)
    sums = lax.all_to_all(sums, ("event", "row"), 0, 0, tiled=True, axis_index_groups=RINGS)
    (sums,) = call(ring_kernel, "ring_sums", [VMEM], [((32, 1, 6 * 256), F32)])(sums)
    sums = lax.all_to_all(sums, ("event", "row"), 0, 0, tiled=True, axis_index_groups=PLANES)
    row = ((1, ZONES), F32)
    final, grad_k, grad_a, grad_n, misfit = call(
        last_kernel,
        "final_head_and_sums",
        [VMEM, VMEM, VMEM],
        [((48, 4, WIDTH), F32), row, row, row, ((1, 1), F32)],
        [VMEM] * 4 + [SMEM],
        scratch=[pltpu.VMEM((16, 1, 128), F32)],
    )(sums, h1, g2)
    return (final[None], misfit[0, 0], grad_k[0], grad_a[0], grad_n[0])


def solution(mesh):
    return jax.shard_map(
        local,
        mesh=mesh,
        in_specs=(
            P("event", None, "row", None),
            P(),
            P(),
            P(),
            P("row", None),
            P("event", None, "row"),
            P("event", "row"),
            P("event", "row"),
        ),
        out_specs=(P("event", None, "row", None), P(), P(), P(), P()),
        check_vma=False,
    )
```

```python
import functools

import jax
import jax.numpy as jnp
from jax import lax
from jax.experimental import pallas as pl
from jax.experimental.pallas import tpu as pltpu
from jax.sharding import PartitionSpec as P

CFL = 0.4
IRRIGATION = 0.2
WATER_RANGE = 0.35

TILES = 6
SUB = 8
WIDTH = 384
ROWS = 8
FIELD = (ROWS, TILES, SUB, WIDTH)
OWN = (4, TILES, SUB, WIDTH)
NEAR = 28
ZONES = 256
KS, AL, N, N1, M, MP, IC0, IN1, LEV0, LEV1, IKS, IAL = range(12)
F32 = jnp.float32


def device(x, z_hi, core, y, z_lo):
    return ((x * 2 + z_hi) * 2 + core) * 32 + y * 8 + z_lo


PLANES = [
    [device(x, z_hi, core, y, z_lo) for y in range(4) for x in range(4) for core in range(2)]
    for z_hi in range(2)
    for z_lo in range(8)
]
RINGS = [
    [device(x, z_hi, core, y, z_lo) for z_hi in range(2) for z_lo in range(8)]
    for x in range(4)
    for core in range(2)
    for y in range(4)
]


def lanes_left(x):
    return pltpu.roll(x, WIDTH - 1, 1)


def lanes_right(x):
    return pltpu.roll(x, 1, 1)


def subs_up(x):
    return pltpu.roll(x, SUB - 1, 0)


def subs_down(x):
    return pltpu.roll(x, 1, 0)


def iota(shape, dim):
    return lax.broadcasted_iota(jnp.int32, shape, dim)


def split3(x):
    hi = x.astype(jnp.bfloat16)
    rest = x - hi.astype(F32)
    mid = rest.astype(jnp.bfloat16)
    return hi, mid, (rest - mid.astype(F32)).astype(jnp.bfloat16)


def exact_dot(pick, x, dims=(((1,), (0,)), ((), ()))):
    parts = [lax.dot_general(pick, part, dims, preferred_element_type=F32) for part in split3(x)]
    return parts[0] + (parts[1] + parts[2])


def axes():
    event = lax.axis_index("event")
    return lax.axis_index("row"), event // 4 * 2 + event % 2, event // 2 % 2


def pack_kernel(head_in, zone_in, plan_in, h0, send_odd, send_even, zones, head, zone, plan, sems):
    copies = [
        pltpu.make_async_copy(src, dst, sems.at[i])
        for i, (src, dst) in enumerate(((head_in, head), (zone_in, zone), (plan_in, plan)))
    ]
    for copy in copies:
        copy.start()
    wide = (iota((192, WIDTH), 1) // 2 == iota((192, WIDTH), 0)).astype(F32)
    copies[1].wait()
    copies[2].wait()
    blocks = jnp.dot(zone[...].astype(F32), wide, preferred_element_type=F32)
    zones[...] = blocks
    level = plan[...].astype(F32)
    copies[0].wait()
    for depth in range(TILES * SUB):
        block = head[depth]
        j, s = depth % TILES, depth // TILES
        for row in range(4):
            h0[2 + row, j, s : s + 1, :] = block[row : row + 1, :]
    sub = iota((SUB, WIDTH), 0)
    odd = lax.axis_index("row") % 2 == 1

    def fill(out, pair):
        out[0:TILES] = h0[2 + 2 * pair]
        out[TILES : 2 * TILES] = h0[3 + 2 * pair]
        out[2 * TILES] = jnp.where(sub == 0, blocks[pair : pair + 1, :], level[0:1, pair : pair + 1])

    @pl.when(odd)
    def _():
        fill(send_odd, 1)
        fill(send_even, 0)

    @pl.when(jnp.logical_not(odd))
    def _():
        fill(send_odd, 0)
        fill(send_even, 1)


def cell_math(head, p, with_store=True):
    wet = jnp.log(-p[AL] * head)
    u = jnp.exp(p[N] * wet)
    d = 1.0 + u
    w = jnp.log(d)
    inv = 1.0 / d
    r = u * inv
    mw = p[M] * w
    q = jnp.exp(-0.5 * mw)
    f = jnp.exp(p[N1] * wet - mw)
    t = 1.0 - f
    kq = p[KS] * q * t
    half, twice = -0.5 * t, 2.0 * f
    e1 = p[MP] * w + p[M] * wet * r
    cond = kq * t
    cond_l = kq * p[N1] * (half * r - twice * inv)
    cond_n = kq * (half * e1 - twice * (wet - e1))
    if not with_store:
        return cond, cond_l, cond_n
    inv_store = d * p[IC0] / f
    store_l = p[N] - r * (2.0 * p[N] - 1.0)
    store_n = p[IN1] + wet - e1 - r * wet
    return cond, cond_l, cond_n, inv_store, store_l, store_n


def derived(sat, alpha, n):
    n1 = n - 1.0
    return (
        sat, alpha, n, n1, 1.0 - 1.0 / n, 1.0 / (n * n), 0.5 / (WATER_RANGE * n1 * alpha), 1.0 / n1,
    )


def row_params(prm, r):
    return [prm[r, i : i + 1, :] for i in range(8)]


def masks():
    last = iota((SUB, WIDTH), 1) == WIDTH - 1
    sub = iota((SUB, WIDTH), 0)
    return last, sub == 0, sub == SUB - 1


def net_row(h, k, r, top, beside, keep=None):
    last, is_top, is_bottom = masks()
    hs = [h[r, j] for j in range(TILES)]
    ks = [k[r, j] for j in range(TILES)]

    def face(j):
        if j < TILES - 1:
            kd = ks[j] + ks[j + 1]
            return kd, kd * (1.0 + hs[j] - hs[j + 1])
        kd = ks[j] + subs_up(ks[0])
        flow = kd * (1.0 + hs[j] - subs_up(hs[0]))
        return jnp.where(is_bottom, 2.0 * ks[j], kd), jnp.where(is_bottom, 2.0 * ks[j], flow)

    final = face(TILES - 1)
    above = (
        jnp.where(is_top, 2.0 * ks[0], subs_down(final[0])),
        jnp.where(is_top, top * ks[0], subs_down(final[1])),
    )
    for j in range(TILES):
        below = final if j == TILES - 1 else face(j)
        hj, kj = hs[j], ks[j]
        kf = jnp.where(last, 0.0, kj + lanes_left(kj))
        difference = jnp.where(last, 0.0, lanes_left(hj) - hj)
        if keep is not None:
            keep[0][r - 2, j], keep[1][r - 2, j] = kf, difference
        flow = kf * difference
        net = flow - lanes_right(flow) + above[1] - below[1]
        total = kf + lanes_right(kf) + above[0] + below[0]
        for other in beside:
            kx = k[other, j] + kj
            net = net + kx * (h[other, j] - hj)
            total = total + kx
        above = below
        yield j, net, total


def reach_row(h, phis, ic, psi, r, same, foreign, top):
    lane = iota((SUB, WIDTH), 1)
    even = lane % 2 == 0
    ends = jnp.logical_or(lane == 0, lane == WIDTH - 1)
    _, is_top, is_bottom = masks()

    def beside(x):
        left, right = lanes_right(x), lanes_left(x)
        return jnp.where(even, right, left), jnp.where(even, left, right)

    for j in range(TILES):
        hj, half = h[r, j], ic[r - 1, j]
        inner, outer = beside(hj)
        d_in = inner - hj
        d_out = jnp.where(ends, 0.0, outer - hj)
        h_below = h[r, j + 1] if j < TILES - 1 else subs_up(h[r, 0])
        h_above = h[r, j - 1] if j > 0 else subs_down(h[r, TILES - 1])
        d_below, d_above = h_below - hj - 1.0, 1.0 + h_above - hj
        self_below, self_above = d_below, d_above
        if j == TILES - 1:
            self_below, d_below = jnp.where(is_bottom, -2.0, d_below), jnp.where(is_bottom, 0.0, d_below)
        if j == 0:
            self_above, d_above = jnp.where(is_top, top, d_above), jnp.where(is_top, 0.0, d_above)
        d_same = h[same, j] - hj
        whole = d_in + d_out + self_below + self_above + d_same
        if foreign is not None:
            d_far = h[foreign, j] - hj
            whole = whole + d_far
        for i, phi in enumerate(phis):
            below = phi[r, j + 1] if j < TILES - 1 else subs_up(phi[r, 0])
            above = phi[r, j - 1] if j > 0 else subs_down(phi[r, TILES - 1])
            inner, outer = beside(phi[r, j])
            own = whole * phi[r, j] + d_in * inner + d_below * below + d_above * above + d_same * phi[same, j]
            psi[i][r - 1, j] = half * own
            psi[3 + i][r - 1, j] = (half * d_out) * outer
            if foreign is not None:
                psi[6 + i][r - 1, j] = (half * d_far) * phi[foreign, j]


def places(cell):
    line = jnp.floor((cell + 0.5) * (1.0 / WIDTH))
    column = cell - WIDTH * line
    depth = jnp.floor((line + 0.5) * 0.25)
    block = jnp.floor((depth + 0.5) * (1.0 / TILES))
    return (line - 4.0 * depth) * 48.0 + (depth - TILES * block) * 8.0 + block, column


def own_kernel(
    tab_k, tab_a, tab_n, plan, h0, zones, cells_at, goals,
    g1, *rest,
):
    psi, rest = rest[:9], rest[9:]
    prm, zrel, most_out, near, pick, put, column, goal, k1, kl1, kn1, ic1, p1, q1 = rest
    base = 8 * lax.axis_index("row") - 4
    sub = iota((SUB, WIDTH), 0)
    rel = (jnp.where(sub < 2, zones[0:1, :], zones[1:2, :]).astype(jnp.int32) - base) & (ZONES - 1)
    for r in range(4):
        zrel[2 + r : 3 + r, :] = rel[r : r + 1, :]
    sat = jnp.ones((SUB, WIDTH), F32)
    alpha, n = sat, 2.0 * sat
    lane = iota((SUB, 128), 1)
    line = iota((SUB, 128), 0)
    table = jnp.ones((SUB, 128), F32)
    for i in range(NEAR):
        at = (base + i) & (ZONES - 1)
        here = rel == i
        sat = jnp.where(here, tab_k[at], sat)
        alpha = jnp.where(here, tab_a[at], alpha)
        n = jnp.where(here, tab_n[at], n)
        entry = jnp.where(line == 0, tab_k[at], jnp.where(line == 1, tab_a[at], tab_n[at]))
        table = jnp.where(lane == i, entry, table)
    near[...] = table
    levels = [
        2.0 * IRRIGATION * jnp.where(sub < 2, plan[step, 0].astype(F32), plan[step, 1].astype(F32))
        for step in range(2)
    ]
    for i, value in enumerate(derived(sat, alpha, n) + (*levels, 1.0 / sat, 1.0 / alpha)):
        for r in range(4):
            prm[2 + r, i : i + 1, :] = value[r : r + 1, :]

    def cells(r, carry):
        p = row_params(prm, r)
        for j in range(TILES):
            values = cell_math(h0[r, j], p)
            k1[r, j], kl1[r, j], kn1[r, j], ic1[r - 1, j], p1[r - 1, j], q1[r - 1, j] = values
        return carry

    lax.fori_loop(2, 6, cells, 0)

    def flow(r, most):
        for j, net, total in net_row(h0, k1, r, prm[r, LEV0 : LEV0 + 1, :], (r - 1, r + 1)):
            ic = ic1[r - 1, j]
            g = net * ic
            g1[r - 1, j] = g
            p1[r - 1, j] = g * p1[r - 1, j]
            q1[r - 1, j] = g * q1[r - 1, j]
            most = jnp.maximum(most, total * ic)
        return most

    def edge_flow(i, carry):
        r = 2 + 3 * i
        for j, net, total in net_row(h0, k1, r, prm[r, LEV0 : LEV0 + 1, :], (3 + i,)):
            g1[r - 1, j] = net
            g1[5 * i, j] = total
            for at, value in enumerate((k1[r, j], kl1[r, j], kn1[r, j])):
                psi[at][5 * i, j] = value
            for at, value in enumerate((ic1[r - 1, j], p1[r - 1, j], q1[r - 1, j])):
                psi[3 + at][5 * i, j] = value
        return carry

    most_out[...] = lax.fori_loop(3, 5, flow, jnp.zeros((SUB, WIDTH), F32))
    lax.fori_loop(0, 2, edge_flow, 0)
    phis = (k1, kl1, kn1)

    def reach(i, carry):
        r = 3 + i
        reach_row(h0, phis, ic1, psi, r, 2 + 3 * i, 4 - i, prm[r, LEV0 : LEV0 + 1, :])
        for j in range(TILES):
            psi[1][r - 1, j] = psi[1][r - 1, j] - p1[r - 1, j]
            psi[2][r - 1, j] = psi[2][r - 1, j] - q1[r - 1, j]
        return carry

    def edge_reach(i, carry):
        r = 2 + 3 * i
        reach_row(h0, phis, ic1, psi, r, 3 + i, None, prm[r, LEV0 : LEV0 + 1, :])
        return carry

    lax.fori_loop(0, 2, reach, 0)
    lax.fori_loop(0, 2, edge_reach, 0)

    count = cells_at.shape[1]
    wide = jnp.where(iota((SUB, count), 0) == 0, cells_at[...].astype(F32), goals[...])
    tall = jnp.transpose(wide)
    line_wide = places(wide[0:1, :])[0].astype(jnp.int32)
    line_tall, column_tall = places(tall[:, 0:1])
    pick[...] = (iota((count, 192), 1) == line_tall.astype(jnp.int32)).astype(F32).astype(jnp.bfloat16)
    put[...] = (iota((192, count), 0) == line_wide).astype(F32).astype(jnp.bfloat16)
    column[...] = (iota((count, WIDTH), 1) == column_tall.astype(jnp.int32)).astype(F32).astype(jnp.bfloat16)
    goal[...] = jnp.broadcast_to(tall[:, 1:2], goal.shape)


def side_kernel(exchange, near, zones, most_in, got, *rest):
    h0, g1, *psi = rest[13:24]
    prm, zrel, result, k1, kl1, kn1, ic1, sl, sn, part, edge = rest[24:]
    position = lax.axis_index("row")
    side = position % 2 if exchange == "odd" else 1 - position % 2
    real = jnp.where(side == 0, position > 0, position < lax.axis_size("row") - 1)
    far, r, own = 7 * side, 1 + 5 * side, 2 + 3 * side
    for row in range(2):
        for j in range(TILES):
            h0[6 * side + row, j] = jnp.where(real, got[row * TILES + j], h0[own, j])
    part[...] = g1[5 * side]
    for at, phi in enumerate((k1, kl1, kn1)):
        phi[own] = psi[at][5 * side]
        edge[at] = psi[3 + at][5 * side]
    extra = got[2 * TILES]
    zone = jnp.where(real, extra[0:1, :], jnp.where(side == 0, zones[0:1, :], zones[1:2, :]))
    rel = (zone.astype(jnp.int32) - (8 * position - 4)) & (ZONES - 1)
    zrel[...] = jnp.where(iota((SUB, WIDTH), 0) // 2 == 3 * side, rel, zrel[...])
    here = (iota((32, WIDTH), 0) == rel).astype(F32).astype(jnp.bfloat16)
    parts = [jnp.dot(x, here, preferred_element_type=F32) for x in split3(near[:, :32])]
    values = parts[0] + (parts[1] + parts[2])
    sat, alpha, n = (values[i : i + 1, :] for i in range(3))
    level = 2.0 * IRRIGATION * extra[1:2, :]
    for i, value in enumerate(derived(sat, alpha, n) + (level, level, 1.0 / sat, 1.0 / alpha)):
        for row in range(2):
            prm[6 * side + row, i : i + 1, :] = value

    p = row_params(prm, far)
    for j in range(TILES):
        k1[far, j], kl1[far, j], kn1[far, j] = cell_math(h0[far, j], p, False)
        cond, kl1[r, j], kn1[r, j], ic1[r - 1, j], sl[j], sn[j] = cell_math(h0[r, j], p)
        k1[r, j] = jnp.where(real, cond, -k1[own, j])

    phis = (k1, kl1, kn1)
    most = most_in[...]
    reach_row(h0, phis, ic1, psi, r, far, own, prm[r, LEV0 : LEV0 + 1, :])
    for j, net, _ in net_row(h0, k1, r, prm[r, LEV0 : LEV0 + 1, :], (far, own)):
        g = jnp.where(real, net * ic1[r - 1, j], 0.0)
        g1[r - 1, j] = g
        psi[1][r - 1, j] = psi[1][r - 1, j] - g * sl[j]
        psi[2][r - 1, j] = psi[2][r - 1, j] - g * sn[j]
        kx = k1[r, j] + k1[own, j]
        ic = edge[0, j]
        d = h0[r, j] - h0[own, j]
        g = (g1[own - 1, j] + kx * d) * ic
        g1[own - 1, j] = g
        d = d * ic
        psi[0][own - 1, j] = psi[0][own - 1, j] + d * k1[own, j]
        psi[1][own - 1, j] = psi[1][own - 1, j] + d * kl1[own, j] - g * edge[1, j]
        psi[2][own - 1, j] = psi[2][own - 1, j] + d * kn1[own, j] - g * edge[2, j]
        for q, phi in enumerate(phis):
            psi[6 + q][own - 1, j] = d * phi[r, j]
        most = jnp.maximum(most, (part[j] + kx) * ic)
    if exchange == "odd":
        result[...] = most
    else:
        most = jnp.maximum(jnp.maximum(most[:, :128], most[:, 128:256]), most[:, 256:])
        most = jnp.max(most, 0, keepdims=True)
        result[...] = jnp.broadcast_to(most[None], result.shape)


def second_kernel(rates, pick, put, column_in, goal, h0, g1, *rest):
    psi, rest = rest[:9], rest[9:]
    prm, zrel, h1_out, g2, spread, *rest = rest
    h1, k2, kl2, kn2, ic2, sl2, sn2, va, vb, kfs, dfs, wa, wb, u0, u1, u2, maps, maps_f, maps_g = rest
    position = lax.axis_index("row")
    size = CFL / jnp.max(rates[...])
    nothing = jnp.zeros((TILES, SUB, WIDTH), F32)
    for r in (1, 6):
        for ref in (wa, wb):
            ref[r] = nothing

    def cells(r, carry):
        p = row_params(prm, r)
        for j in range(TILES):
            head = h0[r, j] + size * g1[r - 1, j]
            h1[r, j] = head
            h1_out[r - 2, j] = head
            values = cell_math(head, p)
            k2[r, j], kl2[r, j], kn2[r, j], ic2[r - 2, j], sl2[r - 2, j], sn2[r - 2, j] = values
        return carry

    def edge_cells(i, carry):
        r = 1 + 5 * i
        p = row_params(prm, r)
        own = 2 + 3 * i
        real = jnp.where(i == 0, position > 0, position < lax.axis_size("row") - 1)
        for j in range(TILES):
            head = jnp.where(real, h0[r, j] + size * g1[r - 1, j], h1[own, j])
            h1[r, j] = head
            cond, kl2[r, j], kn2[r, j] = cell_math(head, p, False)
            k2[r, j] = jnp.where(real, cond, -k2[own, j])
        return carry

    lax.fori_loop(2, 6, cells, 0)
    lax.fori_loop(0, 2, edge_cells, 0)

    def flow(r, most):
        for j, net, total in net_row(h1, k2, r, prm[r, LEV1 : LEV1 + 1, :], (r - 1, r + 1), (kfs, dfs)):
            ic = ic2[r - 2, j]
            g2[r - 2, j] = net * ic
            most = jnp.maximum(most, total * ic)
        return most

    most = jnp.max(lax.fori_loop(2, 6, flow, jnp.zeros((SUB, WIDTH), F32)))

    column = column_in[...].astype(F32)
    field_g = g2[...].reshape(192, WIDTH)
    field_h = h1_out[...].reshape(192, WIDTH) + size * field_g
    seen_h = jnp.sum(column * exact_dot(pick[...], field_h), 1, keepdims=True)
    seen_g = jnp.sum(column * exact_dot(pick[...], field_g), 1, keepdims=True)
    diff = seen_h - goal[:, 0:1]
    events = 16.0
    loss = (
        jnp.sum(diff * diff) * (0.5 / events),
        jnp.sum(diff * seen_g) * (1.0 / events),
        jnp.sum(seen_g * seen_g) * (0.5 / events),
    )
    va[...] = exact_dot(put[...], column * (diff * (1.0 / events))).reshape(OWN)
    vb[...] = exact_dot(put[...], column * (seen_g * (1.0 / events))).reshape(OWN)

    def scaled(r, carry):
        for j in range(TILES):
            ic = ic2[r - 2, j]
            wa[r, j] = va[r - 2, j] * ic
            wb[r, j] = vb[r - 2, j] * ic
        return carry

    lax.fori_loop(2, 6, scaled, 0)
    _, is_top, is_bottom = masks()

    def store_two(r, sums):
        flat = [jnp.sum(x, 0, keepdims=True) for x in sums]
        for q in range(3):
            of_a, of_b = flat[q], flat[3 + q]
            for c, row in enumerate((size * of_a, of_a + size * of_b, of_b)):
                maps[r - 1, 4 * q + c : 4 * q + c + 1, :] = row

    def store_heads(r, j, back):
        (v_a, j_a), (v_b, j_b) = back
        u0[r - 1, j] = v_a + size * j_a
        u1[r - 1, j] = v_b + j_a + size * j_b
        u2[r - 1, j] = j_b

    def edge_two(i, carry):
        r = 1 + 5 * i
        near = 2 + 3 * i
        sums = [jnp.zeros((SUB, WIDTH), F32) for _ in range(6)]
        for j in range(TILES):
            hj = h1[r, j]
            half = h1[near, j] - hj
            kd = k2[near, j] + k2[r, j]
            kj, kl, kn = k2[r, j], kl2[r, j], kn2[r, j]
            inv_h = 1.0 / hj
            back = []
            for part, w_ref in enumerate((wa, wb)):
                w = w_ref[near, j]
                gk, gh = -half * w, kd * w
                to_l = gk * kl
                sums[3 * part] += gk * kj
                sums[3 * part + 1] += to_l
                sums[3 * part + 2] += gk * kn
                back.append((0.0, gh + to_l * inv_h))
            store_heads(r, j, back)
        store_two(r, sums)
        return carry

    def back_two(r, carry):
        top = prm[r, LEV1 : LEV1 + 1, :]
        hs = [h1[r, j] for j in range(TILES)]
        ks = [k2[r, j] for j in range(TILES)]
        sums = [jnp.zeros((SUB, WIDTH), F32) for _ in range(6)]
        ws = [[w[r, j] for j in range(TILES)] for w in (wa, wb)]

        def face(j):
            if j < TILES - 1:
                half = 1.0 + hs[j] - hs[j + 1]
                kd = ks[j] + ks[j + 1]
                out = []
                for w in ws:
                    dw = w[j + 1] - w[j]
                    out.append((half * dw, kd * dw))
                return out
            half = 1.0 + hs[j] - subs_up(hs[0])
            kd = ks[j] + subs_up(ks[0])
            out = []
            for w in ws:
                dw = subs_up(w[0]) - w[j]
                out.append((jnp.where(is_bottom, -2.0 * w[j], half * dw), jnp.where(is_bottom, 0.0, kd * dw)))
            return out

        final = face(TILES - 1)
        above = [
            (jnp.where(is_top, top * w[0], subs_down(f[0])), subs_down(f[1]))
            for w, f in zip(ws, final)
        ]
        for j in range(TILES):
            below = final if j == TILES - 1 else face(j)
            hj, kj = hs[j], ks[j]
            kf, half_c = kfs[r - 2, j], dfs[r - 2, j]
            half_l, half_h = h1[r - 1, j] - hj, h1[r + 1, j] - hj
            k_low, k_high = k2[r - 1, j] + kj, k2[r + 1, j] + kj
            kl, kn = kl2[r, j], kn2[r, j]
            inv_h = 1.0 / hj
            g = g2[r - 2, j]
            gl, gn = g * sl2[r - 2, j], g * sn2[r - 2, j]
            back = []
            for part, (w_ref, v_ref) in enumerate(((wa, va), (wb, vb))):
                w = ws[part][j]
                dw = w - lanes_left(w)
                e, f = half_c * dw, kf * dw
                d_low, d_high = w - w_ref[r - 1, j], w - w_ref[r + 1, j]
                gk = e + lanes_right(e) + below[part][0] + above[part][0]
                gk = gk + half_l * d_low + half_h * d_high
                gh = lanes_right(f) - f + below[part][1] - above[part][1]
                gh = gh - k_low * d_low - k_high * d_high
                v = v_ref[r - 2, j]
                to_l = gk * kl - v * gl
                sums[3 * part] += gk * kj
                sums[3 * part + 1] += to_l
                sums[3 * part + 2] += gk * kn - v * gn
                back.append((v, gh + (to_l + v * g) * inv_h))
            store_heads(r, j, back)
            above = below
        store_two(r, sums)
        return carry

    lax.fori_loop(0, 2, edge_two, 0)
    lax.fori_loop(2, 6, back_two, 0)

    for ref in (maps, maps_f, maps_g):
        for r in range(6):
            for at in (3, 7, 11):
                ref[r, at : at + 1, :] = jnp.zeros((1, WIDTH), F32)
            ref[r, 12:16, :] = jnp.zeros((4, WIDTH), F32)

    def first_part(r, carry):
        for q in range(3):
            sums = [[jnp.zeros((SUB, WIDTH), F32) for _ in range(3)] for _ in range(3)]
            for j in range(TILES):
                us = [ref[r, j] for ref in (u0, u1, u2)]
                for kind in range(3):
                    factor = psi[3 * kind + q][r, j]
                    for c in range(3):
                        sums[kind][c] += us[c] * factor
            for c in range(3):
                at = 4 * q + c
                own, column_off, row_off = (jnp.sum(sums[kind][c], 0, keepdims=True) for kind in range(3))
                maps[r, at : at + 1, :] = maps[r, at : at + 1, :] + size * own
                maps_f[r, at : at + 1, :] = size * column_off
                maps_g[r, at : at + 1, :] = size * row_off
        return carry

    lax.fori_loop(0, 6, first_part, 0)

    odd = iota((16, WIDTH), 1) % 2 == 1
    which = iota((16, WIDTH), 0)
    pieces = []
    for r in range(6):
        off = maps_f[r]
        off = jnp.where(odd, lanes_left(off), lanes_right(off))
        other = r + 1 if r % 2 == 0 else r - 1
        scale = jnp.where(which < 4, prm[r + 1, IKS : IKS + 1, :], jnp.where(which < 8, prm[r + 1, IAL : IAL + 1, :], 1.0))
        pieces.append((maps[r] + off + maps_g[other]) * scale)
    left = jnp.concatenate(pieces, 1)
    near = zrel[...]
    zone_id = iota((32, WIDTH), 0)
    onehot = jnp.concatenate([(zone_id == near[r : r + 1, :]).astype(F32) for r in range(1, 7)], 1)
    onehot = onehot.astype(jnp.bfloat16)
    nt = (((1,), (1,)), ((), ()))
    parts = [lax.dot_general(part, onehot, nt, preferred_element_type=F32) for part in split3(left)]
    by_zone = parts[0] + (parts[1] + parts[2])
    fields = [by_zone[4 * q : 4 * q + 4, :] for q in range(3)]
    sub4 = iota((4, 32), 0)
    fields.append(jnp.where(sub4 == 0, loss[0], jnp.where(sub4 == 1, loss[1], loss[2])))
    sums = jnp.concatenate(fields, 1)
    state = jnp.where(iota((4, 128), 1) < 64, most, size)
    payload = jnp.where(iota((4, 128), 0) == 3, state, sums)
    spread[...] = jnp.broadcast_to(payload[None], spread.shape)


def ring_kernel(parts, spread):
    lane = iota((SUB, 256), 1)
    total = jnp.zeros((SUB, 256), F32)
    blank = jnp.zeros((SUB, 128), F32)
    most = None
    loss = jnp.zeros((SUB, 256), F32)
    for z in range(8):
        tile = jnp.concatenate([parts[z], parts[8 + z]], 0)
        most = tile if most is None else jnp.maximum(most, tile)
        tile = jnp.concatenate([tile, blank], 1)
        for q in range(3):
            start = 84 * q + 8 * z
            moved = pltpu.roll(tile, (start - 32 * q) % 256, 1)
            total = total + jnp.where(jnp.logical_and(lane >= start, lane < start + NEAR), moved, 0.0)
        loss = loss + tile
    total = jnp.where(lane == 252, pltpu.roll(loss, 252 - 96, 1), total)
    rows = []
    one = iota((1, 256), 1)
    for z_hi in range(2):
        state = most[4 * z_hi + 3 : 4 * z_hi + 4, :]
        for power in range(3):
            row = total[4 * z_hi + power : 4 * z_hi + power + 1, :]
            row = jnp.where(one == 253, state[:, 0:1], row)
            rows.append(jnp.where(one == 254, state[:, 64:65], row))
    rows = jnp.concatenate(rows, 1)
    spread[...] = jnp.broadcast_to(rows[None], spread.shape)


def last_kernel(parts, h1, g2, final, grad_k, grad_a, grad_n, misfit, rates):
    sums = [jnp.zeros((1, 256), F32) for _ in range(4)]
    for pair in range(8):
        tiles = [parts[8 * y + pair] for y in range(4)]
        for z_hi in range(2):
            powers = [[tile[:, 256 * (3 * z_hi + i) : 256 * (3 * z_hi + i + 1)] for i in range(3)] for tile in tiles]
            first = [part[0] for part in powers]
            most = jnp.maximum(jnp.maximum(first[0], first[1]), jnp.maximum(first[2], first[3]))
            step = CFL / most[:, 253:254]
            rates[2 * pair + z_hi] = jnp.broadcast_to(step, (1, 128))
            move = step - first[0][:, 254:255]
            for y in range(4):
                a, b, c = powers[y]
                sums[y] = sums[y] + (a + move * (b + move * c))
    lane = iota((1, 256), 1)
    rows = sums
    for q, out in enumerate((grad_k, grad_a, grad_n)):
        total = jnp.zeros((1, 256), F32)
        for y in range(4):
            field = rows[y] if q == 0 else pltpu.roll(rows[y], 256 - 84 * q, 1)
            total = total + pltpu.roll(jnp.where(lane < 84, field, 0.0), (64 * y - 4) % 256, 1)
        out[...] = total
    misfit[0, 0] = jnp.sum(jnp.where(lane == 252, rows[0] + rows[1] + rows[2] + rows[3], 0.0))
    _, pair, z_hi = axes()
    size = rates[2 * pair + z_hi]
    size = jnp.concatenate([size, size, size], 1)
    for j in range(TILES):
        for row in range(4):
            tile = h1[row, j] + size * g2[row, j]
            for s in range(SUB):
                final[TILES * s + j, row : row + 1, :] = tile[s : s + 1, :]


VMEM = pl.BlockSpec(memory_space=pltpu.VMEM)
SMEM = pl.BlockSpec(memory_space=pltpu.SMEM)


def call(kernel, name, ins, outs, out_specs=None, scratch=(), cost=None, in_place=None, room=8):
    return pl.pallas_call(
        kernel,
        name=name,
        in_specs=ins,
        out_specs=out_specs or [VMEM] * len(outs),
        out_shape=[jax.ShapeDtypeStruct(shape, dtype) for shape, dtype in outs],
        scratch_shapes=scratch,
        cost_estimate=cost,
        input_output_aliases=in_place or {},
        compiler_params=pltpu.CompilerParams(vmem_limit_bytes=room * 1024 * 1024),
    )


def local(
    initial_head,
    sat_conductivity,
    vg_alpha,
    vg_n,
    zone_map,
    forcing_plan,
    tensiometer_cells,
    tensiometer_heads,
):
    count = lax.axis_size("row")
    plan = forcing_plan[0]
    edge = (2 * TILES + 1, SUB, WIDTH)
    h0, send_odd, send_even, zones = call(
        pack_kernel,
        "pack_edges",
        [pl.BlockSpec(memory_space=pltpu.HBM)] * 3,
        [(FIELD, F32), (edge, F32), (edge, F32), ((2, WIDTH), F32)],
        scratch=[
            pltpu.VMEM((48, 4, WIDTH), F32),
            pltpu.VMEM((2, 192), jnp.int32),
            pltpu.VMEM((2, 2), jnp.int32),
            pltpu.SemaphoreType.DMA((3,)),
        ],
    )(initial_head[0], zone_map, plan)
    odd = [(i, i + 1) for i in range(1, count - 1, 2)]
    even = [(i, i + 1) for i in range(0, count, 2)]
    got_odd = lax.ppermute(send_odd, "row", odd + [(j, i) for i, j in odd])
    got_even = lax.ppermute(send_even, "row", even + [(j, i) for i, j in even])
    wide = (6, TILES, SUB, WIDTH)
    fields = [(wide, F32)] * 10 + [((ROWS, 16, WIDTH), F32), ((ROWS, WIDTH), jnp.int32)]
    whole = [pltpu.VMEM(FIELD, F32)] * 3 + [pltpu.VMEM(wide, F32)]
    seen = tensiometer_cells.shape[1]
    own = call(
        own_kernel,
        "own_cells",
        [SMEM] * 4 + [VMEM] * 4,
        fields
        + [((SUB, WIDTH), F32), ((SUB, 128), F32)]
        + [((seen, 192), jnp.bfloat16), ((192, seen), jnp.bfloat16), ((seen, WIDTH), jnp.bfloat16), ((seen, 128), F32)],
        scratch=whole + [pltpu.VMEM(wide, F32)] * 2,
        cost=pl.CostEstimate(flops=200_000_000, bytes_accessed=8_000_000, transcendentals=600_000),
    )(sat_conductivity, vg_alpha, vg_n, plan, h0, zones, tensiometer_cells, tensiometer_heads)
    held, (most, near), sensors = (h0, *own[:12]), own[12:14], own[14:]
    row = (TILES, SUB, WIDTH)
    for exchange, got, result in (("odd", got_odd, (SUB, WIDTH)), ("even", got_even, (32, 1, 128))):
        *held, most = call(
            functools.partial(side_kernel, exchange),
            "first_step_" + exchange,
            [VMEM] * 17,
            [(FIELD, F32)] + fields + [(result, F32)],
            scratch=whole + [pltpu.VMEM(row, F32)] * 3 + [pltpu.VMEM((3, *row), F32)],
            in_place={4 + i: i for i in range(13)},
        )(near, zones, most, got, *held)
    fields, rates = held, most
    rates = lax.all_to_all(rates, "row", 0, 0, tiled=True)
    h1, g2, sums = call(
        second_kernel,
        "second_step_and_adjoint",
        [VMEM] * 18,
        [(OWN, F32), (OWN, F32), ((16, 4, 128), F32)],
        scratch=[pltpu.VMEM(FIELD, F32)] * 4
        + [pltpu.VMEM(OWN, F32)] * 7
        + [pltpu.VMEM(FIELD, F32)] * 2
        + [pltpu.VMEM(wide, F32)] * 3
        + [pltpu.VMEM((6, 16, WIDTH), F32)] * 3,
        room=20,
    )(rates, *sensors, *fields)
    sums = lax.all_to_all(sums, ("event", "row"), 0, 0, tiled=True, axis_index_groups=RINGS)
    (sums,) = call(ring_kernel, "ring_sums", [VMEM], [((32, 1, 6 * 256), F32)])(sums)
    sums = lax.all_to_all(sums, ("event", "row"), 0, 0, tiled=True, axis_index_groups=PLANES)
    row = ((1, ZONES), F32)
    final, grad_k, grad_a, grad_n, misfit = call(
        last_kernel,
        "final_head_and_sums",
        [VMEM, VMEM, VMEM],
        [((48, 4, WIDTH), F32), row, row, row, ((1, 1), F32)],
        [VMEM] * 4 + [SMEM],
        scratch=[pltpu.VMEM((16, 1, 128), F32)],
    )(sums, h1, g2)
    return (final[None], misfit[0, 0], grad_k[0], grad_a[0], grad_n[0])


def solution(mesh):
    return jax.shard_map(
        local,
        mesh=mesh,
        in_specs=(
            P("event", None, "row", None),
            P(),
            P(),
            P(),
            P("row", None),
            P("event", None, "row"),
            P("event", "row"),
            P("event", "row"),
        ),
        out_specs=(P("event", None, "row", None), P(), P(), P(), P()),
        check_vma=False,
    )
```

```python
import functools

import jax
import jax.numpy as jnp
from jax import lax
from jax.experimental import pallas as pl
from jax.experimental.pallas import tpu as pltpu
from jax.sharding import PartitionSpec as P

CFL = 0.4
IRRIGATION = 0.2
WATER_RANGE = 0.35

TILES = 6
SUB = 8
WIDTH = 384
ROWS = 8
FIELD = (ROWS, TILES, SUB, WIDTH)
OWN = (4, TILES, SUB, WIDTH)
NEAR = 28
ZONES = 256
KS, AL, N, N1, M, MP, IC0, IN1, LEV0, LEV1, IKS, IAL = range(12)
F32 = jnp.float32


def device(x, z_hi, core, y, z_lo):
    return ((x * 2 + z_hi) * 2 + core) * 32 + y * 8 + z_lo


PLANES = [
    [device(x, z_hi, core, y, z_lo) for y in range(4) for x in range(4) for core in range(2)]
    for z_hi in range(2)
    for z_lo in range(8)
]
RINGS = [
    [device(x, z_hi, core, y, z_lo) for z_hi in range(2) for z_lo in range(8)]
    for x in range(4)
    for core in range(2)
    for y in range(4)
]


def lanes_left(x):
    return pltpu.roll(x, WIDTH - 1, 1)


def lanes_right(x):
    return pltpu.roll(x, 1, 1)


def subs_up(x):
    return pltpu.roll(x, SUB - 1, 0)


def subs_down(x):
    return pltpu.roll(x, 1, 0)


def iota(shape, dim):
    return lax.broadcasted_iota(jnp.int32, shape, dim)


def split3(x):
    hi = x.astype(jnp.bfloat16)
    rest = x - hi.astype(F32)
    mid = rest.astype(jnp.bfloat16)
    return hi, mid, (rest - mid.astype(F32)).astype(jnp.bfloat16)


def exact_dot(pick, x, dims=(((1,), (0,)), ((), ()))):
    parts = [lax.dot_general(pick, part, dims, preferred_element_type=F32) for part in split3(x)]
    return parts[0] + (parts[1] + parts[2])


def axes():
    event = lax.axis_index("event")
    return lax.axis_index("row"), event // 4 * 2 + event % 2, event // 2 % 2


def pack_kernel(head_in, zone_in, plan_in, h0, send_odd, send_even, zones, head, zone, plan, sems):
    copies = [
        pltpu.make_async_copy(src, dst, sems.at[i])
        for i, (src, dst) in enumerate(((head_in, head), (zone_in, zone), (plan_in, plan)))
    ]
    for copy in copies:
        copy.start()
    wide = (iota((192, WIDTH), 1) // 2 == iota((192, WIDTH), 0)).astype(F32)
    copies[1].wait()
    copies[2].wait()
    blocks = jnp.dot(zone[...].astype(F32), wide, preferred_element_type=F32)
    zones[...] = blocks
    level = plan[...].astype(F32)
    copies[0].wait()
    for depth in range(TILES * SUB):
        block = head[depth]
        j, s = depth % TILES, depth // TILES
        for row in range(4):
            h0[2 + row, j, s : s + 1, :] = block[row : row + 1, :]
    sub = iota((SUB, WIDTH), 0)
    odd = lax.axis_index("row") % 2 == 1

    def fill(out, pair):
        out[0:TILES] = h0[2 + 2 * pair]
        out[TILES : 2 * TILES] = h0[3 + 2 * pair]
        out[2 * TILES] = jnp.where(sub == 0, blocks[pair : pair + 1, :], level[0:1, pair : pair + 1])

    @pl.when(odd)
    def _():
        fill(send_odd, 1)
        fill(send_even, 0)

    @pl.when(jnp.logical_not(odd))
    def _():
        fill(send_odd, 0)
        fill(send_even, 1)


def cell_math(head, p, with_store=True):
    wet = jnp.log(-p[AL] * head)
    u = jnp.exp(p[N] * wet)
    d = 1.0 + u
    w = jnp.log(d)
    inv = 1.0 / d
    r = u * inv
    mw = p[M] * w
    q = jnp.exp(-0.5 * mw)
    f = jnp.exp(p[N1] * wet - mw)
    t = 1.0 - f
    kq = p[KS] * q * t
    half, twice = -0.5 * t, 2.0 * f
    e1 = p[MP] * w + p[M] * wet * r
    cond = kq * t
    cond_l = kq * p[N1] * (half * r - twice * inv)
    cond_n = kq * (half * e1 - twice * (wet - e1))
    if not with_store:
        return cond, cond_l, cond_n
    inv_store = d * p[IC0] / f
    store_l = p[N] - r * (2.0 * p[N] - 1.0)
    store_n = p[IN1] + wet - e1 - r * wet
    return cond, cond_l, cond_n, inv_store, store_l, store_n


def derived(sat, alpha, n):
    n1 = n - 1.0
    return (
        sat, alpha, n, n1, 1.0 - 1.0 / n, 1.0 / (n * n), 0.5 / (WATER_RANGE * n1 * alpha), 1.0 / n1,
    )


def row_params(prm, r):
    return [prm[r, i : i + 1, :] for i in range(8)]


def masks():
    last = iota((SUB, WIDTH), 1) == WIDTH - 1
    sub = iota((SUB, WIDTH), 0)
    return last, sub == 0, sub == SUB - 1


def net_row(h, k, r, top, beside, keep=None):
    last, is_top, is_bottom = masks()
    hs = [h[r, j] for j in range(TILES)]
    ks = [k[r, j] for j in range(TILES)]

    def face(j):
        if j < TILES - 1:
            kd = ks[j] + ks[j + 1]
            return kd, kd * (1.0 + hs[j] - hs[j + 1])
        kd = ks[j] + subs_up(ks[0])
        flow = kd * (1.0 + hs[j] - subs_up(hs[0]))
        return jnp.where(is_bottom, 2.0 * ks[j], kd), jnp.where(is_bottom, 2.0 * ks[j], flow)

    final = face(TILES - 1)
    above = (
        jnp.where(is_top, 2.0 * ks[0], subs_down(final[0])),
        jnp.where(is_top, top * ks[0], subs_down(final[1])),
    )
    for j in range(TILES):
        below = final if j == TILES - 1 else face(j)
        hj, kj = hs[j], ks[j]
        kf = jnp.where(last, 0.0, kj + lanes_left(kj))
        difference = jnp.where(last, 0.0, lanes_left(hj) - hj)
        if keep is not None:
            keep[0][r - 2, j], keep[1][r - 2, j] = kf, difference
        flow = kf * difference
        net = flow - lanes_right(flow) + above[1] - below[1]
        total = kf + lanes_right(kf) + above[0] + below[0]
        for other in beside:
            kx = k[other, j] + kj
            net = net + kx * (h[other, j] - hj)
            total = total + kx
        above = below
        yield j, net, total


def reach_row(h, phis, ic, psi, r, same, foreign, top):
    lane = iota((SUB, WIDTH), 1)
    even = lane % 2 == 0
    ends = jnp.logical_or(lane == 0, lane == WIDTH - 1)
    _, is_top, is_bottom = masks()

    def beside(x):
        left, right = lanes_right(x), lanes_left(x)
        return jnp.where(even, right, left), jnp.where(even, left, right)

    for j in range(TILES):
        hj, half = h[r, j], ic[r - 1, j]
        inner, outer = beside(hj)
        d_in = inner - hj
        d_out = jnp.where(ends, 0.0, outer - hj)
        h_below = h[r, j + 1] if j < TILES - 1 else subs_up(h[r, 0])
        h_above = h[r, j - 1] if j > 0 else subs_down(h[r, TILES - 1])
        d_below, d_above = h_below - hj - 1.0, 1.0 + h_above - hj
        self_below, self_above = d_below, d_above
        if j == TILES - 1:
            self_below, d_below = jnp.where(is_bottom, -2.0, d_below), jnp.where(is_bottom, 0.0, d_below)
        if j == 0:
            self_above, d_above = jnp.where(is_top, top, d_above), jnp.where(is_top, 0.0, d_above)
        d_same = h[same, j] - hj
        whole = d_in + d_out + self_below + self_above + d_same
        if foreign is not None:
            d_far = h[foreign, j] - hj
            whole = whole + d_far
        for i, phi in enumerate(phis):
            below = phi[r, j + 1] if j < TILES - 1 else subs_up(phi[r, 0])
            above = phi[r, j - 1] if j > 0 else subs_down(phi[r, TILES - 1])
            inner, outer = beside(phi[r, j])
            own = whole * phi[r, j] + d_in * inner + d_below * below + d_above * above + d_same * phi[same, j]
            psi[i][r - 1, j] = half * own
            psi[3 + i][r - 1, j] = (half * d_out) * outer
            if foreign is not None:
                psi[6 + i][r - 1, j] = (half * d_far) * phi[foreign, j]


def places(cell):
    line = jnp.floor((cell + 0.5) * (1.0 / WIDTH))
    column = cell - WIDTH * line
    depth = jnp.floor((line + 0.5) * 0.25)
    block = jnp.floor((depth + 0.5) * (1.0 / TILES))
    return (line - 4.0 * depth) * 48.0 + (depth - TILES * block) * 8.0 + block, column


def own_kernel(
    tab_k, tab_a, tab_n, plan, h0, zones, cells_at, goals,
    g1, *rest,
):
    psi, rest = rest[:9], rest[9:]
    prm, zrel, most_out, near, pick, put, column, goal, k1, kl1, kn1, ic1, p1, q1 = rest
    base = 8 * lax.axis_index("row") - 4
    sub = iota((SUB, WIDTH), 0)
    rel = (jnp.where(sub < 2, zones[0:1, :], zones[1:2, :]).astype(jnp.int32) - base) & (ZONES - 1)
    for r in range(4):
        zrel[2 + r : 3 + r, :] = rel[r : r + 1, :]
    sat = jnp.ones((SUB, WIDTH), F32)
    alpha, n = sat, 2.0 * sat
    lane = iota((SUB, 128), 1)
    line = iota((SUB, 128), 0)
    table = jnp.ones((SUB, 128), F32)
    for i in range(NEAR):
        at = (base + i) & (ZONES - 1)
        here = rel == i
        sat = jnp.where(here, tab_k[at], sat)
        alpha = jnp.where(here, tab_a[at], alpha)
        n = jnp.where(here, tab_n[at], n)
        entry = jnp.where(line == 0, tab_k[at], jnp.where(line == 1, tab_a[at], tab_n[at]))
        table = jnp.where(lane == i, entry, table)
    near[...] = table
    levels = [
        2.0 * IRRIGATION * jnp.where(sub < 2, plan[step, 0].astype(F32), plan[step, 1].astype(F32))
        for step in range(2)
    ]
    for i, value in enumerate(derived(sat, alpha, n) + (*levels, 1.0 / sat, 1.0 / alpha)):
        for r in range(4):
            prm[2 + r, i : i + 1, :] = value[r : r + 1, :]

    def cells(r, carry):
        p = row_params(prm, r)
        for j in range(TILES):
            values = cell_math(h0[r, j], p)
            k1[r, j], kl1[r, j], kn1[r, j], ic1[r - 1, j], p1[r - 1, j], q1[r - 1, j] = values
        return carry

    lax.fori_loop(2, 6, cells, 0)

    def flow(r, most):
        for j, net, total in net_row(h0, k1, r, prm[r, LEV0 : LEV0 + 1, :], (r - 1, r + 1)):
            ic = ic1[r - 1, j]
            g = net * ic
            g1[r - 1, j] = g
            p1[r - 1, j] = g * p1[r - 1, j]
            q1[r - 1, j] = g * q1[r - 1, j]
            most = jnp.maximum(most, total * ic)
        return most

    def edge_flow(i, carry):
        r = 2 + 3 * i
        for j, net, total in net_row(h0, k1, r, prm[r, LEV0 : LEV0 + 1, :], (3 + i,)):
            g1[r - 1, j] = net
            g1[5 * i, j] = total
            for at, value in enumerate((k1[r, j], kl1[r, j], kn1[r, j])):
                psi[at][5 * i, j] = value
            for at, value in enumerate((ic1[r - 1, j], p1[r - 1, j], q1[r - 1, j])):
                psi[3 + at][5 * i, j] = value
        return carry

    most_out[...] = lax.fori_loop(3, 5, flow, jnp.zeros((SUB, WIDTH), F32))
    lax.fori_loop(0, 2, edge_flow, 0)
    phis = (k1, kl1, kn1)

    def reach(i, carry):
        r = 3 + i
        reach_row(h0, phis, ic1, psi, r, 2 + 3 * i, 4 - i, prm[r, LEV0 : LEV0 + 1, :])
        for j in range(TILES):
            psi[1][r - 1, j] = psi[1][r - 1, j] - p1[r - 1, j]
            psi[2][r - 1, j] = psi[2][r - 1, j] - q1[r - 1, j]
        return carry

    def edge_reach(i, carry):
        r = 2 + 3 * i
        reach_row(h0, phis, ic1, psi, r, 3 + i, None, prm[r, LEV0 : LEV0 + 1, :])
        return carry

    lax.fori_loop(0, 2, reach, 0)
    lax.fori_loop(0, 2, edge_reach, 0)

    count = cells_at.shape[1]
    wide = jnp.where(iota((SUB, count), 0) == 0, cells_at[...].astype(F32), goals[...])
    tall = jnp.transpose(wide)
    line_wide = places(wide[0:1, :])[0].astype(jnp.int32)
    line_tall, column_tall = places(tall[:, 0:1])
    pick[...] = (iota((count, 192), 1) == line_tall.astype(jnp.int32)).astype(F32).astype(jnp.bfloat16)
    put[...] = (iota((192, count), 0) == line_wide).astype(F32).astype(jnp.bfloat16)
    column[...] = (iota((count, WIDTH), 1) == column_tall.astype(jnp.int32)).astype(F32).astype(jnp.bfloat16)
    goal[...] = jnp.broadcast_to(tall[:, 1:2], goal.shape)


def side_kernel(exchange, near, zones, most_in, got, *rest):
    h0, g1, *psi = rest[13:24]
    prm, zrel, result, k1, kl1, kn1, ic1, sl, sn, part, edge = rest[24:]
    position = lax.axis_index("row")
    side = position % 2 if exchange == "odd" else 1 - position % 2
    real = jnp.where(side == 0, position > 0, position < lax.axis_size("row") - 1)
    far, r, own = 7 * side, 1 + 5 * side, 2 + 3 * side
    for row in range(2):
        for j in range(TILES):
            h0[6 * side + row, j] = jnp.where(real, got[row * TILES + j], h0[own, j])
    part[...] = g1[5 * side]
    for at, phi in enumerate((k1, kl1, kn1)):
        phi[own] = psi[at][5 * side]
        edge[at] = psi[3 + at][5 * side]
    extra = got[2 * TILES]
    zone = jnp.where(real, extra[0:1, :], jnp.where(side == 0, zones[0:1, :], zones[1:2, :]))
    rel = (zone.astype(jnp.int32) - (8 * position - 4)) & (ZONES - 1)
    zrel[...] = jnp.where(iota((SUB, WIDTH), 0) // 2 == 3 * side, rel, zrel[...])
    here = (iota((32, WIDTH), 0) == rel).astype(F32).astype(jnp.bfloat16)
    parts = [jnp.dot(x, here, preferred_element_type=F32) for x in split3(near[:, :32])]
    values = parts[0] + (parts[1] + parts[2])
    sat, alpha, n = (values[i : i + 1, :] for i in range(3))
    level = 2.0 * IRRIGATION * extra[1:2, :]
    for i, value in enumerate(derived(sat, alpha, n) + (level, level, 1.0 / sat, 1.0 / alpha)):
        for row in range(2):
            prm[6 * side + row, i : i + 1, :] = value

    p = row_params(prm, far)
    for j in range(TILES):
        k1[far, j], kl1[far, j], kn1[far, j] = cell_math(h0[far, j], p, False)
        cond, kl1[r, j], kn1[r, j], ic1[r - 1, j], sl[j], sn[j] = cell_math(h0[r, j], p)
        k1[r, j] = jnp.where(real, cond, -k1[own, j])

    phis = (k1, kl1, kn1)
    most = most_in[...]
    reach_row(h0, phis, ic1, psi, r, far, own, prm[r, LEV0 : LEV0 + 1, :])
    for j, net, _ in net_row(h0, k1, r, prm[r, LEV0 : LEV0 + 1, :], (far, own)):
        g = jnp.where(real, net * ic1[r - 1, j], 0.0)
        g1[r - 1, j] = g
        psi[1][r - 1, j] = psi[1][r - 1, j] - g * sl[j]
        psi[2][r - 1, j] = psi[2][r - 1, j] - g * sn[j]
        kx = k1[r, j] + k1[own, j]
        ic = edge[0, j]
        d = h0[r, j] - h0[own, j]
        g = (g1[own - 1, j] + kx * d) * ic
        g1[own - 1, j] = g
        d = d * ic
        psi[0][own - 1, j] = psi[0][own - 1, j] + d * k1[own, j]
        psi[1][own - 1, j] = psi[1][own - 1, j] + d * kl1[own, j] - g * edge[1, j]
        psi[2][own - 1, j] = psi[2][own - 1, j] + d * kn1[own, j] - g * edge[2, j]
        for q, phi in enumerate(phis):
            psi[6 + q][own - 1, j] = d * phi[r, j]
        most = jnp.maximum(most, (part[j] + kx) * ic)
    if exchange == "odd":
        result[...] = most
    else:
        most = jnp.maximum(jnp.maximum(most[:, :128], most[:, 128:256]), most[:, 256:])
        most = jnp.max(most, 0, keepdims=True)
        result[...] = jnp.broadcast_to(most[None], result.shape)


def second_kernel(rates, pick, put, column_in, goal, h0, g1, *rest):
    psi, rest = rest[:9], rest[9:]
    prm, zrel, h1_out, g2, spread, *rest = rest
    h1, k2, kl2, kn2, ic2, sl2, sn2, va, vb, kfs, dfs, wa, wb, u0, u1, u2, maps, maps_f, maps_g = rest
    position = lax.axis_index("row")
    size = CFL / jnp.max(rates[...])
    nothing = jnp.zeros((TILES, SUB, WIDTH), F32)
    for r in (1, 6):
        for ref in (wa, wb):
            ref[r] = nothing

    def cells(r, carry):
        p = row_params(prm, r)
        for j in range(TILES):
            head = h0[r, j] + size * g1[r - 1, j]
            h1[r, j] = head
            h1_out[r - 2, j] = head
            values = cell_math(head, p)
            k2[r, j], kl2[r, j], kn2[r, j], ic2[r - 2, j], sl2[r - 2, j], sn2[r - 2, j] = values
        return carry

    def edge_cells(i, carry):
        r = 1 + 5 * i
        p = row_params(prm, r)
        own = 2 + 3 * i
        real = jnp.where(i == 0, position > 0, position < lax.axis_size("row") - 1)
        for j in range(TILES):
            head = jnp.where(real, h0[r, j] + size * g1[r - 1, j], h1[own, j])
            h1[r, j] = head
            cond, kl2[r, j], kn2[r, j] = cell_math(head, p, False)
            k2[r, j] = jnp.where(real, cond, -k2[own, j])
        return carry

    lax.fori_loop(2, 6, cells, 0)
    lax.fori_loop(0, 2, edge_cells, 0)

    def flow(r, most):
        for j, net, total in net_row(h1, k2, r, prm[r, LEV1 : LEV1 + 1, :], (r - 1, r + 1), (kfs, dfs)):
            ic = ic2[r - 2, j]
            g2[r - 2, j] = net * ic
            most = jnp.maximum(most, total * ic)
        return most

    most = jnp.max(lax.fori_loop(2, 6, flow, jnp.zeros((SUB, WIDTH), F32)))

    column = column_in[...].astype(F32)
    field_g = g2[...].reshape(192, WIDTH)
    field_h = h1_out[...].reshape(192, WIDTH) + size * field_g
    seen = exact_dot(pick[...], jnp.concatenate([field_h, field_g], 1))
    seen_h = jnp.sum(column * seen[:, :WIDTH], 1, keepdims=True)
    seen_g = jnp.sum(column * seen[:, WIDTH:], 1, keepdims=True)
    diff = seen_h - goal[:, 0:1]
    events = 16.0
    loss = (
        jnp.sum(diff * diff) * (0.5 / events),
        jnp.sum(diff * seen_g) * (1.0 / events),
        jnp.sum(seen_g * seen_g) * (0.5 / events),
    )
    parts = [column * (diff * (1.0 / events)), column * (seen_g * (1.0 / events))]
    added = exact_dot(put[...], jnp.concatenate(parts, 1))
    va[...] = added[:, :WIDTH].reshape(OWN)
    vb[...] = added[:, WIDTH:].reshape(OWN)

    def scaled(r, carry):
        for j in range(TILES):
            ic = ic2[r - 2, j]
            wa[r, j] = va[r - 2, j] * ic
            wb[r, j] = vb[r - 2, j] * ic
        return carry

    lax.fori_loop(2, 6, scaled, 0)
    _, is_top, is_bottom = masks()

    def store_two(r, sums):
        flat = [jnp.sum(x, 0, keepdims=True) for x in sums]
        for q in range(3):
            of_a, of_b = flat[q], flat[3 + q]
            for c, row in enumerate((size * of_a, of_a + size * of_b, of_b)):
                maps[r - 1, 4 * q + c : 4 * q + c + 1, :] = row

    def store_heads(r, j, back):
        (v_a, j_a), (v_b, j_b) = back
        u0[r - 1, j] = v_a + size * j_a
        u1[r - 1, j] = v_b + j_a + size * j_b
        u2[r - 1, j] = j_b

    def edge_two(i, carry):
        r = 1 + 5 * i
        near = 2 + 3 * i
        sums = [jnp.zeros((SUB, WIDTH), F32) for _ in range(6)]
        for j in range(TILES):
            hj = h1[r, j]
            half = h1[near, j] - hj
            kd = k2[near, j] + k2[r, j]
            kj, kl, kn = k2[r, j], kl2[r, j], kn2[r, j]
            inv_h = 1.0 / hj
            back = []
            for part, w_ref in enumerate((wa, wb)):
                w = w_ref[near, j]
                gk, gh = -half * w, kd * w
                to_l = gk * kl
                sums[3 * part] += gk * kj
                sums[3 * part + 1] += to_l
                sums[3 * part + 2] += gk * kn
                back.append((0.0, gh + to_l * inv_h))
            store_heads(r, j, back)
        store_two(r, sums)
        return carry

    def back_two(r, carry):
        top = prm[r, LEV1 : LEV1 + 1, :]
        hs = [h1[r, j] for j in range(TILES)]
        ks = [k2[r, j] for j in range(TILES)]
        sums = [jnp.zeros((SUB, WIDTH), F32) for _ in range(6)]
        ws = [[w[r, j] for j in range(TILES)] for w in (wa, wb)]

        def face(j):
            if j < TILES - 1:
                half = 1.0 + hs[j] - hs[j + 1]
                kd = ks[j] + ks[j + 1]
                out = []
                for w in ws:
                    dw = w[j + 1] - w[j]
                    out.append((half * dw, kd * dw))
                return out
            half = 1.0 + hs[j] - subs_up(hs[0])
            kd = ks[j] + subs_up(ks[0])
            out = []
            for w in ws:
                dw = subs_up(w[0]) - w[j]
                out.append((jnp.where(is_bottom, -2.0 * w[j], half * dw), jnp.where(is_bottom, 0.0, kd * dw)))
            return out

        final = face(TILES - 1)
        above = [
            (jnp.where(is_top, top * w[0], subs_down(f[0])), subs_down(f[1]))
            for w, f in zip(ws, final)
        ]
        for j in range(TILES):
            below = final if j == TILES - 1 else face(j)
            hj, kj = hs[j], ks[j]
            kf, half_c = kfs[r - 2, j], dfs[r - 2, j]
            half_l, half_h = h1[r - 1, j] - hj, h1[r + 1, j] - hj
            k_low, k_high = k2[r - 1, j] + kj, k2[r + 1, j] + kj
            kl, kn = kl2[r, j], kn2[r, j]
            inv_h = 1.0 / hj
            g = g2[r - 2, j]
            gl, gn = g * sl2[r - 2, j], g * sn2[r - 2, j]
            back = []
            for part, (w_ref, v_ref) in enumerate(((wa, va), (wb, vb))):
                w = ws[part][j]
                dw = w - lanes_left(w)
                e, f = half_c * dw, kf * dw
                d_low, d_high = w - w_ref[r - 1, j], w - w_ref[r + 1, j]
                gk = e + lanes_right(e) + below[part][0] + above[part][0]
                gk = gk + half_l * d_low + half_h * d_high
                gh = lanes_right(f) - f + below[part][1] - above[part][1]
                gh = gh - k_low * d_low - k_high * d_high
                v = v_ref[r - 2, j]
                to_l = gk * kl - v * gl
                sums[3 * part] += gk * kj
                sums[3 * part + 1] += to_l
                sums[3 * part + 2] += gk * kn - v * gn
                back.append((v, gh + (to_l + v * g) * inv_h))
            store_heads(r, j, back)
            above = below
        store_two(r, sums)
        return carry

    lax.fori_loop(0, 2, edge_two, 0)
    lax.fori_loop(2, 6, back_two, 0)

    for ref in (maps, maps_f, maps_g):
        for r in range(6):
            for at in (3, 7, 11):
                ref[r, at : at + 1, :] = jnp.zeros((1, WIDTH), F32)
            ref[r, 12:16, :] = jnp.zeros((4, WIDTH), F32)

    def first_part(r, carry):
        for q in range(3):
            sums = [[jnp.zeros((SUB, WIDTH), F32) for _ in range(3)] for _ in range(3)]
            for j in range(TILES):
                us = [ref[r, j] for ref in (u0, u1, u2)]
                for kind in range(3):
                    factor = psi[3 * kind + q][r, j]
                    for c in range(3):
                        sums[kind][c] += us[c] * factor
            for c in range(3):
                at = 4 * q + c
                own, column_off, row_off = (jnp.sum(sums[kind][c], 0, keepdims=True) for kind in range(3))
                maps[r, at : at + 1, :] = maps[r, at : at + 1, :] + size * own
                maps_f[r, at : at + 1, :] = size * column_off
                maps_g[r, at : at + 1, :] = size * row_off
        return carry

    lax.fori_loop(0, 6, first_part, 0)

    odd = iota((16, WIDTH), 1) % 2 == 1
    which = iota((16, WIDTH), 0)
    pieces = []
    for r in range(6):
        off = maps_f[r]
        off = jnp.where(odd, lanes_left(off), lanes_right(off))
        other = r + 1 if r % 2 == 0 else r - 1
        scale = jnp.where(which < 4, prm[r + 1, IKS : IKS + 1, :], jnp.where(which < 8, prm[r + 1, IAL : IAL + 1, :], 1.0))
        pieces.append((maps[r] + off + maps_g[other]) * scale)
    left = jnp.concatenate(pieces, 1)
    near = zrel[...]
    zone_id = iota((32, WIDTH), 0)
    onehot = jnp.concatenate([(zone_id == near[r : r + 1, :]).astype(F32) for r in range(1, 7)], 1)
    onehot = onehot.astype(jnp.bfloat16)
    nt = (((1,), (1,)), ((), ()))
    parts = [lax.dot_general(part, onehot, nt, preferred_element_type=F32) for part in split3(left)]
    by_zone = parts[0] + (parts[1] + parts[2])
    fields = [by_zone[4 * q : 4 * q + 4, :] for q in range(3)]
    sub4 = iota((4, 32), 0)
    fields.append(jnp.where(sub4 == 0, loss[0], jnp.where(sub4 == 1, loss[1], loss[2])))
    sums = jnp.concatenate(fields, 1)
    state = jnp.where(iota((4, 128), 1) < 64, most, size)
    payload = jnp.where(iota((4, 128), 0) == 3, state, sums)
    spread[...] = jnp.broadcast_to(payload[None], spread.shape)


def ring_kernel(parts, spread):
    lane = iota((SUB, 256), 1)
    total = jnp.zeros((SUB, 256), F32)
    blank = jnp.zeros((SUB, 128), F32)
    most = None
    loss = jnp.zeros((SUB, 256), F32)
    for z in range(8):
        tile = jnp.concatenate([parts[z], parts[8 + z]], 0)
        most = tile if most is None else jnp.maximum(most, tile)
        tile = jnp.concatenate([tile, blank], 1)
        for q in range(3):
            start = 84 * q + 8 * z
            moved = pltpu.roll(tile, (start - 32 * q) % 256, 1)
            total = total + jnp.where(jnp.logical_and(lane >= start, lane < start + NEAR), moved, 0.0)
        loss = loss + tile
    total = jnp.where(lane == 252, pltpu.roll(loss, 252 - 96, 1), total)
    rows = []
    one = iota((1, 256), 1)
    for z_hi in range(2):
        state = most[4 * z_hi + 3 : 4 * z_hi + 4, :]
        for power in range(3):
            row = total[4 * z_hi + power : 4 * z_hi + power + 1, :]
            row = jnp.where(one == 253, state[:, 0:1], row)
            rows.append(jnp.where(one == 254, state[:, 64:65], row))
    rows = jnp.concatenate(rows, 1)
    spread[...] = jnp.broadcast_to(rows[None], spread.shape)


def last_kernel(parts, h1, g2, final, grad_k, grad_a, grad_n, misfit, rates):
    sums = [jnp.zeros((1, 256), F32) for _ in range(4)]
    for pair in range(8):
        tiles = [parts[8 * y + pair] for y in range(4)]
        for z_hi in range(2):
            powers = [[tile[:, 256 * (3 * z_hi + i) : 256 * (3 * z_hi + i + 1)] for i in range(3)] for tile in tiles]
            first = [part[0] for part in powers]
            most = jnp.maximum(jnp.maximum(first[0], first[1]), jnp.maximum(first[2], first[3]))
            step = CFL / most[:, 253:254]
            rates[2 * pair + z_hi] = jnp.broadcast_to(step, (1, 128))
            move = step - first[0][:, 254:255]
            for y in range(4):
                a, b, c = powers[y]
                sums[y] = sums[y] + (a + move * (b + move * c))
    lane = iota((1, 256), 1)
    rows = sums
    for q, out in enumerate((grad_k, grad_a, grad_n)):
        total = jnp.zeros((1, 256), F32)
        for y in range(4):
            field = rows[y] if q == 0 else pltpu.roll(rows[y], 256 - 84 * q, 1)
            total = total + pltpu.roll(jnp.where(lane < 84, field, 0.0), (64 * y - 4) % 256, 1)
        out[...] = total
    misfit[0, 0] = jnp.sum(jnp.where(lane == 252, rows[0] + rows[1] + rows[2] + rows[3], 0.0))
    _, pair, z_hi = axes()
    size = rates[2 * pair + z_hi]
    size = jnp.concatenate([size, size, size], 1)
    for j in range(TILES):
        for row in range(4):
            tile = h1[row, j] + size * g2[row, j]
            for s in range(SUB):
                final[TILES * s + j, row : row + 1, :] = tile[s : s + 1, :]


VMEM = pl.BlockSpec(memory_space=pltpu.VMEM)
SMEM = pl.BlockSpec(memory_space=pltpu.SMEM)


def call(kernel, name, ins, outs, out_specs=None, scratch=(), cost=None, in_place=None, room=8):
    return pl.pallas_call(
        kernel,
        name=name,
        in_specs=ins,
        out_specs=out_specs or [VMEM] * len(outs),
        out_shape=[jax.ShapeDtypeStruct(shape, dtype) for shape, dtype in outs],
        scratch_shapes=scratch,
        cost_estimate=cost,
        input_output_aliases=in_place or {},
        compiler_params=pltpu.CompilerParams(vmem_limit_bytes=room * 1024 * 1024),
    )


def local(
    initial_head,
    sat_conductivity,
    vg_alpha,
    vg_n,
    zone_map,
    forcing_plan,
    tensiometer_cells,
    tensiometer_heads,
):
    count = lax.axis_size("row")
    plan = forcing_plan[0]
    edge = (2 * TILES + 1, SUB, WIDTH)
    h0, send_odd, send_even, zones = call(
        pack_kernel,
        "pack_edges",
        [pl.BlockSpec(memory_space=pltpu.HBM)] * 3,
        [(FIELD, F32), (edge, F32), (edge, F32), ((2, WIDTH), F32)],
        scratch=[
            pltpu.VMEM((48, 4, WIDTH), F32),
            pltpu.VMEM((2, 192), jnp.int32),
            pltpu.VMEM((2, 2), jnp.int32),
            pltpu.SemaphoreType.DMA((3,)),
        ],
    )(initial_head[0], zone_map, plan)
    odd = [(i, i + 1) for i in range(1, count - 1, 2)]
    even = [(i, i + 1) for i in range(0, count, 2)]
    got_odd = lax.ppermute(send_odd, "row", odd + [(j, i) for i, j in odd])
    got_even = lax.ppermute(send_even, "row", even + [(j, i) for i, j in even])
    wide = (6, TILES, SUB, WIDTH)
    fields = [(wide, F32)] * 10 + [((ROWS, 16, WIDTH), F32), ((ROWS, WIDTH), jnp.int32)]
    whole = [pltpu.VMEM(FIELD, F32)] * 3 + [pltpu.VMEM(wide, F32)]
    seen = tensiometer_cells.shape[1]
    own = call(
        own_kernel,
        "own_cells",
        [SMEM] * 4 + [VMEM] * 4,
        fields
        + [((SUB, WIDTH), F32), ((SUB, 128), F32)]
        + [((seen, 192), jnp.bfloat16), ((192, seen), jnp.bfloat16), ((seen, WIDTH), jnp.bfloat16), ((seen, 128), F32)],
        scratch=whole + [pltpu.VMEM(wide, F32)] * 2,
        cost=pl.CostEstimate(flops=200_000_000, bytes_accessed=8_000_000, transcendentals=600_000),
    )(sat_conductivity, vg_alpha, vg_n, plan, h0, zones, tensiometer_cells, tensiometer_heads)
    held, (most, near), sensors = (h0, *own[:12]), own[12:14], own[14:]
    row = (TILES, SUB, WIDTH)
    for exchange, got, result in (("odd", got_odd, (SUB, WIDTH)), ("even", got_even, (32, 1, 128))):
        *held, most = call(
            functools.partial(side_kernel, exchange),
            "first_step_" + exchange,
            [VMEM] * 17,
            [(FIELD, F32)] + fields + [(result, F32)],
            scratch=whole + [pltpu.VMEM(row, F32)] * 3 + [pltpu.VMEM((3, *row), F32)],
            in_place={4 + i: i for i in range(13)},
        )(near, zones, most, got, *held)
    fields, rates = held, most
    rates = lax.all_to_all(rates, "row", 0, 0, tiled=True)
    h1, g2, sums = call(
        second_kernel,
        "second_step_and_adjoint",
        [VMEM] * 18,
        [(OWN, F32), (OWN, F32), ((16, 4, 128), F32)],
        scratch=[pltpu.VMEM(FIELD, F32)] * 4
        + [pltpu.VMEM(OWN, F32)] * 7
        + [pltpu.VMEM(FIELD, F32)] * 2
        + [pltpu.VMEM(wide, F32)] * 3
        + [pltpu.VMEM((6, 16, WIDTH), F32)] * 3,
        room=20,
    )(rates, *sensors, *fields)
    sums = lax.all_to_all(sums, ("event", "row"), 0, 0, tiled=True, axis_index_groups=RINGS)
    (sums,) = call(ring_kernel, "ring_sums", [VMEM], [((32, 1, 6 * 256), F32)])(sums)
    sums = lax.all_to_all(sums, ("event", "row"), 0, 0, tiled=True, axis_index_groups=PLANES)
    row = ((1, ZONES), F32)
    final, grad_k, grad_a, grad_n, misfit = call(
        last_kernel,
        "final_head_and_sums",
        [VMEM, VMEM, VMEM],
        [((48, 4, WIDTH), F32), row, row, row, ((1, 1), F32)],
        [VMEM] * 4 + [SMEM],
        scratch=[pltpu.VMEM((16, 1, 128), F32)],
    )(sums, h1, g2)
    return (final[None], misfit[0, 0], grad_k[0], grad_a[0], grad_n[0])


def solution(mesh):
    return jax.shard_map(
        local,
        mesh=mesh,
        in_specs=(
            P("event", None, "row", None),
            P(),
            P(),
            P(),
            P("row", None),
            P("event", None, "row"),
            P("event", "row"),
            P("event", "row"),
        ),
        out_specs=(P("event", None, "row", None), P(), P(), P(), P()),
        check_vma=False,
    )
```

```python
import functools

import jax
import jax.numpy as jnp
from jax import lax
from jax.experimental import pallas as pl
from jax.experimental.pallas import tpu as pltpu
from jax.sharding import PartitionSpec as P

CFL = 0.4
IRRIGATION = 0.2
WATER_RANGE = 0.35

TILES = 6
SUB = 8
WIDTH = 384
ROWS = 8
FIELD = (ROWS, TILES, SUB, WIDTH)
OWN = (4, TILES, SUB, WIDTH)
NEAR = 28
ZONES = 256
KS, AL, N, N1, M, MP, IC0, IN1, LEV0, LEV1, IKS, IAL = range(12)
F32 = jnp.float32


def device(x, z_hi, core, y, z_lo):
    return ((x * 2 + z_hi) * 2 + core) * 32 + y * 8 + z_lo


PLANES = [
    [device(x, z_hi, core, y, z_lo) for y in range(4) for x in range(4) for core in range(2)]
    for z_hi in range(2)
    for z_lo in range(8)
]
RINGS = [
    [device(x, z_hi, core, y, z_lo) for z_hi in range(2) for z_lo in range(8)]
    for x in range(4)
    for core in range(2)
    for y in range(4)
]


def lanes_left(x):
    return pltpu.roll(x, WIDTH - 1, 1)


def lanes_right(x):
    return pltpu.roll(x, 1, 1)


def subs_up(x):
    return pltpu.roll(x, SUB - 1, 0)


def subs_down(x):
    return pltpu.roll(x, 1, 0)


def iota(shape, dim):
    return lax.broadcasted_iota(jnp.int32, shape, dim)


def split3(x):
    hi = x.astype(jnp.bfloat16)
    rest = x - hi.astype(F32)
    mid = rest.astype(jnp.bfloat16)
    return hi, mid, (rest - mid.astype(F32)).astype(jnp.bfloat16)


def exact_dot(pick, x, dims=(((1,), (0,)), ((), ()))):
    parts = [lax.dot_general(pick, part, dims, preferred_element_type=F32) for part in split3(x)]
    return parts[0] + (parts[1] + parts[2])


def axes():
    event = lax.axis_index("event")
    return lax.axis_index("row"), event // 4 * 2 + event % 2, event // 2 % 2


def pack_kernel(head_in, zone_in, plan_in, h0, send_odd, send_even, zones, head, zone, plan, sems):
    copies = [
        pltpu.make_async_copy(src, dst, sems.at[i])
        for i, (src, dst) in enumerate(((head_in, head), (zone_in, zone), (plan_in, plan)))
    ]
    for copy in copies:
        copy.start()
    wide = (iota((192, WIDTH), 1) // 2 == iota((192, WIDTH), 0)).astype(F32)
    copies[1].wait()
    copies[2].wait()
    blocks = jnp.dot(zone[...].astype(F32), wide, preferred_element_type=F32)
    zones[...] = blocks
    level = plan[...].astype(F32)
    copies[0].wait()
    for depth in range(TILES * SUB):
        block = head[depth]
        j, s = depth % TILES, depth // TILES
        for row in range(4):
            h0[2 + row, j, s : s + 1, :] = block[row : row + 1, :]
    sub = iota((SUB, WIDTH), 0)
    odd = lax.axis_index("row") % 2 == 1

    def fill(out, pair):
        out[0:TILES] = h0[2 + 2 * pair]
        out[TILES : 2 * TILES] = h0[3 + 2 * pair]
        out[2 * TILES] = jnp.where(sub == 0, blocks[pair : pair + 1, :], level[0:1, pair : pair + 1])

    @pl.when(odd)
    def _():
        fill(send_odd, 1)
        fill(send_even, 0)

    @pl.when(jnp.logical_not(odd))
    def _():
        fill(send_odd, 0)
        fill(send_even, 1)


def cell_math(head, p, with_store=True):
    wet = jnp.log(-p[AL] * head)
    u = jnp.exp(p[N] * wet)
    d = 1.0 + u
    w = jnp.log(d)
    inv = 1.0 / d
    r = u * inv
    mw = p[M] * w
    q = jnp.exp(-0.5 * mw)
    f = jnp.exp(p[N1] * wet - mw)
    t = 1.0 - f
    kq = p[KS] * q * t
    half, twice = -0.5 * t, 2.0 * f
    e1 = p[MP] * w + p[M] * wet * r
    cond = kq * t
    cond_l = kq * p[N1] * (half * r - twice * inv)
    cond_n = kq * (half * e1 - twice * (wet - e1))
    if not with_store:
        return cond, cond_l, cond_n
    inv_store = d * p[IC0] / f
    store_l = p[N] - r * (2.0 * p[N] - 1.0)
    store_n = p[IN1] + wet - e1 - r * wet
    return cond, cond_l, cond_n, inv_store, store_l, store_n


def derived(sat, alpha, n):
    n1 = n - 1.0
    return (
        sat, alpha, n, n1, 1.0 - 1.0 / n, 1.0 / (n * n), 0.5 / (WATER_RANGE * n1 * alpha), 1.0 / n1,
    )


def row_params(prm, r):
    return [prm[r, i : i + 1, :] for i in range(8)]


def masks():
    last = iota((SUB, WIDTH), 1) == WIDTH - 1
    sub = iota((SUB, WIDTH), 0)
    return last, sub == 0, sub == SUB - 1


def net_row(h, k, r, top, beside, keep=None):
    last, is_top, is_bottom = masks()
    hs = [h[r, j] for j in range(TILES)]
    ks = [k[r, j] for j in range(TILES)]

    def face(j):
        if j < TILES - 1:
            kd = ks[j] + ks[j + 1]
            return kd, kd * (1.0 + hs[j] - hs[j + 1])
        kd = ks[j] + subs_up(ks[0])
        flow = kd * (1.0 + hs[j] - subs_up(hs[0]))
        return jnp.where(is_bottom, 2.0 * ks[j], kd), jnp.where(is_bottom, 2.0 * ks[j], flow)

    final = face(TILES - 1)
    above = (
        jnp.where(is_top, 2.0 * ks[0], subs_down(final[0])),
        jnp.where(is_top, top * ks[0], subs_down(final[1])),
    )
    for j in range(TILES):
        below = final if j == TILES - 1 else face(j)
        hj, kj = hs[j], ks[j]
        kf = jnp.where(last, 0.0, kj + lanes_left(kj))
        difference = jnp.where(last, 0.0, lanes_left(hj) - hj)
        if keep is not None:
            keep[0][r - 2, j], keep[1][r - 2, j] = kf, difference
        flow = kf * difference
        net = flow - lanes_right(flow) + above[1] - below[1]
        total = kf + lanes_right(kf) + above[0] + below[0]
        for other in beside:
            kx = k[other, j] + kj
            net = net + kx * (h[other, j] - hj)
            total = total + kx
        above = below
        yield j, net, total


def reach_row(h, phis, ic, psi, r, same, foreign, top):
    lane = iota((SUB, WIDTH), 1)
    even = lane % 2 == 0
    ends = jnp.logical_or(lane == 0, lane == WIDTH - 1)
    _, is_top, is_bottom = masks()

    def beside(x):
        left, right = lanes_right(x), lanes_left(x)
        return jnp.where(even, right, left), jnp.where(even, left, right)

    for j in range(TILES):
        hj, half = h[r, j], ic[r - 1, j]
        inner, outer = beside(hj)
        d_in = inner - hj
        d_out = jnp.where(ends, 0.0, outer - hj)
        h_below = h[r, j + 1] if j < TILES - 1 else subs_up(h[r, 0])
        h_above = h[r, j - 1] if j > 0 else subs_down(h[r, TILES - 1])
        d_below, d_above = h_below - hj - 1.0, 1.0 + h_above - hj
        self_below, self_above = d_below, d_above
        if j == TILES - 1:
            self_below, d_below = jnp.where(is_bottom, -2.0, d_below), jnp.where(is_bottom, 0.0, d_below)
        if j == 0:
            self_above, d_above = jnp.where(is_top, top, d_above), jnp.where(is_top, 0.0, d_above)
        d_same = h[same, j] - hj
        whole = d_in + d_out + self_below + self_above + d_same
        if foreign is not None:
            d_far = h[foreign, j] - hj
            whole = whole + d_far
        for i, phi in enumerate(phis):
            below = phi[r, j + 1] if j < TILES - 1 else subs_up(phi[r, 0])
            above = phi[r, j - 1] if j > 0 else subs_down(phi[r, TILES - 1])
            inner, outer = beside(phi[r, j])
            own = whole * phi[r, j] + d_in * inner + d_below * below + d_above * above + d_same * phi[same, j]
            psi[i][r - 1, j] = half * own
            psi[3 + i][r - 1, j] = (half * d_out) * outer
            if foreign is not None:
                psi[6 + i][r - 1, j] = (half * d_far) * phi[foreign, j]


def places(cell):
    line = jnp.floor((cell + 0.5) * (1.0 / WIDTH))
    column = cell - WIDTH * line
    depth = jnp.floor((line + 0.5) * 0.25)
    block = jnp.floor((depth + 0.5) * (1.0 / TILES))
    return (line - 4.0 * depth) * 48.0 + (depth - TILES * block) * 8.0 + block, column


def own_kernel(
    tab_k, tab_a, tab_n, plan, h0, zones, cells_at, goals,
    g1, *rest,
):
    psi, rest = rest[:9], rest[9:]
    prm, zrel, most_out, near, pick, put, column, goal, k1, kl1, kn1, ic1, p1, q1 = rest
    base = 8 * lax.axis_index("row") - 4
    sub = iota((SUB, WIDTH), 0)
    rel = (jnp.where(sub < 2, zones[0:1, :], zones[1:2, :]).astype(jnp.int32) - base) & (ZONES - 1)
    for r in range(4):
        zrel[2 + r : 3 + r, :] = rel[r : r + 1, :]
    sat = jnp.ones((SUB, WIDTH), F32)
    alpha, n = sat, 2.0 * sat
    lane = iota((SUB, 128), 1)
    line = iota((SUB, 128), 0)
    table = jnp.ones((SUB, 128), F32)
    for i in range(NEAR):
        at = (base + i) & (ZONES - 1)
        here = rel == i
        sat = jnp.where(here, tab_k[at], sat)
        alpha = jnp.where(here, tab_a[at], alpha)
        n = jnp.where(here, tab_n[at], n)
        entry = jnp.where(line == 0, tab_k[at], jnp.where(line == 1, tab_a[at], tab_n[at]))
        table = jnp.where(lane == i, entry, table)
    near[...] = table
    levels = [
        2.0 * IRRIGATION * jnp.where(sub < 2, plan[step, 0].astype(F32), plan[step, 1].astype(F32))
        for step in range(2)
    ]
    for i, value in enumerate(derived(sat, alpha, n) + (*levels, 1.0 / sat, 1.0 / alpha)):
        for r in range(4):
            prm[2 + r, i : i + 1, :] = value[r : r + 1, :]

    def cells(r, carry):
        p = row_params(prm, r)
        for j in range(TILES):
            values = cell_math(h0[r, j], p)
            k1[r, j], kl1[r, j], kn1[r, j], ic1[r - 1, j], p1[r - 1, j], q1[r - 1, j] = values
        return carry

    lax.fori_loop(2, 6, cells, 0)

    def flow(r, most):
        for j, net, total in net_row(h0, k1, r, prm[r, LEV0 : LEV0 + 1, :], (r - 1, r + 1)):
            ic = ic1[r - 1, j]
            g = net * ic
            g1[r - 1, j] = g
            p1[r - 1, j] = g * p1[r - 1, j]
            q1[r - 1, j] = g * q1[r - 1, j]
            most = jnp.maximum(most, total * ic)
        return most

    def edge_flow(i, carry):
        r = 2 + 3 * i
        for j, net, total in net_row(h0, k1, r, prm[r, LEV0 : LEV0 + 1, :], (3 + i,)):
            g1[r - 1, j] = net
            g1[5 * i, j] = total
            for at, value in enumerate((k1[r, j], kl1[r, j], kn1[r, j])):
                psi[at][5 * i, j] = value
            for at, value in enumerate((ic1[r - 1, j], p1[r - 1, j], q1[r - 1, j])):
                psi[3 + at][5 * i, j] = value
        return carry

    most_out[...] = lax.fori_loop(3, 5, flow, jnp.zeros((SUB, WIDTH), F32))
    lax.fori_loop(0, 2, edge_flow, 0)
    phis = (k1, kl1, kn1)

    def reach(i, carry):
        r = 3 + i
        reach_row(h0, phis, ic1, psi, r, 2 + 3 * i, 4 - i, prm[r, LEV0 : LEV0 + 1, :])
        for j in range(TILES):
            psi[1][r - 1, j] = psi[1][r - 1, j] - p1[r - 1, j]
            psi[2][r - 1, j] = psi[2][r - 1, j] - q1[r - 1, j]
        return carry

    def edge_reach(i, carry):
        r = 2 + 3 * i
        reach_row(h0, phis, ic1, psi, r, 3 + i, None, prm[r, LEV0 : LEV0 + 1, :])
        return carry

    lax.fori_loop(0, 2, reach, 0)
    lax.fori_loop(0, 2, edge_reach, 0)

    count = cells_at.shape[1]
    wide = jnp.where(iota((SUB, count), 0) == 0, cells_at[...].astype(F32), goals[...])
    tall = jnp.transpose(wide)
    line_wide = places(wide[0:1, :])[0].astype(jnp.int32)
    line_tall, column_tall = places(tall[:, 0:1])
    pick[...] = (iota((count, 192), 1) == line_tall.astype(jnp.int32)).astype(F32).astype(jnp.bfloat16)
    put[...] = (iota((192, count), 0) == line_wide).astype(F32).astype(jnp.bfloat16)
    column[...] = (iota((count, WIDTH), 1) == column_tall.astype(jnp.int32)).astype(F32).astype(jnp.bfloat16)
    goal[...] = jnp.broadcast_to(tall[:, 1:2], goal.shape)


def side_kernel(exchange, near, zones, most_in, got, *rest):
    h0, g1, *psi = rest[13:24]
    prm, zrel, result, k1, kl1, kn1, ic1, sl, sn, part, edge = rest[24:]
    position = lax.axis_index("row")
    side = position % 2 if exchange == "odd" else 1 - position % 2
    real = jnp.where(side == 0, position > 0, position < lax.axis_size("row") - 1)
    far, r, own = 7 * side, 1 + 5 * side, 2 + 3 * side
    for row in range(2):
        for j in range(TILES):
            h0[6 * side + row, j] = jnp.where(real, got[row * TILES + j], h0[own, j])
    part[...] = g1[5 * side]
    for at, phi in enumerate((k1, kl1, kn1)):
        phi[own] = psi[at][5 * side]
        edge[at] = psi[3 + at][5 * side]
    extra = got[2 * TILES]
    zone = jnp.where(real, extra[0:1, :], jnp.where(side == 0, zones[0:1, :], zones[1:2, :]))
    rel = (zone.astype(jnp.int32) - (8 * position - 4)) & (ZONES - 1)
    zrel[...] = jnp.where(iota((SUB, WIDTH), 0) // 2 == 3 * side, rel, zrel[...])
    here = (iota((32, WIDTH), 0) == rel).astype(F32).astype(jnp.bfloat16)
    parts = [jnp.dot(x, here, preferred_element_type=F32) for x in split3(near[:, :32])]
    values = parts[0] + (parts[1] + parts[2])
    sat, alpha, n = (values[i : i + 1, :] for i in range(3))
    level = 2.0 * IRRIGATION * extra[1:2, :]
    for i, value in enumerate(derived(sat, alpha, n) + (level, level, 1.0 / sat, 1.0 / alpha)):
        for row in range(2):
            prm[6 * side + row, i : i + 1, :] = value

    p = row_params(prm, far)
    for j in range(TILES):
        k1[far, j], kl1[far, j], kn1[far, j] = cell_math(h0[far, j], p, False)
        cond, kl1[r, j], kn1[r, j], ic1[r - 1, j], sl[j], sn[j] = cell_math(h0[r, j], p)
        k1[r, j] = jnp.where(real, cond, -k1[own, j])

    phis = (k1, kl1, kn1)
    most = most_in[...]
    reach_row(h0, phis, ic1, psi, r, far, own, prm[r, LEV0 : LEV0 + 1, :])
    for j, net, _ in net_row(h0, k1, r, prm[r, LEV0 : LEV0 + 1, :], (far, own)):
        g = jnp.where(real, net * ic1[r - 1, j], 0.0)
        g1[r - 1, j] = g
        psi[1][r - 1, j] = psi[1][r - 1, j] - g * sl[j]
        psi[2][r - 1, j] = psi[2][r - 1, j] - g * sn[j]
        kx = k1[r, j] + k1[own, j]
        ic = edge[0, j]
        d = h0[r, j] - h0[own, j]
        g = (g1[own - 1, j] + kx * d) * ic
        g1[own - 1, j] = g
        d = d * ic
        psi[0][own - 1, j] = psi[0][own - 1, j] + d * k1[own, j]
        psi[1][own - 1, j] = psi[1][own - 1, j] + d * kl1[own, j] - g * edge[1, j]
        psi[2][own - 1, j] = psi[2][own - 1, j] + d * kn1[own, j] - g * edge[2, j]
        for q, phi in enumerate(phis):
            psi[6 + q][own - 1, j] = d * phi[r, j]
        most = jnp.maximum(most, (part[j] + kx) * ic)
    if exchange == "odd":
        result[...] = most
    else:
        most = jnp.maximum(jnp.maximum(most[:, :128], most[:, 128:256]), most[:, 256:])
        most = jnp.max(most, 0, keepdims=True)
        result[...] = jnp.broadcast_to(most[None], result.shape)


def second_kernel(rates, pick, put, column_in, goal, h0, g1, *rest):
    psi, rest = rest[:9], rest[9:]
    prm, zrel, h1_out, g2, spread, *rest = rest
    h1, k2, kl2, kn2, ic2, sl2, sn2, va, vb, kfs, dfs, wa, wb, u0, u1, u2, maps, maps_f, maps_g = rest
    position = lax.axis_index("row")
    size = CFL / jnp.max(rates[...])
    nothing = jnp.zeros((TILES, SUB, WIDTH), F32)
    for r in (1, 6):
        for ref in (wa, wb):
            ref[r] = nothing

    def cells(r, carry):
        p = row_params(prm, r)
        for j in range(TILES):
            head = h0[r, j] + size * g1[r - 1, j]
            h1[r, j] = head
            h1_out[r - 2, j] = head
            values = cell_math(head, p)
            k2[r, j], kl2[r, j], kn2[r, j], ic2[r - 2, j], sl2[r - 2, j], sn2[r - 2, j] = values
        return carry

    def edge_cells(i, carry):
        r = 1 + 5 * i
        p = row_params(prm, r)
        own = 2 + 3 * i
        real = jnp.where(i == 0, position > 0, position < lax.axis_size("row") - 1)
        for j in range(TILES):
            head = jnp.where(real, h0[r, j] + size * g1[r - 1, j], h1[own, j])
            h1[r, j] = head
            cond, kl2[r, j], kn2[r, j] = cell_math(head, p, False)
            k2[r, j] = jnp.where(real, cond, -k2[own, j])
        return carry

    lax.fori_loop(2, 6, cells, 0)
    lax.fori_loop(0, 2, edge_cells, 0)

    def flow(r, most):
        for j, net, total in net_row(h1, k2, r, prm[r, LEV1 : LEV1 + 1, :], (r - 1, r + 1), (kfs, dfs)):
            ic = ic2[r - 2, j]
            g2[r - 2, j] = net * ic
            most = jnp.maximum(most, total * ic)
        return most

    most = jnp.max(lax.fori_loop(2, 6, flow, jnp.zeros((SUB, WIDTH), F32)))

    column = column_in[...].astype(F32)
    field_g = g2[...].reshape(192, WIDTH)
    field_h = h1_out[...].reshape(192, WIDTH) + size * field_g
    seen_h = jnp.sum(column * exact_dot(pick[...], field_h), 1, keepdims=True)
    seen_g = jnp.sum(column * exact_dot(pick[...], field_g), 1, keepdims=True)
    diff = seen_h - goal[:, 0:1]
    events = 16.0
    loss = (
        jnp.sum(diff * diff) * (0.5 / events),
        jnp.sum(diff * seen_g) * (1.0 / events),
        jnp.sum(seen_g * seen_g) * (0.5 / events),
    )
    va[...] = exact_dot(put[...], column * (diff * (1.0 / events))).reshape(OWN)
    vb[...] = exact_dot(put[...], column * (seen_g * (1.0 / events))).reshape(OWN)

    def scaled(r, carry):
        for j in range(TILES):
            ic = ic2[r - 2, j]
            wa[r, j] = va[r - 2, j] * ic
            wb[r, j] = vb[r - 2, j] * ic
        return carry

    lax.fori_loop(2, 6, scaled, 0)
    _, is_top, is_bottom = masks()

    def store_two(r, sums):
        flat = [jnp.sum(x, 0, keepdims=True) for x in sums]
        for q in range(3):
            of_a, of_b = flat[q], flat[3 + q]
            for c, row in enumerate((size * of_a, of_a + size * of_b, of_b)):
                maps[r - 1, 4 * q + c : 4 * q + c + 1, :] = row

    def store_heads(r, j, back):
        (v_a, j_a), (v_b, j_b) = back
        u0[r - 1, j] = v_a + size * j_a
        u1[r - 1, j] = v_b + j_a + size * j_b
        u2[r - 1, j] = j_b

    def edge_two(i, carry):
        r = 1 + 5 * i
        near = 2 + 3 * i
        sums = [jnp.zeros((SUB, WIDTH), F32) for _ in range(6)]
        for j in range(TILES):
            hj = h1[r, j]
            half = h1[near, j] - hj
            kd = k2[near, j] + k2[r, j]
            kj, kl, kn = k2[r, j], kl2[r, j], kn2[r, j]
            inv_h = 1.0 / hj
            back = []
            for part, w_ref in enumerate((wa, wb)):
                w = w_ref[near, j]
                gk, gh = -half * w, kd * w
                to_l = gk * kl
                sums[3 * part] += gk * kj
                sums[3 * part + 1] += to_l
                sums[3 * part + 2] += gk * kn
                back.append((0.0, gh + to_l * inv_h))
            store_heads(r, j, back)
        store_two(r, sums)
        return carry

    def back_two(r, carry):
        top = prm[r, LEV1 : LEV1 + 1, :]
        hs = [h1[r, j] for j in range(TILES)]
        ks = [k2[r, j] for j in range(TILES)]
        sums = [jnp.zeros((SUB, WIDTH), F32) for _ in range(6)]
        ws = [[w[r, j] for j in range(TILES)] for w in (wa, wb)]

        def face(j):
            if j < TILES - 1:
                half = 1.0 + hs[j] - hs[j + 1]
                kd = ks[j] + ks[j + 1]
                out = []
                for w in ws:
                    dw = w[j + 1] - w[j]
                    out.append((half * dw, kd * dw))
                return out
            half = 1.0 + hs[j] - subs_up(hs[0])
            kd = ks[j] + subs_up(ks[0])
            out = []
            for w in ws:
                dw = subs_up(w[0]) - w[j]
                out.append((jnp.where(is_bottom, -2.0 * w[j], half * dw), jnp.where(is_bottom, 0.0, kd * dw)))
            return out

        final = face(TILES - 1)
        above = [
            (jnp.where(is_top, top * w[0], subs_down(f[0])), subs_down(f[1]))
            for w, f in zip(ws, final)
        ]
        for j in range(TILES):
            below = final if j == TILES - 1 else face(j)
            hj, kj = hs[j], ks[j]
            kf, half_c = kfs[r - 2, j], dfs[r - 2, j]
            half_l, half_h = h1[r - 1, j] - hj, h1[r + 1, j] - hj
            k_low, k_high = k2[r - 1, j] + kj, k2[r + 1, j] + kj
            kl, kn = kl2[r, j], kn2[r, j]
            inv_h = 1.0 / hj
            g = g2[r - 2, j]
            gl, gn = g * sl2[r - 2, j], g * sn2[r - 2, j]
            back = []
            for part, (w_ref, v_ref) in enumerate(((wa, va), (wb, vb))):
                w = ws[part][j]
                dw = w - lanes_left(w)
                e, f = half_c * dw, kf * dw
                d_low, d_high = w - w_ref[r - 1, j], w - w_ref[r + 1, j]
                gk = e + lanes_right(e) + below[part][0] + above[part][0]
                gk = gk + half_l * d_low + half_h * d_high
                gh = lanes_right(f) - f + below[part][1] - above[part][1]
                gh = gh - k_low * d_low - k_high * d_high
                v = v_ref[r - 2, j]
                to_l = gk * kl - v * gl
                sums[3 * part] += gk * kj
                sums[3 * part + 1] += to_l
                sums[3 * part + 2] += gk * kn - v * gn
                back.append((v, gh + (to_l + v * g) * inv_h))
            store_heads(r, j, back)
            above = below
        store_two(r, sums)
        return carry

    lax.fori_loop(0, 2, edge_two, 0)
    lax.fori_loop(2, 6, back_two, 0)

    for ref in (maps, maps_f, maps_g):
        for r in range(6):
            for at in (3, 7, 11):
                ref[r, at : at + 1, :] = jnp.zeros((1, WIDTH), F32)
            ref[r, 12:16, :] = jnp.zeros((4, WIDTH), F32)

    def first_part(r, carry):
        for q in range(3):
            sums = [[jnp.zeros((SUB, WIDTH), F32) for _ in range(3)] for _ in range(3)]
            for j in range(TILES):
                us = [ref[r, j] for ref in (u0, u1, u2)]
                for kind in range(3):
                    factor = psi[3 * kind + q][r, j]
                    for c in range(3):
                        sums[kind][c] += us[c] * factor
            for c in range(3):
                at = 4 * q + c
                own, column_off, row_off = (jnp.sum(sums[kind][c], 0, keepdims=True) for kind in range(3))
                maps[r, at : at + 1, :] = maps[r, at : at + 1, :] + size * own
                maps_f[r, at : at + 1, :] = size * column_off
                maps_g[r, at : at + 1, :] = size * row_off
        return carry

    lax.fori_loop(0, 6, first_part, 0)

    odd = iota((16, WIDTH), 1) % 2 == 1
    which = iota((16, WIDTH), 0)
    pieces = []
    for r in range(6):
        off = maps_f[r]
        off = jnp.where(odd, lanes_left(off), lanes_right(off))
        other = r + 1 if r % 2 == 0 else r - 1
        scale = jnp.where(which < 4, prm[r + 1, IKS : IKS + 1, :], jnp.where(which < 8, prm[r + 1, IAL : IAL + 1, :], 1.0))
        pieces.append((maps[r] + off + maps_g[other]) * scale)
    left = jnp.concatenate(pieces, 1)
    near = zrel[...]
    zone_id = iota((32, WIDTH), 0)
    onehot = jnp.concatenate([(zone_id == near[r : r + 1, :]).astype(F32) for r in range(1, 7)], 1)
    onehot = onehot.astype(jnp.bfloat16)
    nt = (((1,), (1,)), ((), ()))
    parts = [lax.dot_general(part, onehot, nt, preferred_element_type=F32) for part in split3(left)]
    by_zone = parts[0] + (parts[1] + parts[2])
    fields = [by_zone[4 * q : 4 * q + 4, :] for q in range(3)]
    sub4 = iota((4, 32), 0)
    lane4 = iota((4, 32), 1)
    losses = jnp.where(sub4 == 0, loss[0], jnp.where(sub4 == 1, loss[1], loss[2]))
    fields.append(jnp.where(lane4 == 0, losses, jnp.where(lane4 == 1, most, size)))
    sums = jnp.concatenate(fields, 1)
    payload = jnp.concatenate([sums[i : i + 1, :] for i in range(3)], 1)
    spread[...] = jnp.broadcast_to(payload[None], spread.shape)


def ring_kernel(parts, spread):
    lane = iota((SUB, 256), 1)
    total = jnp.zeros((SUB, 256), F32)
    blank = jnp.zeros((SUB, 128), F32)
    most = None
    loss = jnp.zeros((SUB, 256), F32)
    for z in range(8):
        lines = []
        for part in (parts[z], parts[8 + z]):
            lines += [part[:, 128 * i : 128 * (i + 1)] for i in range(3)] + [blank[0:1, :]]
        tile = jnp.concatenate(lines, 0)
        most = tile if most is None else jnp.maximum(most, tile)
        tile = jnp.concatenate([tile, blank], 1)
        for q in range(3):
            start = 84 * q + 8 * z
            moved = pltpu.roll(tile, (start - 32 * q) % 256, 1)
            total = total + jnp.where(jnp.logical_and(lane >= start, lane < start + NEAR), moved, 0.0)
        loss = loss + tile
    total = jnp.where(lane == 252, pltpu.roll(loss, 252 - 96, 1), total)
    rows = []
    one = iota((1, 256), 1)
    for z_hi in range(2):
        state = most[4 * z_hi : 4 * z_hi + 1, :]
        for power in range(3):
            row = total[4 * z_hi + power : 4 * z_hi + power + 1, :]
            row = jnp.where(one == 253, state[:, 97:98], row)
            rows.append(jnp.where(one == 254, state[:, 98:99], row))
    rows = jnp.concatenate(rows, 1)
    spread[...] = jnp.broadcast_to(rows[None], spread.shape)


def last_kernel(parts, h1, g2, final, grad_k, grad_a, grad_n, misfit, rates):
    sums = [jnp.zeros((1, 256), F32) for _ in range(4)]
    for pair in range(8):
        tiles = [parts[8 * y + pair] for y in range(4)]
        for z_hi in range(2):
            powers = [[tile[:, 256 * (3 * z_hi + i) : 256 * (3 * z_hi + i + 1)] for i in range(3)] for tile in tiles]
            first = [part[0] for part in powers]
            most = jnp.maximum(jnp.maximum(first[0], first[1]), jnp.maximum(first[2], first[3]))
            step = CFL / most[:, 253:254]
            rates[2 * pair + z_hi] = jnp.broadcast_to(step, (1, 128))
            move = step - first[0][:, 254:255]
            for y in range(4):
                a, b, c = powers[y]
                sums[y] = sums[y] + (a + move * (b + move * c))
    lane = iota((1, 256), 1)
    rows = sums
    for q, out in enumerate((grad_k, grad_a, grad_n)):
        total = jnp.zeros((1, 256), F32)
        for y in range(4):
            field = rows[y] if q == 0 else pltpu.roll(rows[y], 256 - 84 * q, 1)
            total = total + pltpu.roll(jnp.where(lane < 84, field, 0.0), (64 * y - 4) % 256, 1)
        out[...] = total
    misfit[0, 0] = jnp.sum(jnp.where(lane == 252, rows[0] + rows[1] + rows[2] + rows[3], 0.0))
    _, pair, z_hi = axes()
    size = rates[2 * pair + z_hi]
    size = jnp.concatenate([size, size, size], 1)
    for j in range(TILES):
        for row in range(4):
            tile = h1[row, j] + size * g2[row, j]
            for s in range(SUB):
                final[TILES * s + j, row : row + 1, :] = tile[s : s + 1, :]


VMEM = pl.BlockSpec(memory_space=pltpu.VMEM)
SMEM = pl.BlockSpec(memory_space=pltpu.SMEM)


def call(kernel, name, ins, outs, out_specs=None, scratch=(), cost=None, in_place=None, room=8):
    return pl.pallas_call(
        kernel,
        name=name,
        in_specs=ins,
        out_specs=out_specs or [VMEM] * len(outs),
        out_shape=[jax.ShapeDtypeStruct(shape, dtype) for shape, dtype in outs],
        scratch_shapes=scratch,
        cost_estimate=cost,
        input_output_aliases=in_place or {},
        compiler_params=pltpu.CompilerParams(vmem_limit_bytes=room * 1024 * 1024),
    )


def local(
    initial_head,
    sat_conductivity,
    vg_alpha,
    vg_n,
    zone_map,
    forcing_plan,
    tensiometer_cells,
    tensiometer_heads,
):
    count = lax.axis_size("row")
    plan = forcing_plan[0]
    edge = (2 * TILES + 1, SUB, WIDTH)
    h0, send_odd, send_even, zones = call(
        pack_kernel,
        "pack_edges",
        [pl.BlockSpec(memory_space=pltpu.HBM)] * 3,
        [(FIELD, F32), (edge, F32), (edge, F32), ((2, WIDTH), F32)],
        scratch=[
            pltpu.VMEM((48, 4, WIDTH), F32),
            pltpu.VMEM((2, 192), jnp.int32),
            pltpu.VMEM((2, 2), jnp.int32),
            pltpu.SemaphoreType.DMA((3,)),
        ],
    )(initial_head[0], zone_map, plan)
    odd = [(i, i + 1) for i in range(1, count - 1, 2)]
    even = [(i, i + 1) for i in range(0, count, 2)]
    got_odd = lax.ppermute(send_odd, "row", odd + [(j, i) for i, j in odd])
    got_even = lax.ppermute(send_even, "row", even + [(j, i) for i, j in even])
    wide = (6, TILES, SUB, WIDTH)
    fields = [(wide, F32)] * 10 + [((ROWS, 16, WIDTH), F32), ((ROWS, WIDTH), jnp.int32)]
    whole = [pltpu.VMEM(FIELD, F32)] * 3 + [pltpu.VMEM(wide, F32)]
    seen = tensiometer_cells.shape[1]
    own = call(
        own_kernel,
        "own_cells",
        [SMEM] * 4 + [VMEM] * 4,
        fields
        + [((SUB, WIDTH), F32), ((SUB, 128), F32)]
        + [((seen, 192), jnp.bfloat16), ((192, seen), jnp.bfloat16), ((seen, WIDTH), jnp.bfloat16), ((seen, 128), F32)],
        scratch=whole + [pltpu.VMEM(wide, F32)] * 2,
        cost=pl.CostEstimate(flops=200_000_000, bytes_accessed=8_000_000, transcendentals=600_000),
    )(sat_conductivity, vg_alpha, vg_n, plan, h0, zones, tensiometer_cells, tensiometer_heads)
    held, (most, near), sensors = (h0, *own[:12]), own[12:14], own[14:]
    row = (TILES, SUB, WIDTH)
    for exchange, got, result in (("odd", got_odd, (SUB, WIDTH)), ("even", got_even, (32, 1, 128))):
        *held, most = call(
            functools.partial(side_kernel, exchange),
            "first_step_" + exchange,
            [VMEM] * 17,
            [(FIELD, F32)] + fields + [(result, F32)],
            scratch=whole + [pltpu.VMEM(row, F32)] * 3 + [pltpu.VMEM((3, *row), F32)],
            in_place={4 + i: i for i in range(13)},
        )(near, zones, most, got, *held)
    fields, rates = held, most
    rates = lax.all_to_all(rates, "row", 0, 0, tiled=True)
    h1, g2, sums = call(
        second_kernel,
        "second_step_and_adjoint",
        [VMEM] * 18,
        [(OWN, F32), (OWN, F32), ((16, 1, 384), F32)],
        scratch=[pltpu.VMEM(FIELD, F32)] * 4
        + [pltpu.VMEM(OWN, F32)] * 7
        + [pltpu.VMEM(FIELD, F32)] * 2
        + [pltpu.VMEM(wide, F32)] * 3
        + [pltpu.VMEM((6, 16, WIDTH), F32)] * 3,
        room=20,
    )(rates, *sensors, *fields)
    sums = lax.all_to_all(sums, ("event", "row"), 0, 0, tiled=True, axis_index_groups=RINGS)
    (sums,) = call(ring_kernel, "ring_sums", [VMEM], [((32, 1, 6 * 256), F32)])(sums)
    sums = lax.all_to_all(sums, ("event", "row"), 0, 0, tiled=True, axis_index_groups=PLANES)
    row = ((1, ZONES), F32)
    final, grad_k, grad_a, grad_n, misfit = call(
        last_kernel,
        "final_head_and_sums",
        [VMEM, VMEM, VMEM],
        [((48, 4, WIDTH), F32), row, row, row, ((1, 1), F32)],
        [VMEM] * 4 + [SMEM],
        scratch=[pltpu.VMEM((16, 1, 128), F32)],
    )(sums, h1, g2)
    return (final[None], misfit[0, 0], grad_k[0], grad_a[0], grad_n[0])


def solution(mesh):
    return jax.shard_map(
        local,
        mesh=mesh,
        in_specs=(
            P("event", None, "row", None),
            P(),
            P(),
            P(),
            P("row", None),
            P("event", None, "row"),
            P("event", "row"),
            P("event", "row"),
        ),
        out_specs=(P("event", None, "row", None), P(), P(), P(), P()),
        check_vma=False,
    )
```
